32 devices in a mesh: dp: 16 (over z, x, core), blk: 2 (over y).
Axes of the slice: x: 2, y: 2, z: 4, core: 2. Of those that a mesh axis runs over, the one named last changes fastest.
Arguments:
- tokens: bfloat16 [16, 768, 768], P('dp', 'blk'), may hold values from -6 to 6
- visible: int32 [16, 768], P('dp', 'blk'), may hold values from 0 to 1535, as said below
- ln1_gain: float32 [768], replicated, may hold values from 0.1 to 1.9
- w_qkv: bfloat16 [768, 2304], replicated, may hold values from -0.21875 to 0.21875
- w_proj: bfloat16 [768, 768], replicated, may hold values from -3.5 to 3.5
- ln2_gain: float32 [768], replicated, may hold values from 0.1 to 1.9
- w_up: bfloat16 [768, 3072], replicated, may hold values from -0.21875 to 0.21875
- w_down: bfloat16 [3072, 768], replicated, may hold values from -0.109375 to 0.109375
- d_out: bfloat16 [16, 768, 768], P('dp', 'blk'), may hold values from -6 to 6
Outputs:
- out: bfloat16 [16, 768, 768], P('dp', 'blk')
- d_tokens: float32 [16, 768, 768], P('dp', 'blk')
- d_ln1_gain: float32 [768], replicated
- d_w_qkv: float32 [768, 2304], replicated
- d_w_proj: float32 [768, 768], replicated
- d_ln2_gain: float32 [768], replicated
- d_w_up: float32 [768, 3072], replicated
- d_w_down: float32 [3072, 768], replicated
The draws below stay inside these ranges and needn't reach their ends.
Inputs may be any that keep to these rules, and one draw needn't show every extreme that they name: `visible`: each row is strictly increasing, starts at 0 and ends at 1535.
All inputs are finite; a program needn't handle non-finite values.
Results may differ from the reference program's by a relative error of at most 0.015.
Values may be sent and summed in bfloat16 or wider, within the bound.
No kernel may reach another device: no remote copies, remote signals or barrier semaphores. Data moves between devices by JAX's collectives and lax.ppermute only.
A program may use at most 192 MiB of HBM per device.

```python
import math
import jax
import jax.numpy as jnp
from jax import lax

D = 768
HEADS = 12
HD = 64
FF = 3072
SEQ_LEN = 768
SEQS = 16


def draw_visible(key, part):
    key = jax.random.fold_in(key, 7)
    row_keys = jax.random.split(key, SEQS)

    def one_row(row_key):
        chosen = jax.random.permutation(row_key, 2 * SEQ_LEN - 2)[:SEQ_LEN - 2] + 1
        inner = jnp.sort(chosen).astype(jnp.int32)
        first = jnp.zeros((1,), jnp.int32)
        final = jnp.full((1,), 2 * SEQ_LEN - 1, jnp.int32)
        return jnp.concatenate([first, inner, final])
    return jax.vmap(one_row)(row_keys)


def levels(rng, shape, pieces, low, largest):
    factor_of = 1.0
    for dim, shards_of in pieces:
        draws = jax.random.uniform(jax.random.fold_in(jax.random.fold_in(rng, 6), dim), (shards_of,), jnp.float32, low / len(pieces), largest / len(pieces))
        factor_of = factor_of * jnp.repeat(jnp.exp(draws), shape[dim] // shards_of).reshape((-1,) + (1,) * (len(shape) - 1 - dim))
    return factor_of


def gaussian(own_key, dims, scale, limit, pieces=(), kind=jnp.bfloat16):
    drawn = scale * jax.random.normal(own_key, dims, jnp.float32)
    if pieces:
        drawn = drawn * levels(own_key, dims, pieces, -0.22, 0.18)
    return jnp.clip(drawn, -limit, limit).astype(kind)


def setup_inputs(seed: int = 0) -> dict:
    streams_of = jax.random.split(jax.random.key(seed), 10)
    tokens = gaussian(streams_of[0], (SEQS, SEQ_LEN, D), 1.0, 6.0, ((0, 16), (1, 2)))
    visible = draw_visible(jax.random.fold_in(streams_of[9], 71), 0)
    ln1_gain = jnp.clip(1.0 + 0.18 * jax.random.normal(streams_of[2], (D,), jnp.float32), 0.1, 1.9)
    w_qkv = gaussian(streams_of[3], (D, 3 * D), D ** -0.5, 0.21875)
    w_proj = gaussian(streams_of[4], (D, D), (max(1, 3 * D // SEQ_LEN)) ** -0.5, 3.5)
    ln2_gain = jnp.clip(1.0 + 0.18 * jax.random.normal(streams_of[5], (D,), jnp.float32), 0.1, 1.9)
    w_up = gaussian(streams_of[6], (D, FF), D ** -0.5, 0.21875)
    w_down = gaussian(streams_of[7], (FF, D), FF ** -0.5, 0.109375)
    d_out = gaussian(streams_of[8], (SEQS, SEQ_LEN, D), 1.0, 6.0, ((0, 16), (1, 2)))
    return dict(tokens=tokens, visible=visible, ln1_gain=ln1_gain, w_qkv=w_qkv, w_proj=w_proj, ln2_gain=ln2_gain, w_up=w_up, w_down=w_down, d_out=d_out)


@jax.custom_vjp
def low(v):
    return lax.optimization_barrier(v.astype(jnp.bfloat16)).astype(jnp.float32)

@jax.custom_vjp
def low_back(v):
    return v

def low_keep(v):
    return (low(v), None)

def low_pass(kept, grad):
    return (grad,)

def back_keep(v):
    return (v, None)

def back_low(kept, grad):
    return (low(grad),)
low.defvjp(low_keep, low_pass)
low_back.defvjp(back_keep, back_low)
epsilon = 1e-06

def matmul(left, right):
    return jnp.dot(left, right, precision=lax.Precision.HIGHEST, preferred_element_type=jnp.float32)

def layer_norm(values, gain):
    center = values - lax.optimization_barrier(jnp.mean(values, -1, keepdims=True))
    spread = lax.optimization_barrier(jnp.mean(center * center, -1, keepdims=True))
    return center * lax.rsqrt(spread + epsilon) * gain

def position_table(visible):
    half = D // 2
    column = jnp.arange(half, dtype=jnp.float32)
    freqs = jnp.exp(column * (-math.log(10000.0) / half))
    angles = visible.astype(jnp.float32)[..., None] * freqs
    return jnp.concatenate([jnp.sin(angles), jnp.cos(angles)], -1)

def head_attention(operands):
    query, keys, values = operands
    scores = low_back(matmul(query, keys.T) * HD ** (-0.5))
    probs = jax.nn.softmax(scores, -1)
    return matmul(low(probs), values)

def sequence_layer(tokens, ln1_gain, w_qkv, w_proj, ln2_gain, w_up, w_down, position):
    length = tokens.shape[0]
    resid = tokens + position
    normed1 = low(layer_norm(resid, ln1_gain))
    qkv = low(low_back(matmul(normed1, w_qkv)))

    def split_heads(block):
        return block.reshape(length, HEADS, HD).transpose(1, 0, 2)
    query = split_heads(qkv[:, :D])
    keys = split_heads(qkv[:, D:2 * D])
    values = split_heads(qkv[:, 2 * D:])
    per_head = lax.map(jax.checkpoint(head_attention), (query, keys, values))
    attended = per_head.transpose(1, 0, 2).reshape(length, D)
    attended = low(low_back(attended))
    resid2 = resid + low_back(matmul(attended, w_proj))
    normed2 = low(layer_norm(resid2, ln2_gain))
    hidden = low_back(matmul(normed2, w_up))
    activated = low(jax.nn.gelu(hidden))
    return resid2 + low_back(matmul(activated, w_down))

def reference(tokens, visible, ln1_gain, w_qkv, w_proj, ln2_gain, w_up, w_down, d_out):
    weights = (ln1_gain.astype(jnp.float32), w_qkv.astype(jnp.float32), w_proj.astype(jnp.float32), ln2_gain.astype(jnp.float32), w_up.astype(jnp.float32), w_down.astype(jnp.float32))
    position = position_table(visible)

    def one_sequence(totals, item):
        seq_tokens, seq_position, seq_cotangent = item

        def apply_layer(inputs, *params):
            return sequence_layer(inputs, *params, seq_position)
        result, backward = jax.vjp(apply_layer, seq_tokens, *weights)
        grads = backward(seq_cotangent)
        totals = tuple((total + grad for total, grad in zip(totals, grads[1:])))
        return (totals, (result.astype(jnp.bfloat16), grads[0]))
    start = tuple((jnp.zeros(weight.shape, jnp.float32) for weight in weights))
    totals, (outputs, input_grads) = lax.scan(one_sequence, start, (tokens.astype(jnp.float32), position, d_out.astype(jnp.float32)))
    return (outputs, input_grads, totals[0], totals[1], totals[2], totals[3], totals[4], totals[5])
```

```python
import functools
import math

import jax
import jax.numpy as jnp
from jax import lax
from jax.experimental import pallas as pl
from jax.experimental.pallas import tpu as pltpu
from jax.sharding import PartitionSpec as P

HEADS = 12
HD = 64
PAIR = 2 * HD
epsilon = 1e-06
f32 = jnp.float32
bf16 = jnp.bfloat16
NN = ((1,), (0,))
NT = ((1,), (1,))
TN = ((0,), (0,))
AXES = ("dp", "blk")
MIB = 1 << 20


def dot(left, right, dims=NN):
    return lax.dot_general(left, right, (dims, ((), ())), preferred_element_type=f32)


def position_table(visible, width):
    half = width // 2
    column = jnp.arange(half, dtype=f32)
    freqs = jnp.exp(column * (-math.log(10000.0) / half))
    angles = visible.astype(f32)[..., None] * freqs
    return jnp.concatenate([jnp.sin(angles), jnp.cos(angles)], -1)


def normalize(values):
    center = values - jnp.mean(values, -1, keepdims=True)
    spread = jnp.mean(center * center, -1, keepdims=True)
    scale = lax.rsqrt(spread + epsilon)
    return center * scale, scale


def norm_backward(grad, gain, xhat, scale):
    e = grad * gain
    return scale * (
        e - jnp.mean(e, -1, keepdims=True) - xhat * jnp.mean(e * xhat, -1, keepdims=True)
    )


def call(kernel, grid, in_specs, out_specs, out_shape, args, scalars, vmem, scratch=(), aliases=None):
    return pl.pallas_call(
        kernel,
        grid_spec=pltpu.PrefetchScalarGridSpec(
            num_scalar_prefetch=1,
            grid=grid,
            in_specs=in_specs,
            out_specs=out_specs,
            scratch_shapes=list(scratch),
        ),
        out_shape=out_shape,
        input_output_aliases=aliases or {},
        compiler_params=pltpu.CompilerParams(vmem_limit_bytes=vmem * MIB),
    )(scalars, *args)


def spec(shape, index):
    return pl.BlockSpec(shape, index)


def whole(array):
    zeros = (0,) * array.ndim
    return pl.BlockSpec(array.shape, lambda i, s: zeros)


def shape(dims, dtype):
    return jax.ShapeDtypeStruct(dims, dtype)


FF_ORDERS = (
    (("x", "y", "z0", "z1"), ("z0", "x", "y", "z1")),
    (("y", "z0", "x", "z1"), ("x", "y", "z0", "z1")),
    (("z0", "x", "y", "z1"), ("y", "z0", "x", "z1")),
)
QKV_ORDER = (("x", "z0", "z1"), ("z0", "x", "z1"))
DP_BIT = {"c": 1, "x": 2, "z0": 4, "z1": 8}


def swap(array, first, second=None):
    second = second or first
    pairs = []
    for d in range(16):
        for b in range(2):
            bit = second if d & 1 else first
            to = (d, b ^ 1) if bit == "y" else (d ^ DP_BIT[bit], b)
            pairs.append((d * 2 + b, to[0] * 2 + to[1]))
    return lax.ppermute(array, AXES, pairs)


def place(order):
    d, b = lax.axis_index("dp"), lax.axis_index("blk")
    code = jnp.int32(0)
    for bit in order:
        value = b & 1 if bit == "y" else (d // DP_BIT[bit]) & 1
        code = code * 2 + value
    return code


def places(orders):
    core = lax.axis_index("dp") & 1
    first, second = place(orders[0]), place(orders[1])
    return jnp.where(core == 0, first, second), jnp.where(core == 0, second, first)


def add(a, b):
    return (a.astype(f32) + b.astype(f32)).astype(bf16)


def reduce_halves(keep, send, orders):
    received = swap(send, "c")
    count = len(orders[0])
    for step in range(count - 1):
        half = keep.shape[0] // 2
        send = add(keep[half:], received[half:])
        keep = add(keep[:half], received[:half])
        received = swap(send, orders[0][step], orders[1][step])
    keep = add(keep, received)
    received = swap(keep, orders[0][-1], orders[1][-1])
    return add(keep, received[::-1])


def spread_halves(block, orders):
    for step in range(len(orders[0]) - 2, 0, -1):
        block = jnp.concatenate([block, swap(block, orders[0][step], orders[1][step])], 0)
    other = swap(block, "c")
    far = swap(block, orders[0][0], orders[1][0])
    return block, far, other, swap(far, "c")


def ln_qkv_kernel(s, tok, pos, gain, w, normed, qkv):
    @pl.when(pl.program_id(0) == 0)
    def _():
        xhat, _ = normalize(tok[...].astype(f32) + pos[...])
        normed[...] = (xhat * gain[...]).astype(bf16)

    qkv[...] = dot(normed[...], w[...]).astype(bf16)


def ln_qkv(scalars, tok, pos, gain, w):
    rows, width = tok.shape
    return call(
        ln_qkv_kernel,
        (3,),
        [whole(tok), whole(pos), whole(gain), spec((width, width), lambda i, s: (0, i))],
        [spec((rows, width), lambda i, s: (0, 0)), spec((rows, width), lambda i, s: (0, i))],
        [shape((rows, width), bf16), shape((rows, 3 * width), bf16)],
        (tok, pos, gain, w),
        scalars,
        24,
    )


def head_masks(x):
    lane = lax.broadcasted_iota(jnp.int32, x.shape, 1)
    return jnp.where(lane < HD, x, 0.0).astype(bf16), jnp.where(lane >= HD, x, 0.0).astype(bf16)


def attn_kernel(s, q, k_own, v_own, k_far, v_far, out):
    rows = q.shape[0]
    k = jnp.concatenate([k_own[...], k_far[...]], 0)
    vt = jnp.concatenate([v_own[...], v_far[...]], 0).T
    parts = []
    for h, qh in enumerate(head_masks(q[...].astype(f32) * HD**-0.5)):
        scores = dot(k, qh, NT)
        e = jnp.exp(scores - jnp.max(scores, 0, keepdims=True))
        total = jnp.sum(e, 0, keepdims=True)
        part = dot(vt[h * HD : (h + 1) * HD], e.astype(bf16))
        parts.append(part * (1.0 / total))
    out[...] = jnp.concatenate(parts, 0).T.astype(bf16)


def attention(scalars, qkv, qkv_far):
    rows, width = qkv.shape[0], qkv.shape[1] // 3
    pairs = width // PAIR

    def column(part):
        return spec((rows, PAIR), lambda i, s: (0, part * pairs + i))

    return call(
        attn_kernel,
        (pairs,),
        [column(0), column(1), column(2), column(1), column(2)],
        spec((rows, PAIR), lambda i, s: (0, i)),
        shape((rows, width), bf16),
        (qkv, qkv, qkv, qkv_far, qkv_far),
        scalars,
        32,
    )


def proj_kernel(s, att, w, tok, pos, gain, resid2, normed2, normed2_t):
    value = tok[...].astype(f32) + pos[...] + dot(att[...], w[...])
    resid2[...] = value
    xhat, _ = normalize(value)
    low = (xhat * gain[...]).astype(bf16)
    normed2[...] = low
    normed2_t[...] = low.T


def project(scalars, att, w, tok, pos, gain):
    rows, width = att.shape
    args = (att, w, tok, pos, gain)
    full = spec((rows, width), lambda i, s: (0, 0))
    return call(
        proj_kernel,
        (1,),
        [whole(a) for a in args],
        [full, full, spec((width, rows), lambda i, s: (0, 0))],
        [shape((rows, width), f32), shape((rows, width), bf16), shape((width, rows), bf16)],
        args,
        scalars,
        24,
    )


def gelu_and_slope(v):
    c = math.sqrt(2.0 / math.pi)
    square = v * v
    t = jnp.tanh(v * (c + (c * 0.044715) * square))
    act = 0.5 * v * (1.0 + t)
    slope = 0.5 * (1.0 + t) + (0.5 * v) * (1.0 - t * t) * (c + (3.0 * c * 0.044715) * square)
    return act, slope


def ff_kernel(s, normed, normed_t, cot, up, down, out_in, back_in, keep, send, out, back):
    step = pl.program_id(0)
    hidden = dot(normed[...], up[...])
    act, slope = gelu_and_slope(hidden)
    act = act.astype(bf16)
    grad = (dot(cot[...], down[...], NT) * slope).astype(bf16)
    out_part = dot(act, down[...])
    back_part = dot(grad, up[...], NT)

    @pl.when(step == 0)
    def _():
        out[...] = out_in[...] + out_part
        back[...] = back_in[...] + back_part

    @pl.when(step == 1)
    def _():
        out[...] += out_part
        back[...] += back_part

    g_down = dot(act, cot[...], TN).astype(bf16)
    g_up = dot(normed_t[...], grad).astype(bf16)

    def store(target, code):
        rows_d = g_down.shape[0] // 16
        rows_u = g_up.shape[0] // 16
        half = g_up.shape[1] // 2
        for block in range(16):
            at = block ^ code
            target[at, :rows_d, :] = g_down[block * rows_d : (block + 1) * rows_d]
            part = g_up[block * rows_u : (block + 1) * rows_u]
            target[at, rows_d:, : 2 * half] = part[:rows_d]
            target[at, rows_d : rows_d + 16, 2 * half :] = part[rows_d:, :half]
            target[at, rows_d + 16 :, 2 * half :] = part[rows_d:, half:]

    @pl.when(step == 0)
    def _():
        store(send, s[2])

    @pl.when(step == 1)
    def _():
        store(keep, s[1])


def ff_chunk(scalars, chunk, normed, normed_t, cot, up, down, out_in, back_in):
    rows, width = normed.shape
    wide = 512

    def half(i, s):
        return 2 * chunk + (s[0] ^ (1 - i))

    full = spec((rows, width), lambda i, s: (0, 0))
    piece = spec((16, 64, width), lambda i, s: (0, 0, 0))
    return call(
        ff_kernel,
        (2,),
        [
            whole(normed),
            whole(normed_t),
            whole(cot),
            spec((width, wide), lambda i, s: (0, half(i, s))),
            spec((wide, width), lambda i, s: (half(i, s), 0)),
            full,
            full,
        ],
        [piece, piece, full, full],
        [shape((16, 64, width), bf16)] * 2 + [shape((rows, width), f32)] * 2,
        (normed, normed_t, cot, up, down, out_in, back_in),
        scalars,
        40,
    )


def mid_kernel(s, back, resid2, out_acc, cot, gain, w_own, w_other, out, grad2, branch, g_own, g_other):
    value = resid2[...]
    out[...] = (value + out_acc[...]).astype(bf16)
    xhat, scale = normalize(value)
    grad = cot[...].astype(f32) + norm_backward(back[...], gain[...], xhat, scale)
    grad2[...] = grad
    low = grad.astype(bf16)
    branch[...] = low
    g_other[...] = dot(low, w_other[...], NT).astype(bf16)
    g_own[...] = dot(low, w_own[...], NT).astype(bf16)


def middle(scalars, back, resid2, out_acc, cot, gain, w):
    rows, width = resid2.shape
    half = width // 2
    full = spec((rows, width), lambda i, s: (0, 0))
    part = spec((rows, half), lambda i, s: (0, 0))
    return call(
        mid_kernel,
        (1,),
        [
            full,
            full,
            full,
            full,
            whole(gain),
            spec((half, width), lambda i, s: (s[0], 0)),
            spec((half, width), lambda i, s: (1 - s[0], 0)),
        ],
        [full, full, full, part, part],
        [
            shape((rows, width), bf16),
            shape((rows, width), f32),
            shape((rows, width), bf16),
            shape((rows, half), bf16),
            shape((rows, half), bf16),
        ],
        (back, resid2, out_acc, cot, gain, w, w),
        scalars,
        32,
    )


def attn_back_kernel(s, q_o, k_o, v_o, q_f, k_f, v_f, g_o, g_f, gq, gk, gv):
    k = jnp.concatenate([k_o[...], k_f[...]], 0)
    v = jnp.concatenate([v_o[...], v_f[...]], 0)
    q = jnp.concatenate([q_o[...], q_f[...]], 0).astype(f32) * HD**-0.5
    g = jnp.concatenate([g_o[...], g_f[...]], 0).astype(f32)
    kt = (k.astype(f32) * HD**-0.5).astype(bf16).T
    grad_q, grad_k, grad_v = [], 0.0, 0.0
    for h, (qh, gh) in enumerate(zip(head_masks(q), head_masks(g))):
        scores = dot(k, qh, NT)
        e = jnp.exp(scores - jnp.max(scores, 0, keepdims=True))
        probs = e * (1.0 / jnp.sum(e, 0, keepdims=True))
        grad_v = grad_v + dot(probs.astype(bf16), gh)
        grad_p = dot(v, gh, NT)
        row = jnp.sum(probs * grad_p, 0, keepdims=True)
        grad_s = (probs * (grad_p - row)).astype(bf16)
        grad_k = grad_k + dot(grad_s, qh)
        grad_q.append(dot(kt[h * HD : (h + 1) * HD], grad_s))
    gq[...] = jnp.concatenate(grad_q, 0).T.astype(bf16)
    gk[...] = grad_k.astype(bf16)
    gv[...] = grad_v.astype(bf16)


def attention_back(scalars, qkv, qkv_far, g_own, g_far):
    rows, width = qkv.shape[0], qkv.shape[1] // 3
    pairs = width // PAIR
    mine = pairs // 2

    def column(part):
        return spec((rows, PAIR), lambda i, s: (0, part * pairs + mine * s[0] + i))

    block = spec((rows, PAIR), lambda i, s: (0, i))
    out = spec((2 * rows, PAIR), lambda i, s: (0, i))
    return call(
        attn_back_kernel,
        (mine,),
        [column(0), column(1), column(2)] * 2 + [block, block],
        [out] * 3,
        [shape((2 * rows, width // 2), bf16)] * 3,
        (qkv, qkv, qkv, qkv_far, qkv_far, qkv_far, g_own, g_far),
        scalars,
        48,
    )


def joint_kernel(s, n_own, n_far, gq, gk, gv, att, branch, keep, send):
    step = pl.program_id(0)
    n = jnp.concatenate([n_own[...], n_far[...]], 0)
    cols = gq.shape[1]

    def fill(target, code):
        tiles = [dot(n, g[...], TN).astype(bf16) for g in (gq, gk, gv)]
        tiles.append(dot(att[...], branch[...], TN).astype(bf16))
        rows = tiles[0].shape[0] // 8
        for block in range(8):
            at = block ^ code
            for i, tile in enumerate(tiles):
                part = tile[block * rows : (block + 1) * rows]
                target[at, :, i * cols : i * cols + part.shape[1]] = part

    @pl.when(step == 0)
    def _():
        fill(send, s[2])

    @pl.when(step == 1)
    def _():
        fill(keep, s[1])


def joint_grads(scalars, n_own, n_far, gq, gk, gv, att, branch):
    rows, width = n_own.shape
    half = width // 2
    feature = spec((rows, half), lambda i, s: (0, s[0] ^ (1 - i)))
    cols = 3 * half + width
    piece = spec((8, half // 8, cols), lambda i, s: (0, 0, 0))
    return call(
        joint_kernel,
        (2,),
        [feature, feature, whole(gq), whole(gk), whole(gv), feature, whole(branch)],
        [piece, piece],
        [shape((8, half // 8, cols), bf16)] * 2,
        (n_own, n_far, gq, gk, gv, att, branch),
        scalars,
        32,
    )


def back_qkv_kernel(s, gq, gk, gv, wq, wk, wv, own, far):
    rows = own.shape[0]

    def part(at):
        total = dot(gq[pl.ds(at, rows)], wq[...], NT)
        total += dot(gk[pl.ds(at, rows)], wk[...], NT)
        return total + dot(gv[pl.ds(at, rows)], wv[...], NT)

    far[...] = part(rows).astype(bf16)
    own[...] = part(0)


def back_qkv(scalars, gq, gk, gv, w):
    rows, half = gq.shape[0] // 2, gq.shape[1]
    width = 2 * half

    def column(part):
        return spec((width, half), lambda i, s: (0, 2 * part + s[0]))

    full = spec((rows, width), lambda i, s: (0, 0))
    return call(
        back_qkv_kernel,
        (1,),
        [whole(gq), whole(gk), whole(gv), column(0), column(1), column(2)],
        [full, full],
        [shape((rows, width), f32), shape((rows, width), bf16)],
        (gq, gk, gv, w, w, w),
        scalars,
        32,
    )


def last_kernel(s, own, far, tok, pos, gain, grad2, out):
    xhat, scale = normalize(tok[...].astype(f32) + pos[...])
    grad = own[...] + far[...].astype(f32)
    out[...] = grad2[...] + norm_backward(grad, gain[...], xhat, scale)


def token_grad(scalars, own, far, tok, pos, gain, grad2):
    args = (own, far, tok, pos, gain, grad2)
    return call(
        last_kernel,
        (1,),
        [whole(a) for a in args],
        whole(own),
        shape(own.shape, f32),
        args,
        scalars,
        24,
    )


def unpack_ff_kernel(s, near, far, *refs):
    down, up = refs[-2:]
    step = pl.program_id(0)
    low = s[1] & 7

    def unpack(source):
        for block in range(8):
            at = block ^ low
            down[pl.ds(pl.multiple_of(at * 32, 32), 32), :] = source[block, :32, :].astype(f32)
            row = pl.multiple_of(at * 48, 16)
            up[pl.ds(row, 32), :] = source[block, 32:, :512].astype(f32)
            up[pl.ds(row + 32, 16), :256] = source[block, 32:48, 512:].astype(f32)
            up[pl.ds(row + 32, 16), 256:] = source[block, 48:, 512:].astype(f32)

    @pl.when(step == 0)
    def _():
        unpack(near)

    @pl.when(step == 1)
    def _():
        unpack(far)


def unpack_ff(scalars, chunk, near, far, width, hidden, so_far):
    def side(i, s):
        return i ^ (s[1] // 8)

    any_spec = pl.BlockSpec(memory_space=pl.ANY)
    return call(
        unpack_ff_kernel,
        (2,),
        [whole(near), whole(far)] + [any_spec] * len(so_far),
        [
            spec((256, width), lambda i, s: (2 * (2 * chunk + s[0]) + side(i, s), 0)),
            spec((width // 2, 512), lambda i, s: (side(i, s), 2 * chunk + s[0])),
        ],
        [shape((hidden, width), f32), shape((width, hidden), f32)],
        (near, far) + tuple(so_far),
        scalars,
        32,
        aliases={3: 0, 4: 1} if so_far else None,
    )


def unpack_qkv_kernel(s, near, far, *refs):
    joint, proj = refs[-2:]
    step = pl.program_id(0)
    low = s[1] & 3
    mine = s[2]

    def unpack(source):
        half = source.shape[2] // 8
        for block in range(4):
            at = pl.multiple_of((block ^ low) * 48, 16)
            rows = pl.ds(at, 48)
            for part in range(3):
                for side in range(2):
                    column = pl.multiple_of(2 * half * part + half * (mine ^ side), 128)
                    value = source[block, :, (3 * side + part) * half : (3 * side + part + 1) * half]
                    joint[rows, pl.ds(column, half)] = value.astype(f32)
            proj[rows, :] = source[block, :, 6 * half :].astype(f32)

    @pl.when(step == 0)
    def _():
        unpack(near)

    @pl.when(step == 1)
    def _():
        unpack(far)


def unpack_qkv(scalars, near, far, width, so_far):
    def row(i, s):
        return 2 * s[0] + (i ^ (s[1] // 4))

    any_spec = pl.BlockSpec(memory_space=pl.ANY)
    return call(
        unpack_qkv_kernel,
        (2,),
        [whole(near), whole(far)] + [any_spec] * len(so_far),
        [
            spec((width // 4, 3 * width), lambda i, s: (row(i, s), 0)),
            spec((width // 4, width), lambda i, s: (row(i, s), 0)),
        ],
        [shape((width, 3 * width), f32), shape((width, width), f32)],
        (near, far) + tuple(so_far),
        scalars,
        32,
        aliases={3: 0, 4: 1} if so_far else None,
    )


def fast(tokens, visible, ln1_gain, w_qkv, w_proj, ln2_gain, w_up, w_down, d_out):
    tok, cot = tokens[0], d_out[0]
    rows, width = tok.shape
    hidden = w_up.shape[1]
    gain1, gain2 = ln1_gain[None], ln2_gain[None]
    core = lax.axis_index("dp") & 1
    head_half = lax.axis_index("blk")
    ints = lambda *values: jnp.stack([jnp.int32(v) for v in values])
    none = ints(0)
    heads = ints(head_half)

    vis_far = swap(visible, "y")[0]
    tok_far = swap(tok, "y")
    pos = position_table(visible[0], width)
    pos_far = position_table(vis_far, width)
    normed1, qkv = ln_qkv(none, tok, pos, gain1, w_qkv)
    normed1_far, qkv_far = ln_qkv(none, tok_far, pos_far, gain1, w_qkv)
    attended = attention(none, qkv, qkv_far)
    resid2, normed2, normed2_t = project(none, attended, w_proj, tok, pos, gain2)

    out_acc = jnp.zeros((rows, width), f32)
    back = jnp.zeros((rows, width), f32)
    pieces = []
    for chunk, orders in enumerate(FF_ORDERS):
        own_code, other_code = places(orders)
        keep, send, out_acc, back = ff_chunk(
            ints(core, own_code, other_code), chunk, normed2, normed2_t, cot, w_up, w_down, out_acc, back
        )
        pieces.append((keep, send))
    out, grad2, branch, g_own, g_other = middle(heads, back, resid2, out_acc, cot, gain2, w_proj)
    g_far = swap(g_other, "y")

    summed = [reduce_halves(*pair, orders) for pair, orders in zip(pieces, FF_ORDERS)]
    gathered = [spread_halves(block, orders) for block, orders in zip(summed, FF_ORDERS)]

    gq, gk, gv = attention_back(heads, qkv, qkv_far, g_own, g_far)
    own_code, other_code = places(QKV_ORDER)
    keep, send = joint_grads(
        ints(core, own_code, other_code), normed1, normed1_far, gq, gk, gv, attended, branch
    )
    back_own, back_far = back_qkv(heads, gq, gk, gv, w_qkv)
    back_far = swap(back_far, "y")
    block = reduce_halves(keep, send, QKV_ORDER)
    other = swap(block, "y")
    cut = 3 * (width // 2)
    block = jnp.concatenate(
        [block[..., :cut], other[..., :cut], add(block[..., cut:], other[..., cut:])], -1
    )
    joint_pieces = spread_halves(block, QKV_ORDER)

    d_tokens = token_grad(none, back_own, back_far, tok, pos, gain1, grad2)

    ff = ()
    for chunk, orders in enumerate(FF_ORDERS):
        own_code, other_code = places(orders)
        near, far, near_other, far_other = gathered[chunk]
        ff = unpack_ff(ints(core, own_code), chunk, near, far, width, hidden, ff)
        ff = unpack_ff(ints(1 - core, other_code), chunk, near_other, far_other, width, hidden, ff)
    own_code, other_code = places(QKV_ORDER)
    near, far, near_other, far_other = joint_pieces
    qkvp = unpack_qkv(ints(core, own_code, head_half), near, far, width, ())
    qkvp = unpack_qkv(ints(1 - core, other_code, head_half), near_other, far_other, width, qkvp)
    d_down, d_up = ff
    d_qkv, d_proj = qkvp
    d_gain1 = jnp.sum(w_qkv.astype(f32) * d_qkv, 1) / ln1_gain
    d_gain2 = jnp.sum(w_up.astype(f32) * d_up, 1) / ln2_gain
    return out[None], d_tokens[None], d_gain1, d_qkv, d_proj, d_gain2, d_up, d_down


def layer_norm(values, gain):
    center = values - jnp.mean(values, -1, keepdims=True)
    spread = jnp.mean(center * center, -1, keepdims=True)
    return center * lax.rsqrt(spread + epsilon) * gain


def outer_product(left, right):
    return lax.dot_general(
        left, right, (((0,), (0,)), ((), ())), preferred_element_type=jnp.float32
    )


def times_transposed(left, weight):
    return lax.dot_general(
        left, weight, (((1,), (1,)), ((), ())), preferred_element_type=jnp.float32
    )


def split_blocks(keys, values):
    count = keys.shape[0]
    size = math.gcd(count, 512)
    shape = (count // size, size, HEADS, HD)
    return (keys.reshape(shape), values.reshape(shape))


def general(tokens, visible, ln1_gain, w_qkv, w_proj, ln2_gain, w_up, w_down, d_out):
    rows = tokens.shape[1]
    width = tokens.shape[2]
    factor = HD ** (-0.5)
    resid = tokens[0].astype(jnp.float32) + position_table(visible[0], width)
    normed1, back_one = jax.vjp(layer_norm, resid, ln1_gain)
    normed1 = normed1.astype(jnp.bfloat16)
    qkv = jnp.dot(normed1, w_qkv, preferred_element_type=jnp.float32).astype(jnp.bfloat16)
    query = qkv[:, :width]
    keys = qkv[:, width : 2 * width]
    values = qkv[:, 2 * width :]
    query_heads = query.reshape(rows, HEADS, HD)
    initial = (
        jnp.full((HEADS, rows), -1e30, jnp.float32),
        jnp.zeros((HEADS, rows), jnp.float32),
        jnp.zeros((HEADS, rows, HD), jnp.float32),
    )
    key_blocks, value_blocks = split_blocks(
        lax.all_gather(keys, "blk", axis=0, tiled=True),
        lax.all_gather(values, "blk", axis=0, tiled=True),
    )

    def one_block(state, block):
        running, total, accum = state
        block_keys, block_values = block
        scores = (
            jnp.einsum("qhd,khd->hqk", query_heads, block_keys, preferred_element_type=jnp.float32)
            * factor
        )
        top = jnp.maximum(running, jnp.max(scores, -1))
        weights = jnp.exp(scores - top[..., None])
        shrink = jnp.exp(running - top)
        total = total * shrink + jnp.sum(weights, -1)
        accum = accum * shrink[..., None] + jnp.einsum(
            "hqk,khd->hqd",
            weights.astype(jnp.bfloat16),
            block_values,
            preferred_element_type=jnp.float32,
        )
        return ((top, total, accum), None)

    running, total, accum = lax.scan(one_block, initial, (key_blocks, value_blocks))[0]
    log_total = running + jnp.log(total)
    attended = (accum / total[..., None]).transpose(1, 0, 2).reshape(rows, width)
    attended_low = attended.astype(jnp.bfloat16)
    resid2 = resid + jnp.dot(attended_low, w_proj, preferred_element_type=jnp.float32)
    normed2, back_two = jax.vjp(layer_norm, resid2, ln2_gain)
    normed2 = normed2.astype(jnp.bfloat16)
    hidden = jnp.dot(normed2, w_up, preferred_element_type=jnp.float32)
    activated, back_gelu = jax.vjp(jax.nn.gelu, hidden)
    activated = activated.astype(jnp.bfloat16)
    result = resid2 + jnp.dot(activated, w_down, preferred_element_type=jnp.float32)
    cotangent = d_out[0]
    grad_down = outer_product(activated, cotangent)
    (grad_hidden,) = back_gelu(times_transposed(cotangent, w_down))
    grad_hidden = grad_hidden.astype(jnp.bfloat16)
    grad_up = outer_product(normed2, grad_hidden)
    grad_resid2, grad_gain2 = back_two(times_transposed(grad_hidden, w_up))
    grad_resid2 = grad_resid2 + cotangent.astype(jnp.float32)
    grad_branch = grad_resid2.astype(jnp.bfloat16)
    grad_proj = outer_product(attended_low, grad_branch)
    grad_attended = times_transposed(grad_branch, w_proj).astype(jnp.bfloat16)
    correction = (grad_attended.astype(jnp.float32) * attended).reshape(rows, HEADS, HD)
    correction = jnp.sum(correction, -1).T
    grad_heads = grad_attended.reshape(rows, HEADS, HD)
    all_keys, all_values = (
        lax.all_gather(keys, "blk", axis=0, tiled=True),
        lax.all_gather(values, "blk", axis=0, tiled=True),
    )
    full_rows = all_keys.shape[0]
    key_blocks, value_blocks = split_blocks(all_keys, all_values)

    def back_block(grad_query, block):
        block_keys, block_values = block
        scores = (
            jnp.einsum("qhd,khd->hqk", query_heads, block_keys, preferred_element_type=jnp.float32)
            * factor
        )
        probs = jnp.exp(scores - log_total[..., None])
        grad_value = jnp.einsum(
            "hqk,qhd->khd",
            probs.astype(jnp.bfloat16),
            grad_heads,
            preferred_element_type=jnp.float32,
        )
        grad_probs = jnp.einsum(
            "qhd,khd->hqk", grad_heads, block_values, preferred_element_type=jnp.float32
        )
        grad_scores = (probs * (grad_probs - correction[..., None])).astype(jnp.bfloat16)
        grad_query = grad_query + jnp.einsum(
            "hqk,khd->qhd", grad_scores, block_keys, preferred_element_type=jnp.float32
        )
        grad_key = (
            jnp.einsum("hqk,qhd->khd", grad_scores, query_heads, preferred_element_type=jnp.float32)
            * factor
        )
        return (grad_query, (grad_key, grad_value))

    grad_query, (key_parts, value_parts) = lax.scan(
        back_block, jnp.zeros((rows, HEADS, HD), jnp.float32), (key_blocks, value_blocks)
    )
    grad_query = (grad_query * factor).reshape(rows, width)
    grad_keys, grad_values = (
        lax.psum_scatter(
            key_parts.reshape(full_rows, width).astype(jnp.bfloat16),
            "blk",
            scatter_dimension=0,
            tiled=True,
        ).astype(jnp.float32),
        lax.psum_scatter(
            value_parts.reshape(full_rows, width).astype(jnp.bfloat16),
            "blk",
            scatter_dimension=0,
            tiled=True,
        ).astype(jnp.float32),
    )
    grad_qkv = jnp.concatenate([grad_query, grad_keys, grad_values], 1).astype(jnp.bfloat16)
    grad_joint = outer_product(normed1, grad_qkv)
    grad_resid, grad_gain1 = back_one(times_transposed(grad_qkv, w_qkv))
    input_grad = grad_resid2 + grad_resid
    flats = (
        grad_joint.reshape(-1),
        grad_proj.reshape(-1),
        grad_up.reshape(-1),
        grad_down.reshape(-1),
    )
    shares = (
        lax.psum_scatter(flats[0], ("dp", "blk"), scatter_dimension=0, tiled=True),
        lax.psum_scatter(flats[1], ("dp", "blk"), scatter_dimension=0, tiled=True),
        lax.psum_scatter(flats[2], ("dp", "blk"), scatter_dimension=0, tiled=True),
        lax.psum_scatter(flats[3], ("dp", "blk"), scatter_dimension=0, tiled=True),
    )
    summed = (
        lax.all_gather(shares[0].astype(jnp.bfloat16), ("dp", "blk"), axis=0, tiled=True).astype(
            jnp.float32
        ),
        lax.all_gather(shares[1].astype(jnp.bfloat16), ("dp", "blk"), axis=0, tiled=True).astype(
            jnp.float32
        ),
        lax.all_gather(shares[2].astype(jnp.bfloat16), ("dp", "blk"), axis=0, tiled=True).astype(
            jnp.float32
        ),
        lax.all_gather(shares[3].astype(jnp.bfloat16), ("dp", "blk"), axis=0, tiled=True).astype(
            jnp.float32
        ),
    )
    gain_one, gain_two = lax.psum((grad_gain1, grad_gain2), ("dp", "blk"))
    return (
        result.astype(jnp.bfloat16)[None],
        input_grad[None],
        gain_one,
        summed[0].reshape(w_qkv.shape),
        summed[1].reshape(w_proj.shape),
        gain_two,
        summed[2].reshape(w_up.shape),
        summed[3].reshape(w_down.shape),
    )


def solution(mesh):
    split = mesh.shape["dp"] == 16 and mesh.shape["blk"] == 2
    return jax.shard_map(
        fast if split else general,
        mesh=mesh,
        in_specs=(
            P("dp", "blk", None),
            P("dp", "blk"),
            P(),
            P(),
            P(),
            P(),
            P(),
            P(),
            P("dp", "blk", None),
        ),
        out_specs=(P("dp", "blk", None), P("dp", "blk", None), P(), P(), P(), P(), P(), P()),
        check_vma=False,
    )
```

```python
import functools
import math

import jax
import jax.numpy as jnp
from jax import lax
from jax.experimental import pallas as pl
from jax.experimental.pallas import tpu as pltpu
from jax.sharding import PartitionSpec as P

HEADS = 12
HD = 64
PAIR = 2 * HD
epsilon = 1e-06
f32 = jnp.float32
bf16 = jnp.bfloat16
NN = ((1,), (0,))
NT = ((1,), (1,))
TN = ((0,), (0,))
AXES = ("dp", "blk")
MIB = 1 << 20


def dot(left, right, dims=NN):
    return lax.dot_general(left, right, (dims, ((), ())), preferred_element_type=f32)


def position_table(visible, width):
    half = width // 2
    column = jnp.arange(half, dtype=f32)
    freqs = jnp.exp(column * (-math.log(10000.0) / half))
    angles = visible.astype(f32)[..., None] * freqs
    return jnp.concatenate([jnp.sin(angles), jnp.cos(angles)], -1)


def normalize(values):
    center = values - jnp.mean(values, -1, keepdims=True)
    spread = jnp.mean(center * center, -1, keepdims=True)
    scale = lax.rsqrt(spread + epsilon)
    return center * scale, scale


def norm_backward(grad, gain, xhat, scale):
    e = grad * gain
    return scale * (
        e - jnp.mean(e, -1, keepdims=True) - xhat * jnp.mean(e * xhat, -1, keepdims=True)
    )


def call(kernel, grid, in_specs, out_specs, out_shape, args, scalars, vmem, scratch=(), aliases=None):
    return pl.pallas_call(
        kernel,
        grid_spec=pltpu.PrefetchScalarGridSpec(
            num_scalar_prefetch=1,
            grid=grid,
            in_specs=in_specs,
            out_specs=out_specs,
            scratch_shapes=list(scratch),
        ),
        out_shape=out_shape,
        input_output_aliases=aliases or {},
        compiler_params=pltpu.CompilerParams(vmem_limit_bytes=28 * MIB),
        cost_estimate=pl.CostEstimate(flops=1, bytes_accessed=1, transcendentals=0),
    )(scalars, *args)


def spec(shape, index):
    return pl.BlockSpec(shape, index)


def whole(array):
    zeros = (0,) * array.ndim
    return pl.BlockSpec(array.shape, lambda i, s: zeros)


def shape(dims, dtype):
    return jax.ShapeDtypeStruct(dims, dtype)


FF_ORDERS = (
    (("z0", "y", "x", "z1"), ("y", "x", "z0", "z1")),
    (("x", "z0", "y", "z1"), ("z0", "y", "x", "z1")),
    (("y", "x", "z0", "z1"), ("x", "z0", "y", "z1")),
)
QKV_ORDER = (("x", "z0", "z1"), ("z0", "x", "z1"))
DP_BIT = {"c": 1, "x": 2, "z0": 4, "z1": 8}


def swap(array, first, second=None):
    second = second or first
    pairs = []
    for d in range(16):
        for b in range(2):
            bit = second if d & 1 else first
            to = (d, b ^ 1) if bit == "y" else (d ^ DP_BIT[bit], b)
            pairs.append((d * 2 + b, to[0] * 2 + to[1]))
    return lax.ppermute(array, AXES, pairs)


def place(order):
    d, b = lax.axis_index("dp"), lax.axis_index("blk")
    code = jnp.int32(0)
    for bit in order:
        value = b & 1 if bit == "y" else (d // DP_BIT[bit]) & 1
        code = code * 2 + value
    return code


def places(orders):
    core = lax.axis_index("dp") & 1
    first, second = place(orders[0]), place(orders[1])
    return jnp.where(core == 0, first, second), jnp.where(core == 0, second, first)


def add(a, b):
    return (a.astype(f32) + b.astype(f32)).astype(bf16)


class Order:
    def __init__(self):
        self.last = None

    def pin(self, *arrays):
        if self.last is None:
            return arrays
        return lax.optimization_barrier((*arrays, self.last))[:-1]

    def run(self, function, *arrays):
        result = function(*self.pin(*arrays))
        self.last = result[0] if isinstance(result, (tuple, list)) else result
        return result

    def swap(self, array, first, second=None):
        return swap(self.pin(array)[0], first, second)


def total(order, keep, send, orders, widen=None):
    received = order.swap(send, "c")
    yield
    count = len(orders[0])
    for step in range(count - 1):
        half = keep.shape[0] // 2
        send = order.run(lambda k, r: add(k[half:], r[half:]), keep, received)
        coming = order.swap(send, orders[0][step], orders[1][step])
        keep = order.run(lambda k, r: add(k[:half], r[:half]), keep, received)
        received = coming
        yield
    keep = order.run(add, keep, received)
    received = order.swap(keep, orders[0][-1], orders[1][-1])
    yield
    block = order.run(lambda k, r: add(k, r[::-1]), keep, received)
    if widen is not None:
        received = order.swap(block, "y")
        yield
        block = order.run(widen, block, received)
    for step in range(count - 2, 0, -1):
        received = order.swap(block, orders[0][step], orders[1][step])
        yield
        block = order.run(lambda k, r: jnp.concatenate([k, r], 0), block, received)
    far = order.swap(block, orders[0][0], orders[1][0])
    other = order.swap(block, "c")
    yield
    far_other = order.swap(far, "c")
    yield block, far, other, far_other


def ln_qkv_kernel(s, tok, pos, gain, w, normed, qkv):
    @pl.when(pl.program_id(0) == 0)
    def _():
        xhat, _ = normalize(tok[...].astype(f32) + pos[...])
        normed[...] = (xhat * gain[...]).astype(bf16)

    qkv[...] = dot(normed[...], w[...]).astype(bf16)


def ln_qkv(scalars, tok, pos, gain, w):
    rows, width = tok.shape
    return call(
        ln_qkv_kernel,
        (3,),
        [whole(tok), whole(pos), whole(gain), spec((width, width), lambda i, s: (0, i))],
        [spec((rows, width), lambda i, s: (0, 0)), spec((rows, width), lambda i, s: (0, i))],
        [shape((rows, width), bf16), shape((rows, 3 * width), bf16)],
        (tok, pos, gain, w),
        scalars,
        24,
    )


def head_masks(x):
    lane = lax.broadcasted_iota(jnp.int32, x.shape, 1)
    return jnp.where(lane < HD, x, 0.0).astype(bf16), jnp.where(lane >= HD, x, 0.0).astype(bf16)


def attn_kernel(s, q, k_own, v_own, k_far, v_far, out):
    rows = q.shape[0]
    k = jnp.concatenate([k_own[...], k_far[...]], 0)
    vt = jnp.concatenate([v_own[...], v_far[...]], 0).T
    parts = []
    for h, qh in enumerate(head_masks(q[...].astype(f32) * HD**-0.5)):
        scores = dot(k, qh, NT)
        e = jnp.exp(scores - jnp.max(scores, 0, keepdims=True))
        total = jnp.sum(e, 0, keepdims=True)
        part = dot(vt[h * HD : (h + 1) * HD], e.astype(bf16))
        parts.append(part * (1.0 / total))
    out[...] = jnp.concatenate(parts, 0).T.astype(bf16)


def attention(scalars, qkv, qkv_far):
    rows, width = qkv.shape[0], qkv.shape[1] // 3
    pairs = width // PAIR

    def column(part):
        return spec((rows, PAIR), lambda i, s: (0, part * pairs + i))

    return call(
        attn_kernel,
        (pairs,),
        [column(0), column(1), column(2), column(1), column(2)],
        spec((rows, PAIR), lambda i, s: (0, i)),
        shape((rows, width), bf16),
        (qkv, qkv, qkv, qkv_far, qkv_far),
        scalars,
        32,
    )


def proj_kernel(s, att, w, tok, pos, gain, resid2, normed2, normed2_t):
    value = tok[...].astype(f32) + pos[...] + dot(att[...], w[...])
    resid2[...] = value
    xhat, _ = normalize(value)
    low = (xhat * gain[...]).astype(bf16)
    normed2[...] = low
    normed2_t[...] = low.T


def project(scalars, att, w, tok, pos, gain):
    rows, width = att.shape
    args = (att, w, tok, pos, gain)
    full = spec((rows, width), lambda i, s: (0, 0))
    return call(
        proj_kernel,
        (1,),
        [whole(a) for a in args],
        [full, full, spec((width, rows), lambda i, s: (0, 0))],
        [shape((rows, width), f32), shape((rows, width), bf16), shape((width, rows), bf16)],
        args,
        scalars,
        24,
    )


def gelu_and_slope(v):
    c = math.sqrt(2.0 / math.pi)
    square = v * v
    t = jnp.tanh(v * (c + (c * 0.044715) * square))
    act = 0.5 * v * (1.0 + t)
    slope = 0.5 * (1.0 + t) + (0.5 * v) * (1.0 - t * t) * (c + (3.0 * c * 0.044715) * square)
    return act, slope


def ff_kernel(at, first, last, s, normed, normed_t, cot, up, down, *refs):
    step = pl.program_id(0)
    if not first:
        out_in, back_in, *refs = refs
    if last:
        resid2, gain, w_own, w_other, *refs = refs
        keep, send, out_low, grad2, branch, g_own, g_other, out, back = refs
    else:
        keep, send, out, back = refs
    hidden = dot(normed[...], up[...])
    act, slope = gelu_and_slope(hidden)
    act = act.astype(bf16)
    grad = (dot(cot[...], down[...], NT) * slope).astype(bf16)
    out_part = dot(act, down[...])
    back_part = dot(grad, up[...], NT)

    @pl.when(step == 0)
    def _():
        out[...] = out_part if first else out_in[...] + out_part
        back[...] = back_part if first else back_in[...] + back_part

    @pl.when(step == 1)
    def _():
        out[...] += out_part
        back[...] += back_part

    g_down = dot(act, cot[...], TN).astype(bf16)
    g_up = dot(normed_t[...], grad).astype(bf16)

    def store(target, code):
        rows_d = g_down.shape[0] // 16
        rows_u = g_up.shape[0] // 16
        half = g_up.shape[1] // 2
        for block in range(16):
            to = block ^ code
            target[to, :rows_d, :] = g_down[block * rows_d : (block + 1) * rows_d]
            part = g_up[block * rows_u : (block + 1) * rows_u]
            target[to, rows_d:, : 2 * half] = part[:rows_d]
            target[to, rows_d : rows_d + 16, 2 * half :] = part[rows_d:, :half]
            target[to, rows_d + 16 :, 2 * half :] = part[rows_d:, half:]

    @pl.when(step == 0)
    def _():
        store(send, s[at + 1])

    @pl.when(step == 1)
    def _():
        store(keep, s[at])
        if last:
            value = resid2[...]
            out_low[...] = (value + out[...]).astype(bf16)
            xhat, scale = normalize(value)
            g = cot[...].astype(f32) + norm_backward(back[...], gain[...], xhat, scale)
            grad2[...] = g
            low = g.astype(bf16)
            branch[...] = low
            g_other[...] = dot(low, w_other[...], NT).astype(bf16)
            g_own[...] = dot(low, w_own[...], NT).astype(bf16)


def ff_chunk(scalars, chunk, last, normed, normed_t, cot, up, down, *more):
    rows, width = normed.shape
    half = width // 2
    wide = 512
    first = chunk == 0

    def column(i, s):
        return 2 * chunk + (s[0] ^ (1 - i))

    full = spec((rows, width), lambda i, s: (0, 0))
    part = spec((rows, half), lambda i, s: (0, 0))
    piece = spec((16, 64, width), lambda i, s: (0, 0, 0))
    in_specs = [
        whole(normed),
        whole(normed_t),
        whole(cot),
        spec((width, wide), lambda i, s: (0, column(i, s))),
        spec((wide, width), lambda i, s: (column(i, s), 0)),
    ]
    out_specs = [piece, piece]
    out_shape = [shape((16, 64, width), bf16)] * 2
    scratch = []
    if not first:
        in_specs += [full, full]
    if last:
        in_specs += [
            full,
            spec((1, width), lambda i, s: (0, 0)),
            spec((half, width), lambda i, s: (s[1], 0)),
            spec((half, width), lambda i, s: (1 - s[1], 0)),
        ]
        out_specs += [full, full, full, part, part]
        out_shape += [shape((rows, width), t) for t in (bf16, f32, bf16)]
        out_shape += [shape((rows, half), bf16)] * 2
        scratch = [pltpu.VMEM((rows, width), f32)] * 2
    else:
        out_specs += [full, full]
        out_shape += [shape((rows, width), f32)] * 2
    return call(
        functools.partial(ff_kernel, 2 + 2 * chunk, first, last),
        (2,),
        in_specs,
        out_specs,
        out_shape,
        (normed, normed_t, cot, up, down) + more,
        scalars,
        40,
        scratch,
    )


def attn_back_kernel(s, q, g, k_o, k_f, v_o, v_f, *refs):
    gk_in, gv_in = refs[:2] if len(refs) == 5 else (None, None)
    gq, gk, gv = refs[-3:]
    k = jnp.concatenate([k_o[...], k_f[...]], 0)
    v = jnp.concatenate([v_o[...], v_f[...]], 0)
    kt = (k.astype(f32) * HD**-0.5).astype(bf16).T
    grad_q = []
    grad_k, grad_v = (gk_in[...], gv_in[...]) if gk_in is not None else (0.0, 0.0)
    q_heads = head_masks(q[...].astype(f32) * HD**-0.5)
    g_heads = head_masks(g[...].astype(f32))
    for h, (qh, gh) in enumerate(zip(q_heads, g_heads)):
        scores = dot(k, qh, NT)
        e = jnp.exp(scores - jnp.max(scores, 0, keepdims=True))
        probs = e * (1.0 / jnp.sum(e, 0, keepdims=True))
        grad_v = grad_v + dot(probs.astype(bf16), gh)
        grad_p = dot(v, gh, NT)
        row = jnp.sum(probs * grad_p, 0, keepdims=True)
        grad_s = (probs * (grad_p - row)).astype(bf16)
        grad_k = grad_k + dot(grad_s, qh)
        grad_q.append(dot(kt[h * HD : (h + 1) * HD], grad_s))
    gq[...] = jnp.concatenate(grad_q, 0).T.astype(bf16)
    gk[...] = grad_k.astype(gk.dtype)
    gv[...] = grad_v.astype(gv.dtype)


def attention_back(scalars, far, qkv, qkv_far, grad, *so_far):
    rows, width = qkv.shape[0], qkv.shape[1] // 3
    pairs = width // PAIR
    mine = pairs // 2

    def column(part):
        return spec((rows, PAIR), lambda i, s: (0, part * pairs + mine * s[1] + i))

    block = spec((rows, PAIR), lambda i, s: (0, i))
    both = spec((2 * rows, PAIR), lambda i, s: (0, i))
    dtype = bf16 if so_far else f32
    return call(
        attn_back_kernel,
        (mine,),
        [column(0), block, column(1), column(1), column(2), column(2)] + [both] * len(so_far),
        [block, both, both],
        [shape((rows, width // 2), bf16)] + [shape((2 * rows, width // 2), dtype)] * 2,
        (qkv_far if far else qkv, grad, qkv, qkv_far, qkv, qkv_far) + so_far,
        scalars,
        48,
    )


def joint_kernel(s, n_own, n_far, gq_o, gq_f, gk, gv, att, branch, keep, send):
    step = pl.program_id(0)
    gq = jnp.concatenate([gq_o[...], gq_f[...]], 0)
    n = jnp.concatenate([n_own[...], n_far[...]], 0)
    cols = gk.shape[1]

    def fill(target, code):
        tiles = [dot(n, g, TN).astype(bf16) for g in (gq, gk[...], gv[...])]
        tiles.append(dot(att[...], branch[...], TN).astype(bf16))
        rows = tiles[0].shape[0] // 8
        for block in range(8):
            at = block ^ code
            for i, tile in enumerate(tiles):
                part = tile[block * rows : (block + 1) * rows]
                target[at, :, i * cols : i * cols + part.shape[1]] = part

    @pl.when(step == 0)
    def _():
        fill(send, s[9])

    @pl.when(step == 1)
    def _():
        fill(keep, s[8])


def joint_grads(scalars, n_own, n_far, gq, gq_far, gk, gv, att, branch):
    rows, width = n_own.shape
    half = width // 2
    feature = spec((rows, half), lambda i, s: (0, s[0] ^ (1 - i)))
    cols = 3 * half + width
    piece = spec((8, half // 8, cols), lambda i, s: (0, 0, 0))
    return call(
        joint_kernel,
        (2,),
        [feature, feature, whole(gq), whole(gq), whole(gk), whole(gv), feature, whole(branch)],
        [piece, piece],
        [shape((8, half // 8, cols), bf16)] * 2,
        (n_own, n_far, gq, gq_far, gk, gv, att, branch),
        scalars,
        32,
    )


def back_qkv_kernel(s, gq_o, gq_f, gk, gv, wq, wk, wv, own, far):
    rows = own.shape[0]

    def part(gq, at):
        total = dot(gq[...], wq[...], NT)
        total += dot(gk[pl.ds(at, rows)], wk[...], NT)
        return total + dot(gv[pl.ds(at, rows)], wv[...], NT)

    far[...] = part(gq_f, rows).astype(bf16)
    own[...] = part(gq_o, 0)


def back_qkv(scalars, gq, gq_far, gk, gv, w):
    rows, half = gq.shape
    width = 2 * half

    def column(part):
        return spec((width, half), lambda i, s: (0, 2 * part + s[1]))

    full = spec((rows, width), lambda i, s: (0, 0))
    return call(
        back_qkv_kernel,
        (1,),
        [whole(gq), whole(gq), whole(gk), whole(gv), column(0), column(1), column(2)],
        [full, full],
        [shape((rows, width), f32), shape((rows, width), bf16)],
        (gq, gq_far, gk, gv, w, w, w),
        scalars,
        32,
    )


def last_kernel(s, own, far, tok, pos, gain, grad2, out):
    xhat, scale = normalize(tok[...].astype(f32) + pos[...])
    grad = own[...] + far[...].astype(f32)
    out[...] = grad2[...] + norm_backward(grad, gain[...], xhat, scale)


def token_grad(scalars, own, far, tok, pos, gain, grad2):
    args = (own, far, tok, pos, gain, grad2)
    return call(
        last_kernel,
        (1,),
        [whole(a) for a in args],
        whole(own),
        shape(own.shape, f32),
        args,
        scalars,
        24,
    )


def unpack_ff_kernel(at, s, near, far, *refs):
    down, up = refs[-2:]
    step = pl.program_id(0)
    low = s[at] & 7

    def unpack(source):
        for block in range(8):
            at = block ^ low
            down[pl.ds(pl.multiple_of(at * 32, 32), 32), :] = source[block, :32, :].astype(f32)
            row = pl.multiple_of(at * 48, 16)
            up[pl.ds(row, 32), :] = source[block, 32:, :512].astype(f32)
            up[pl.ds(row + 32, 16), :256] = source[block, 32:48, 512:].astype(f32)
            up[pl.ds(row + 32, 16), 256:] = source[block, 48:, 512:].astype(f32)

    @pl.when(step == 0)
    def _():
        unpack(near)

    @pl.when(step == 1)
    def _():
        unpack(far)


def unpack_ff(scalars, chunk, other, near, far, width, hidden, so_far):
    at = 2 + 2 * chunk + other

    def side(i, s):
        return i ^ (s[at] // 8)

    def half(s):
        return 2 * chunk + (s[0] ^ other)

    any_spec = pl.BlockSpec(memory_space=pl.ANY)
    return call(
        functools.partial(unpack_ff_kernel, at),
        (2,),
        [whole(near), whole(far)] + [any_spec] * len(so_far),
        [
            spec((256, width), lambda i, s: (2 * half(s) + side(i, s), 0)),
            spec((width // 2, 512), lambda i, s: (side(i, s), half(s))),
        ],
        [shape((hidden, width), f32), shape((width, hidden), f32)],
        (near, far) + tuple(so_far),
        scalars,
        32,
        aliases={3: 0, 4: 1} if so_far else None,
    )


def unpack_qkv_kernel(at, s, near, far, *refs):
    joint, proj = refs[-2:]
    step = pl.program_id(0)
    low = s[at] & 3
    mine = s[1]

    def unpack(source):
        half = source.shape[2] // 8
        for block in range(4):
            at = pl.multiple_of((block ^ low) * 48, 16)
            rows = pl.ds(at, 48)
            for part in range(3):
                for side in range(2):
                    column = pl.multiple_of(2 * half * part + half * (mine ^ side), 128)
                    value = source[block, :, (3 * side + part) * half : (3 * side + part + 1) * half]
                    joint[rows, pl.ds(column, half)] = value.astype(f32)
            proj[rows, :] = source[block, :, 6 * half :].astype(f32)

    @pl.when(step == 0)
    def _():
        unpack(near)

    @pl.when(step == 1)
    def _():
        unpack(far)


def unpack_qkv(scalars, other, near, far, width, so_far):
    at = 8 + other

    def row(i, s):
        return 2 * (s[0] ^ other) + (i ^ (s[at] // 4))

    any_spec = pl.BlockSpec(memory_space=pl.ANY)
    return call(
        functools.partial(unpack_qkv_kernel, at),
        (2,),
        [whole(near), whole(far)] + [any_spec] * len(so_far),
        [
            spec((width // 4, 3 * width), lambda i, s: (row(i, s), 0)),
            spec((width // 4, width), lambda i, s: (row(i, s), 0)),
        ],
        [shape((width, 3 * width), f32), shape((width, width), f32)],
        (near, far) + tuple(so_far),
        scalars,
        32,
        aliases={3: 0, 4: 1} if so_far else None,
    )


def fast(tokens, visible, ln1_gain, w_qkv, w_proj, ln2_gain, w_up, w_down, d_out):
    tok, cot = tokens[0], d_out[0]
    rows, width = tok.shape
    hidden = w_up.shape[1]
    gain1, gain2 = ln1_gain[None], ln2_gain[None]
    scalars = [lax.axis_index("dp") & 1, lax.axis_index("blk")]
    for orders in FF_ORDERS + (QKV_ORDER,):
        scalars.extend(places(orders))
    scalars = jnp.stack([jnp.int32(v) for v in scalars])

    order = Order()
    run = order.run
    vis_far = swap(visible, "y")[0]
    tok_far = swap(tok, "y")
    pos = position_table(visible[0], width)
    pos_far = position_table(vis_far, width)
    normed1, qkv = run(functools.partial(ln_qkv, scalars), tok, pos, gain1, w_qkv)
    normed1_far, qkv_far = run(functools.partial(ln_qkv, scalars), tok_far, pos_far, gain1, w_qkv)
    attended = run(functools.partial(attention, scalars), qkv, qkv_far)
    resid2, normed2, normed2_t = run(functools.partial(project, scalars), attended, w_proj, tok, pos, gain2)

    streams, near = [], [None] * 4

    def go(*which):
        for i in which:
            near[i] = next(streams[i], near[i])

    def feed_forward(chunk, *more):
        keep, send, *rest = run(
            functools.partial(ff_chunk, scalars, chunk, chunk == 2),
            normed2, normed2_t, cot, w_up, w_down, *more,
        )
        streams.append(total(order, keep, send, FF_ORDERS[chunk]))
        return rest

    sums = feed_forward(0)
    go(0)
    sums = feed_forward(1, *sums)
    go(0, 1)
    out, grad2, branch, g_own, g_other = feed_forward(2, *sums, resid2, gain2, w_proj, w_proj)
    g_far = order.swap(g_other, "y")
    go(0, 1, 2)
    gq, *sums = run(functools.partial(attention_back, scalars, False), qkv, qkv_far, g_own)
    go(0, 1, 2)
    gq_far, gk, gv = run(functools.partial(attention_back, scalars, True), qkv, qkv_far, g_far, *sums)
    go(0, 1, 2)
    keep, send = run(
        functools.partial(joint_grads, scalars),
        normed1, normed1_far, gq, gq_far, gk, gv, attended, branch,
    )
    cut = 3 * (width // 2)

    def widen(mine, theirs):
        proj = add(mine[..., cut:], theirs[..., cut:])
        return jnp.concatenate([mine[..., :cut], theirs[..., :cut], proj], -1)

    streams.append(total(order, keep, send, QKV_ORDER, widen))
    go(3, 0, 1, 2)
    back_own, back_far = run(functools.partial(back_qkv, scalars), gq, gq_far, gk, gv, w_qkv)
    back_far = order.swap(back_far, "y")
    go(3, 0, 1, 2)
    go(3, 0, 1, 2)
    go(3, 0, 1, 2)
    d_tokens = run(functools.partial(token_grad, scalars), back_own, back_far, tok, pos, gain1, grad2)
    go(3, 0, 1, 2)

    ff = ()

    def finish(chunk, other):
        nonlocal ff
        ff = run(
            lambda a, b, *f: unpack_ff(scalars, chunk, other, a, b, width, hidden, f),
            near[chunk][2 * other], near[chunk][2 * other + 1], *ff,
        )

    go(3, 0, 1, 2)
    finish(0, 0)
    go(3, 1, 2)
    finish(0, 1)
    finish(1, 0)
    finish(2, 0)
    finish(1, 1)
    finish(2, 1)
    go(3)
    qkvp = ()
    for other in range(2):
        qkvp = run(
            lambda a, b, *f: unpack_qkv(scalars, other, a, b, width, f),
            near[3][2 * other], near[3][2 * other + 1], *qkvp,
        )
    d_down, d_up = ff
    d_qkv, d_proj = qkvp
    d_gain1 = jnp.sum(w_qkv.astype(f32) * d_qkv, 1) / ln1_gain
    d_gain2 = jnp.sum(w_up.astype(f32) * d_up, 1) / ln2_gain
    return out[None], d_tokens[None], d_gain1, d_qkv, d_proj, d_gain2, d_up, d_down


def layer_norm(values, gain):
    center = values - jnp.mean(values, -1, keepdims=True)
    spread = jnp.mean(center * center, -1, keepdims=True)
    return center * lax.rsqrt(spread + epsilon) * gain


def outer_product(left, right):
    return lax.dot_general(
        left, right, (((0,), (0,)), ((), ())), preferred_element_type=jnp.float32
    )


def times_transposed(left, weight):
    return lax.dot_general(
        left, weight, (((1,), (1,)), ((), ())), preferred_element_type=jnp.float32
    )


def split_blocks(keys, values):
    count = keys.shape[0]
    size = math.gcd(count, 512)
    shape = (count // size, size, HEADS, HD)
    return (keys.reshape(shape), values.reshape(shape))


def general(tokens, visible, ln1_gain, w_qkv, w_proj, ln2_gain, w_up, w_down, d_out):
    rows = tokens.shape[1]
    width = tokens.shape[2]
    factor = HD ** (-0.5)
    resid = tokens[0].astype(jnp.float32) + position_table(visible[0], width)
    normed1, back_one = jax.vjp(layer_norm, resid, ln1_gain)
    normed1 = normed1.astype(jnp.bfloat16)
    qkv = jnp.dot(normed1, w_qkv, preferred_element_type=jnp.float32).astype(jnp.bfloat16)
    query = qkv[:, :width]
    keys = qkv[:, width : 2 * width]
    values = qkv[:, 2 * width :]
    query_heads = query.reshape(rows, HEADS, HD)
    initial = (
        jnp.full((HEADS, rows), -1e30, jnp.float32),
        jnp.zeros((HEADS, rows), jnp.float32),
        jnp.zeros((HEADS, rows, HD), jnp.float32),
    )
    key_blocks, value_blocks = split_blocks(
        lax.all_gather(keys, "blk", axis=0, tiled=True),
        lax.all_gather(values, "blk", axis=0, tiled=True),
    )

    def one_block(state, block):
        running, total, accum = state
        block_keys, block_values = block
        scores = (
            jnp.einsum("qhd,khd->hqk", query_heads, block_keys, preferred_element_type=jnp.float32)
            * factor
        )
        top = jnp.maximum(running, jnp.max(scores, -1))
        weights = jnp.exp(scores - top[..., None])
        shrink = jnp.exp(running - top)
        total = total * shrink + jnp.sum(weights, -1)
        accum = accum * shrink[..., None] + jnp.einsum(
            "hqk,khd->hqd",
            weights.astype(jnp.bfloat16),
            block_values,
            preferred_element_type=jnp.float32,
        )
        return ((top, total, accum), None)

    running, total, accum = lax.scan(one_block, initial, (key_blocks, value_blocks))[0]
    log_total = running + jnp.log(total)
    attended = (accum / total[..., None]).transpose(1, 0, 2).reshape(rows, width)
    attended_low = attended.astype(jnp.bfloat16)
    resid2 = resid + jnp.dot(attended_low, w_proj, preferred_element_type=jnp.float32)
    normed2, back_two = jax.vjp(layer_norm, resid2, ln2_gain)
    normed2 = normed2.astype(jnp.bfloat16)
    hidden = jnp.dot(normed2, w_up, preferred_element_type=jnp.float32)
    activated, back_gelu = jax.vjp(jax.nn.gelu, hidden)
    activated = activated.astype(jnp.bfloat16)
    result = resid2 + jnp.dot(activated, w_down, preferred_element_type=jnp.float32)
    cotangent = d_out[0]
    grad_down = outer_product(activated, cotangent)
    (grad_hidden,) = back_gelu(times_transposed(cotangent, w_down))
    grad_hidden = grad_hidden.astype(jnp.bfloat16)
    grad_up = outer_product(normed2, grad_hidden)
    grad_resid2, grad_gain2 = back_two(times_transposed(grad_hidden, w_up))
    grad_resid2 = grad_resid2 + cotangent.astype(jnp.float32)
    grad_branch = grad_resid2.astype(jnp.bfloat16)
    grad_proj = outer_product(attended_low, grad_branch)
    grad_attended = times_transposed(grad_branch, w_proj).astype(jnp.bfloat16)
    correction = (grad_attended.astype(jnp.float32) * attended).reshape(rows, HEADS, HD)
    correction = jnp.sum(correction, -1).T
    grad_heads = grad_attended.reshape(rows, HEADS, HD)
    all_keys, all_values = (
        lax.all_gather(keys, "blk", axis=0, tiled=True),
        lax.all_gather(values, "blk", axis=0, tiled=True),
    )
    full_rows = all_keys.shape[0]
    key_blocks, value_blocks = split_blocks(all_keys, all_values)

    def back_block(grad_query, block):
        block_keys, block_values = block
        scores = (
            jnp.einsum("qhd,khd->hqk", query_heads, block_keys, preferred_element_type=jnp.float32)
            * factor
        )
        probs = jnp.exp(scores - log_total[..., None])
        grad_value = jnp.einsum(
            "hqk,qhd->khd",
            probs.astype(jnp.bfloat16),
            grad_heads,
            preferred_element_type=jnp.float32,
        )
        grad_probs = jnp.einsum(
            "qhd,khd->hqk", grad_heads, block_values, preferred_element_type=jnp.float32
        )
        grad_scores = (probs * (grad_probs - correction[..., None])).astype(jnp.bfloat16)
        grad_query = grad_query + jnp.einsum(
            "hqk,khd->qhd", grad_scores, block_keys, preferred_element_type=jnp.float32
        )
        grad_key = (
            jnp.einsum("hqk,qhd->khd", grad_scores, query_heads, preferred_element_type=jnp.float32)
            * factor
        )
        return (grad_query, (grad_key, grad_value))

    grad_query, (key_parts, value_parts) = lax.scan(
        back_block, jnp.zeros((rows, HEADS, HD), jnp.float32), (key_blocks, value_blocks)
    )
    grad_query = (grad_query * factor).reshape(rows, width)
    grad_keys, grad_values = (
        lax.psum_scatter(
            key_parts.reshape(full_rows, width).astype(jnp.bfloat16),
            "blk",
            scatter_dimension=0,
            tiled=True,
        ).astype(jnp.float32),
        lax.psum_scatter(
            value_parts.reshape(full_rows, width).astype(jnp.bfloat16),
            "blk",
            scatter_dimension=0,
            tiled=True,
        ).astype(jnp.float32),
    )
    grad_qkv = jnp.concatenate([grad_query, grad_keys, grad_values], 1).astype(jnp.bfloat16)
    grad_joint = outer_product(normed1, grad_qkv)
    grad_resid, grad_gain1 = back_one(times_transposed(grad_qkv, w_qkv))
    input_grad = grad_resid2 + grad_resid
    flats = (
        grad_joint.reshape(-1),
        grad_proj.reshape(-1),
        grad_up.reshape(-1),
        grad_down.reshape(-1),
    )
    shares = (
        lax.psum_scatter(flats[0], ("dp", "blk"), scatter_dimension=0, tiled=True),
        lax.psum_scatter(flats[1], ("dp", "blk"), scatter_dimension=0, tiled=True),
        lax.psum_scatter(flats[2], ("dp", "blk"), scatter_dimension=0, tiled=True),
        lax.psum_scatter(flats[3], ("dp", "blk"), scatter_dimension=0, tiled=True),
    )
    summed = (
        lax.all_gather(shares[0].astype(jnp.bfloat16), ("dp", "blk"), axis=0, tiled=True).astype(
            jnp.float32
        ),
        lax.all_gather(shares[1].astype(jnp.bfloat16), ("dp", "blk"), axis=0, tiled=True).astype(
            jnp.float32
        ),
        lax.all_gather(shares[2].astype(jnp.bfloat16), ("dp", "blk"), axis=0, tiled=True).astype(
            jnp.float32
        ),
        lax.all_gather(shares[3].astype(jnp.bfloat16), ("dp", "blk"), axis=0, tiled=True).astype(
            jnp.float32
        ),
    )
    gain_one, gain_two = lax.psum((grad_gain1, grad_gain2), ("dp", "blk"))
    return (
        result.astype(jnp.bfloat16)[None],
        input_grad[None],
        gain_one,
        summed[0].reshape(w_qkv.shape),
        summed[1].reshape(w_proj.shape),
        gain_two,
        summed[2].reshape(w_up.shape),
        summed[3].reshape(w_down.shape),
    )


def solution(mesh):
    split = mesh.shape["dp"] == 16 and mesh.shape["blk"] == 2
    return jax.shard_map(
        fast if split else general,
        mesh=mesh,
        in_specs=(
            P("dp", "blk", None),
            P("dp", "blk"),
            P(),
            P(),
            P(),
            P(),
            P(),
            P(),
            P("dp", "blk", None),
        ),
        out_specs=(P("dp", "blk", None), P("dp", "blk", None), P(), P(), P(), P(), P(), P()),
        check_vma=False,
    )
```

```python
import functools
import math

import jax
import jax.numpy as jnp
from jax import lax
from jax.experimental import pallas as pl
from jax.experimental.pallas import tpu as pltpu
from jax.sharding import PartitionSpec as P

HEADS = 12
HD = 64
PAIR = 2 * HD
epsilon = 1e-06
f32 = jnp.float32
bf16 = jnp.bfloat16
NN = ((1,), (0,))
NT = ((1,), (1,))
TN = ((0,), (0,))
AXES = ("dp", "blk")
MIB = 1 << 20


def dot(left, right, dims=NN):
    return lax.dot_general(left, right, (dims, ((), ())), preferred_element_type=f32)


def position_table(visible, width):
    half = width // 2
    column = jnp.arange(half, dtype=f32)
    freqs = jnp.exp(column * (-math.log(10000.0) / half))
    angles = visible.astype(f32)[..., None] * freqs
    return jnp.concatenate([jnp.sin(angles), jnp.cos(angles)], -1)


def normalize(values):
    center = values - jnp.mean(values, -1, keepdims=True)
    spread = jnp.mean(center * center, -1, keepdims=True)
    scale = lax.rsqrt(spread + epsilon)
    return center * scale, scale


def norm_backward(grad, gain, xhat, scale):
    e = grad * gain
    return scale * (
        e - jnp.mean(e, -1, keepdims=True) - xhat * jnp.mean(e * xhat, -1, keepdims=True)
    )


def call(kernel, grid, in_specs, out_specs, out_shape, args, scalars, vmem, scratch=(), aliases=None):
    return pl.pallas_call(
        kernel,
        grid_spec=pltpu.PrefetchScalarGridSpec(
            num_scalar_prefetch=1,
            grid=grid,
            in_specs=in_specs,
            out_specs=out_specs,
            scratch_shapes=list(scratch),
        ),
        out_shape=out_shape,
        input_output_aliases=aliases or {},
        compiler_params=pltpu.CompilerParams(vmem_limit_bytes=28 * MIB),
        cost_estimate=pl.CostEstimate(flops=1, bytes_accessed=1, transcendentals=0),
    )(scalars, *args)


def spec(shape, index):
    return pl.BlockSpec(shape, index)


def whole(array):
    zeros = (0,) * array.ndim
    return pl.BlockSpec(array.shape, lambda i, s: zeros)


def shape(dims, dtype):
    return jax.ShapeDtypeStruct(dims, dtype)


FF_ORDERS = (
    (("y", "x", "z0", "z1"), ("x", "z0", "y", "z1")),
    (("z0", "x", "y", "z1"), ("x", "y", "z0", "z1")),
    (("x", "y", "z0", "z1"), ("z0", "x", "y", "z1")),
)
QKV_ORDER = (("x", "z0", "z1"), ("z0", "x", "z1"))
PLAN = (
    ("ff", 0), ("ff", 1), ("wait", "e0"), ("wait", "early"), ("ff", 2), ("dw", 0),
    ("wait", "branch_other"), ("wait", "e1"), ("dw", 1), ("own",), ("wait", "g"), ("go", 0),
    ("wait", "e2"), ("dw", 2), ("far",), ("go", 0), ("go", 1), ("joint",), ("go", 0), ("go", 2),
    ("go", 1), ("go", 3), ("back",), ("go", 0), ("go", 1), ("go", 2), ("go", 0), ("go", 2),
    ("go", 3), ("go", 1), ("go", 0), ("go", 3), ("wait", "bf"), ("go", 2), ("go", 1), ("go", 2),
    ("go", 0), ("tokens",), ("go", 1), ("unpack", 0, 0), ("go", 3), ("go", 2), ("unpack", 1, 0),
    ("unpack", 0, 1), ("go", 3), ("go", 1), ("go", 3), ("go", 2), ("unpack", 1, 1),
    ("unpack", 2, 0), ("unpack", 3, 0), ("go", 3), ("unpack", 2, 1), ("unpack", 3, 1),
)
DP_BIT = {"c": 1, "x": 2, "z0": 4, "z1": 8}


def swap(array, first, second=None):
    second = second or first
    pairs = []
    for d in range(16):
        for b in range(2):
            bit = second if d & 1 else first
            to = (d, b ^ 1) if bit == "y" else (d ^ DP_BIT[bit], b)
            pairs.append((d * 2 + b, to[0] * 2 + to[1]))
    return lax.ppermute(array, AXES, pairs)


def place(order):
    d, b = lax.axis_index("dp"), lax.axis_index("blk")
    code = jnp.int32(0)
    for bit in order:
        value = b & 1 if bit == "y" else (d // DP_BIT[bit]) & 1
        code = code * 2 + value
    return code


def places(orders):
    core = lax.axis_index("dp") & 1
    first, second = place(orders[0]), place(orders[1])
    return jnp.where(core == 0, first, second), jnp.where(core == 0, second, first)


def add(a, b):
    return (a.astype(f32) + b.astype(f32)).astype(bf16)


class Order:
    def __init__(self):
        self.last = None

    def pin(self, *arrays):
        if self.last is None:
            return arrays
        return lax.optimization_barrier((*arrays, self.last))[:-1]

    def run(self, function, *arrays):
        result = function(*self.pin(*arrays))
        self.last = result[0] if isinstance(result, (tuple, list)) else result
        return result

    def swap(self, array, first, second=None):
        return swap(self.pin(array)[0], first, second)


def total(order, keep, send, links, widen=None):
    received = order.swap(send, *links[0])
    yield
    for link in links[1:-1]:
        half = keep.shape[0] // 2
        send = order.run(lambda k, r: add(k[half:], r[half:]), keep, received)
        coming = order.swap(send, *link)
        keep = order.run(lambda k, r: add(k[:half], r[:half]), keep, received)
        received = coming
        yield
    keep = order.run(add, keep, received)
    received = order.swap(keep, *links[-1])
    yield
    block = order.run(lambda k, r: add(k, r[::-1]), keep, received)
    if widen is not None:
        received = order.swap(block, "y")
        yield
        block = order.run(widen, block, received)
    back = [link for link in links[:-1] if link[0] != "c"][::-1]
    for link in back[:-1]:
        received = order.swap(block, *link)
        yield
        block = order.run(lambda k, r: jnp.concatenate([k, r], 0), block, received)
    far = order.swap(block, *back[-1])
    other = order.swap(block, "c")
    yield block, other
    far = order.run(lambda value: value, far)
    yield far, order.swap(far, "c")


def ln_qkv_kernel(s, tok, pos, gain, w, normed, qkv):
    @pl.when(pl.program_id(0) == 0)
    def _():
        xhat, _ = normalize(tok[...].astype(f32) + pos[...])
        normed[...] = (xhat * gain[...]).astype(bf16)

    qkv[...] = dot(normed[...], w[...]).astype(bf16)


def ln_qkv(scalars, tok, pos, gain, w):
    rows, width = tok.shape
    return call(
        ln_qkv_kernel,
        (3,),
        [whole(tok), whole(pos), whole(gain), spec((width, width), lambda i, s: (0, i))],
        [spec((rows, width), lambda i, s: (0, 0)), spec((rows, width), lambda i, s: (0, i))],
        [shape((rows, width), bf16), shape((rows, 3 * width), bf16)],
        (tok, pos, gain, w),
        scalars,
        24,
    )


def head_masks(x):
    lane = lax.broadcasted_iota(jnp.int32, x.shape, 1)
    return jnp.where(lane < HD, x, 0.0).astype(bf16), jnp.where(lane >= HD, x, 0.0).astype(bf16)


def attn_kernel(s, q, k_own, v_own, k_far, v_far, out):
    rows = q.shape[0]
    k = jnp.concatenate([k_own[...], k_far[...]], 0)
    vt = jnp.concatenate([v_own[...], v_far[...]], 0).T
    parts = []
    for h, qh in enumerate(head_masks(q[...].astype(f32) * HD**-0.5)):
        scores = dot(k, qh, NT)
        e = jnp.exp(scores - jnp.max(scores, 0, keepdims=True))
        total = jnp.sum(e, 0, keepdims=True)
        part = dot(vt[h * HD : (h + 1) * HD], e.astype(bf16))
        parts.append(part * (1.0 / total))
    out[...] = jnp.concatenate(parts, 0).T.astype(bf16)


def attention(scalars, qkv, qkv_far):
    rows, width = qkv.shape[0], qkv.shape[1] // 3
    pairs = width // PAIR

    def column(part):
        return spec((rows, PAIR), lambda i, s: (0, part * pairs + i))

    return call(
        attn_kernel,
        (pairs,),
        [column(0), column(1), column(2), column(1), column(2)],
        spec((rows, PAIR), lambda i, s: (0, i)),
        shape((rows, width), bf16),
        (qkv, qkv, qkv, qkv_far, qkv_far),
        scalars,
        32,
    )


def proj_kernel(s, att, att_half, w, tok, pos, gain, resid2, normed2, normed2_t, att_send):
    att_send[...] = att_half[...]
    value = tok[...].astype(f32) + pos[...] + dot(att[...], w[...])
    resid2[...] = value
    xhat, _ = normalize(value)
    low = (xhat * gain[...]).astype(bf16)
    normed2[...] = low
    normed2_t[...] = low.T


def project(scalars, att, w, tok, pos, gain):
    rows, width = att.shape
    full = spec((rows, width), lambda i, s: (0, 0))
    half = spec((rows, width // 2), lambda i, s: (0, 1 - s[0]))
    return call(
        proj_kernel,
        (1,),
        [full, half, whole(w), full, full, whole(gain)],
        [
            full,
            full,
            spec((width, rows), lambda i, s: (0, 0)),
            spec((rows, width // 2), lambda i, s: (0, 0)),
        ],
        [
            shape((rows, width), f32),
            shape((rows, width), bf16),
            shape((width, rows), bf16),
            shape((rows, width // 2), bf16),
        ],
        (att, att, w, tok, pos, gain),
        scalars,
        24,
    )


def gelu_and_slope(v):
    c = math.sqrt(2.0 / math.pi)
    square = v * v
    t = jnp.tanh(v * (c + (c * 0.044715) * square))
    act = 0.5 * v * (1.0 + t)
    slope = 0.5 * (1.0 + t) + (0.5 * v) * (1.0 - t * t) * (c + (3.0 * c * 0.044715) * square)
    return act, slope


def ff_kernel(first, last, s, normed, cot, up, down, *refs):
    step = pl.program_id(0)
    if not first:
        out_in, back_in, *refs = refs
    if last:
        resid2, gain, w_own, w_other, *refs = refs
        keep, send, out_low, grad2, branch, g_own, g_other, out, back = refs
    else:
        keep, send, out, back = refs
    hidden = dot(normed[...], up[...])
    act, slope = gelu_and_slope(hidden)
    act = act.astype(bf16)
    grad = (dot(cot[...], down[...], NT) * slope).astype(bf16)
    out_part = dot(act, down[...])
    back_part = dot(grad, up[...], NT)

    @pl.when(step == 0)
    def _():
        send[0] = act
        send[1] = grad
        out[...] = out_part if first else out_in[...] + out_part
        back[...] = back_part if first else back_in[...] + back_part

    @pl.when(step == 1)
    def _():
        keep[0] = act
        keep[1] = grad
        out[...] += out_part
        back[...] += back_part
        if last:
            value = resid2[...]
            out_low[...] = (value + out[...]).astype(bf16)
            xhat, scale = normalize(value)
            g = cot[...].astype(f32) + norm_backward(back[...], gain[...], xhat, scale)
            grad2[...] = g
            low = g.astype(bf16)
            branch[...] = low
            g_other[...] = dot(low, w_other[...], NT).astype(bf16)
            g_own[...] = dot(low, w_own[...], NT).astype(bf16)


def ff_chunk(scalars, chunk, last, normed, cot, up, down, *more):
    rows, width = normed.shape
    half = width // 2
    wide = 512
    first = chunk == 0

    def column(i, s):
        return 2 * chunk + (s[0] ^ (1 - i))

    full = spec((rows, width), lambda i, s: (0, 0))
    part = spec((rows, half), lambda i, s: (0, 0))
    piece = spec((2, rows, wide), lambda i, s: (0, 0, 0))
    in_specs = [
        whole(normed),
        whole(cot),
        spec((width, wide), lambda i, s: (0, column(i, s))),
        spec((wide, width), lambda i, s: (column(i, s), 0)),
    ]
    out_specs = [piece, piece]
    out_shape = [shape((2, rows, wide), bf16)] * 2
    scratch = []
    if not first:
        in_specs += [full, full]
    if last:
        in_specs += [
            full,
            spec((1, width), lambda i, s: (0, 0)),
            spec((half, width), lambda i, s: (s[1], 0)),
            spec((half, width), lambda i, s: (1 - s[1], 0)),
        ]
        out_specs += [full, full, full, part, part]
        out_shape += [shape((rows, width), t) for t in (bf16, f32, bf16)]
        out_shape += [shape((rows, half), bf16)] * 2
        scratch = [pltpu.VMEM((rows, width), f32)] * 2
    else:
        out_specs += [full, full]
        out_shape += [shape((rows, width), f32)] * 2
    return call(
        functools.partial(ff_kernel, first, last),
        (2,),
        in_specs,
        out_specs,
        out_shape,
        (normed, cot, up, down) + more,
        scalars,
        40,
        scratch,
    )


def ff_grads_kernel(at, s, act, act_o, grad, grad_o, cot, cot_o, nt, nt_o, *refs):
    keep, send = refs[-2:]
    step = pl.program_id(0)
    rows_both = jnp.concatenate([cot[...], cot_o[...]], 0)
    g_down = dot(jnp.concatenate([act[0], act_o[0]], 0), rows_both, TN).astype(bf16)
    grads = jnp.concatenate([grad[0], grad_o[0]], 0)
    g_up = dot(jnp.concatenate([nt[...], nt_o[...]], 1), grads).astype(bf16)
    g_proj = None
    if len(refs) > 2:
        att, att_o, branch, branch_o = refs[:4]
        both = jnp.concatenate([branch[...], branch_o[...]], 0)
        g_proj = dot(jnp.concatenate([att[...], att_o[...]], 0), both, TN).astype(bf16)
    code = s[at] & 7

    def store(target):
        rows_d = g_down.shape[0] // 8
        rows_u = g_up.shape[0] // 8
        half = g_up.shape[1] // 2
        for block in range(8):
            to = block ^ code
            target[to, :rows_d, :] = g_down[block * rows_d : (block + 1) * rows_d]
            part = g_up[block * rows_u : (block + 1) * rows_u]
            target[to, 32:64, : 2 * half] = part[:32]
            target[to, 32:48, 2 * half :] = part[32:, :half]
            target[to, 48:64, 2 * half :] = part[32:, half:]
            if g_proj is not None:
                part = g_proj[block * rows_u : (block + 1) * rows_u]
                wide = part.shape[1]
                target[to, 64:80, :wide] = part[:16]
                target[to, 64:80, wide:] = part[16:32]
                target[to, 80:, :wide] = part[32:]
                target[to, 80:, wide:] = jnp.zeros_like(part[32:])

    @pl.when(step == 0)
    def _():
        store(send)

    @pl.when(step == 1)
    def _():
        store(keep)


def ff_grads(scalars, chunk, mine, theirs, cot, cot_other, normed_t_other, normed_t, *proj):
    rows, width = cot.shape
    wide = mine.shape[2]
    at = 2 + 2 * chunk

    def side(i, s):
        return (1 - i) ^ (s[at] // 8)

    act = spec((1, rows, wide // 2), lambda i, s: (0, 0, side(i, s)))
    grad = spec((1, rows, wide), lambda i, s: (1, 0, 0))
    feature = spec((width // 2, rows), lambda i, s: (side(i, s), 0))
    in_specs = [act, act, grad, grad, whole(cot), whole(cot), feature, feature]
    if proj:
        half = width // 2
        column = spec((rows, half), lambda i, s: (0, side(i, s)))
        in_specs += [spec((rows, half), lambda i, s: (0, s[0])), whole(proj[1]), column, column]
    deep = 96 if proj else 64
    piece = spec((8, deep, width), lambda i, s: (0, 0, 0))
    return call(
        functools.partial(ff_grads_kernel, at),
        (2,),
        in_specs,
        [piece, piece],
        [shape((8, deep, width), bf16)] * 2,
        (mine, theirs, mine, theirs, cot, cot_other, normed_t, normed_t_other) + proj,
        scalars,
        32,
    )


def attn_back_kernel(s, q, g, k_o, k_f, v_o, v_f, *refs):
    gk_in, gv_in = refs[:2] if len(refs) == 5 else (None, None)
    gq, gk, gv = refs[-3:]
    k = jnp.concatenate([k_o[...], k_f[...]], 0)
    v = jnp.concatenate([v_o[...], v_f[...]], 0)
    kt = (k.astype(f32) * HD**-0.5).astype(bf16).T
    grad_q = []
    grad_k, grad_v = (gk_in[...], gv_in[...]) if gk_in is not None else (0.0, 0.0)
    q_heads = head_masks(q[...].astype(f32) * HD**-0.5)
    g_heads = head_masks(g[...].astype(f32))
    for h, (qh, gh) in enumerate(zip(q_heads, g_heads)):
        scores = dot(k, qh, NT)
        e = jnp.exp(scores - jnp.max(scores, 0, keepdims=True))
        probs = e * (1.0 / jnp.sum(e, 0, keepdims=True))
        grad_v = grad_v + dot(probs.astype(bf16), gh)
        grad_p = dot(v, gh, NT)
        row = jnp.sum(probs * grad_p, 0, keepdims=True)
        grad_s = (probs * (grad_p - row)).astype(bf16)
        grad_k = grad_k + dot(grad_s, qh)
        grad_q.append(dot(kt[h * HD : (h + 1) * HD], grad_s))
    gq[...] = jnp.concatenate(grad_q, 0).T.astype(bf16)
    gk[...] = grad_k.astype(gk.dtype)
    gv[...] = grad_v.astype(gv.dtype)


def attention_back(scalars, far, qkv, qkv_far, grad, *so_far):
    rows, width = qkv.shape[0], qkv.shape[1] // 3
    pairs = width // PAIR
    mine = pairs // 2

    def column(part):
        return spec((rows, PAIR), lambda i, s: (0, part * pairs + mine * s[1] + i))

    block = spec((rows, PAIR), lambda i, s: (0, i))
    both = spec((2 * rows, PAIR), lambda i, s: (0, i))
    dtype = bf16 if so_far else f32
    return call(
        attn_back_kernel,
        (mine,),
        [column(0), block, column(1), column(1), column(2), column(2)] + [both] * len(so_far),
        [block, both, both],
        [shape((rows, width // 2), bf16)] + [shape((2 * rows, width // 2), dtype)] * 2,
        (qkv_far if far else qkv, grad, qkv, qkv_far, qkv, qkv_far) + so_far,
        scalars,
        48,
    )


def joint_kernel(s, n_own, n_far, gq_o, gq_f, gk, gv, keep, send):
    step = pl.program_id(0)
    gq = jnp.concatenate([gq_o[...], gq_f[...]], 0)
    n = jnp.concatenate([n_own[...], n_far[...]], 0)
    cols = gk.shape[1]

    def fill(target, code):
        tiles = [dot(n, g, TN).astype(bf16) for g in (gq, gk[...], gv[...])]
        rows = tiles[0].shape[0] // 8
        for block in range(8):
            at = block ^ code
            for i, tile in enumerate(tiles):
                part = tile[block * rows : (block + 1) * rows]
                target[at, :, i * cols : i * cols + part.shape[1]] = part

    @pl.when(step == 0)
    def _():
        fill(send, s[9])

    @pl.when(step == 1)
    def _():
        fill(keep, s[8])


def joint_grads(scalars, n_own, n_far, gq, gq_far, gk, gv):
    rows, width = n_own.shape
    half = width // 2
    feature = spec((rows, half), lambda i, s: (0, s[0] ^ (1 - i)))
    cols = 3 * half
    piece = spec((8, half // 8, cols), lambda i, s: (0, 0, 0))
    return call(
        joint_kernel,
        (2,),
        [feature, feature, whole(gq), whole(gq), whole(gk), whole(gv)],
        [piece, piece],
        [shape((8, half // 8, cols), bf16)] * 2,
        (n_own, n_far, gq, gq_far, gk, gv),
        scalars,
        32,
    )


def back_qkv_kernel(s, gq_o, gq_f, gk, gv, wq, wk, wv, own, far):
    rows = own.shape[0]

    def part(gq, at):
        total = dot(gq[...], wq[...], NT)
        total += dot(gk[pl.ds(at, rows)], wk[...], NT)
        return total + dot(gv[pl.ds(at, rows)], wv[...], NT)

    far[...] = part(gq_f, rows).astype(bf16)
    own[...] = part(gq_o, 0)


def back_qkv(scalars, gq, gq_far, gk, gv, w):
    rows, half = gq.shape
    width = 2 * half

    def column(part):
        return spec((width, half), lambda i, s: (0, 2 * part + s[1]))

    full = spec((rows, width), lambda i, s: (0, 0))
    return call(
        back_qkv_kernel,
        (1,),
        [whole(gq), whole(gq), whole(gk), whole(gv), column(0), column(1), column(2)],
        [full, full],
        [shape((rows, width), f32), shape((rows, width), bf16)],
        (gq, gq_far, gk, gv, w, w, w),
        scalars,
        32,
    )


def last_kernel(s, own, far, tok, pos, gain, grad2, out):
    xhat, scale = normalize(tok[...].astype(f32) + pos[...])
    grad = own[...] + far[...].astype(f32)
    out[...] = grad2[...] + norm_backward(grad, gain[...], xhat, scale)


def token_grad(scalars, own, far, tok, pos, gain, grad2):
    args = (own, far, tok, pos, gain, grad2)
    return call(
        last_kernel,
        (1,),
        [whole(a) for a in args],
        whole(own),
        shape(own.shape, f32),
        args,
        scalars,
        24,
    )


def lane_sums(values):
    return sum(values[:, at : at + 128] for at in range(0, values.shape[1], 128))


def unpack_ff_kernel(at, last, s, own, other, w, gain_in, *refs):
    gain, down, up, *proj = refs[-4:] if last else refs[-3:]
    step = pl.program_id(0)

    def unpack(source, code):
        for block in range(8):
            to = block ^ (code & 7)
            down[pl.ds(pl.multiple_of(to * 32, 32), 32), :] = source[block, :32, :].astype(f32)
            row = pl.multiple_of(to * 48, 16)
            up[pl.ds(row, 32), :] = source[block, 32:64, :512].astype(f32)
            up[pl.ds(row + 32, 16), :256] = source[block, 32:48, 512:].astype(f32)
            up[pl.ds(row + 32, 16), 256:] = source[block, 48:64, 512:].astype(f32)
            if last:
                wide = source.shape[2] // 2
                proj[0][pl.ds(row, 16), :] = source[block, 64:80, :wide].astype(f32)
                proj[0][pl.ds(row + 16, 16), :] = source[block, 64:80, wide:].astype(f32)
                proj[0][pl.ds(row + 32, 16), :] = source[block, 80:, :wide].astype(f32)

    @pl.when(step == 0)
    def _():
        unpack(own, s[at])

    @pl.when(step == 1)
    def _():
        unpack(other, s[at + 1])

    sums = lane_sums(up[...] * w[...].astype(f32))
    gain[...] = gain_in[...] + sums


def unpack_ff(scalars, chunk, far, own, other, w, so_far):
    width, hidden = w.shape
    at = 2 + 2 * chunk
    last = own.shape[1] > 64

    def side(i, s):
        return (s[at + i] // 8) ^ far

    def half(i, s):
        return 2 * chunk + (s[0] ^ i)

    any_spec = pl.BlockSpec(memory_space=pl.ANY)
    column = spec((width // 2, 512), lambda i, s: (side(i, s), half(i, s)))
    gain = spec((None, width // 2, 128), lambda i, s: (i, side(i, s), 0))
    out_specs = [gain, spec((256, width), lambda i, s: (2 * half(i, s) + side(i, s), 0)), column]
    out_shape = [shape((2, width, 128), f32), shape((hidden, width), f32), shape((width, hidden), f32)]
    if last:
        out_specs.append(spec((width // 2, width // 2), lambda i, s: (s[0] ^ i, side(i, s))))
        out_shape.append(shape((width, width), f32))
    in_specs = [whole(own), whole(other), column]
    in_specs += [gain, any_spec, any_spec, any_spec][: len(so_far)]
    return call(
        functools.partial(unpack_ff_kernel, at, last),
        (2,),
        in_specs,
        out_specs,
        out_shape,
        (own, other, w) + tuple(so_far),
        scalars,
        32,
        aliases={4 + i: i for i in range(len(so_far))},
    )


def unpack_qkv_kernel(s, own, other, w, *refs):
    joint, gain = refs[-2:]
    step = pl.program_id(0)
    mine = s[1]

    def unpack(source, code):
        half = source.shape[2] // 6
        for block in range(4):
            rows = pl.ds(pl.multiple_of((block ^ (code & 3)) * 48, 16), 48)
            for part in range(3):
                for side in range(2):
                    column = pl.multiple_of(2 * half * part + half * (mine ^ side), 128)
                    value = source[block, :, (3 * side + part) * half : (3 * side + part + 1) * half]
                    joint[rows, pl.ds(column, half)] = value.astype(f32)

    @pl.when(step == 0)
    def _():
        unpack(own, s[8])

    @pl.when(step == 1)
    def _():
        unpack(other, s[9])

    gain[...] = lane_sums(joint[...] * w[...].astype(f32))


def unpack_qkv(scalars, far, own, other, w, so_far):
    width = w.shape[0]

    def rows(columns):
        return spec((width // 4, columns), lambda i, s: (2 * (s[0] ^ i) + ((s[8 + i] // 4) ^ far), 0))

    any_spec = pl.BlockSpec(memory_space=pl.ANY)
    return call(
        unpack_qkv_kernel,
        (2,),
        [whole(own), whole(other), rows(3 * width)] + [any_spec] * len(so_far),
        [rows(3 * width), rows(128)],
        [shape((width, 3 * width), f32), shape((width, 128), f32)],
        (own, other, w) + tuple(so_far),
        scalars,
        32,
        aliases={4 + i: i for i in range(len(so_far))},
    )


def fast(tokens, visible, ln1_gain, w_qkv, w_proj, ln2_gain, w_up, w_down, d_out):
    tok, cot = tokens[0], d_out[0]
    rows, width = tok.shape
    gain1, gain2 = ln1_gain[None], ln2_gain[None]
    scalars = [lax.axis_index("dp") & 1, lax.axis_index("blk")]
    for orders in FF_ORDERS + (QKV_ORDER,):
        scalars.extend(places(orders))
    scalars = jnp.stack([jnp.int32(v) for v in scalars])

    order = Order()
    run = order.run
    vis_far = swap(visible, "y")[0]
    tok_far = swap(tok, "y")
    cot_other = swap(cot, "c")
    pos = position_table(visible[0], width)
    pos_far = position_table(vis_far, width)
    normed1, qkv = run(functools.partial(ln_qkv, scalars), tok, pos, gain1, w_qkv)
    normed1_far, qkv_far = run(functools.partial(ln_qkv, scalars), tok_far, pos_far, gain1, w_qkv)
    attended = run(functools.partial(attention, scalars), qkv, qkv_far)
    resid2, normed2, normed2_t, att_half = run(
        functools.partial(project, scalars), attended, w_proj, tok, pos, gain2
    )
    early = cot_other, order.swap(normed2_t, "c"), order.swap(att_half, "c")

    streams, blocks, values = {}, {}, {"early": early}
    ff, proj, joint = (jnp.zeros((2, width, 128), f32),), (), ()

    def feed_forward(chunk):
        more = values.pop("sums", ())
        if chunk == 2:
            more += (resid2, gain2, w_proj, w_proj)
        keep, send, *rest = run(
            functools.partial(ff_chunk, scalars, chunk, chunk == 2), normed2, cot, w_up, w_down, *more
        )
        values["act", chunk], values["e%d" % chunk] = keep, order.swap(send, "c")
        if chunk == 2:
            out, grad2, branch, g_own, g_other = rest
            values["branch"], values["branch_other"] = branch, order.swap(branch, "c")
            values["g"] = order.swap(g_other, "y")
            values.update(out=out, grad2=grad2, own=g_own)
        else:
            values["sums"] = tuple(rest)

    def weight_grads(chunk):
        early = (*values["early"][:2], normed2_t)
        more = ()
        if chunk == 2:
            more = (attended, values["early"][2], values["branch"], values["branch_other"])
        keep, send = run(
            functools.partial(ff_grads, scalars, chunk),
            values["act", chunk], values["e%d" % chunk], cot, *early, *more,
        )
        streams[chunk] = total(order, keep, send, list(zip(*FF_ORDERS[chunk])))
        advance(chunk)

    def advance(chunk):
        pair = next(streams[chunk])
        if pair is not None:
            blocks.setdefault(chunk, []).append(pair)

    def wait(key):
        value = values[key]
        values[key] = run(lambda *v: v if isinstance(value, tuple) else v[0], *(value if isinstance(value, tuple) else (value,)))

    def own_queries():
        values["attn"] = run(functools.partial(attention_back, scalars, False), qkv, qkv_far, values["own"])

    def far_queries():
        gq, *sums = values["attn"]
        back = run(functools.partial(attention_back, scalars, True), qkv, qkv_far, values["g"], *sums)
        values["attn"] = (gq, *back)

    def joint_weights():
        keep, send = run(functools.partial(joint_grads, scalars), normed1, normed1_far, *values["attn"])
        links = [("c", "c")] + list(zip(*QKV_ORDER))
        streams[3] = total(order, keep, send, links, lambda a, b: jnp.concatenate([a, b], -1))
        advance(3)

    def back_joint():
        own, far = run(functools.partial(back_qkv, scalars), *values["attn"], w_qkv)
        values["norm"], values["bf"] = own, order.swap(far, "y")

    def finish_tokens():
        args = (values["norm"], values["bf"], tok, pos, gain1, values["grad2"])
        values["tokens"] = run(functools.partial(token_grad, scalars), *args)

    def unpack(chunk, far):
        nonlocal ff, proj, joint
        own, other = blocks[chunk][far]
        if chunk == 3:
            joint = run(lambda a, b, *f: unpack_qkv(scalars, far, a, b, w_qkv, f), own, other, *joint)
            return
        so_far = ff + proj if chunk == 2 else ff
        result = tuple(
            run(lambda a, b, *f: unpack_ff(scalars, chunk, far, a, b, w_up, f), own, other, *so_far)
        )
        ff, proj = result[:3], result[3:] or proj

    steps = {
        "ff": feed_forward,
        "dw": weight_grads,
        "go": advance,
        "wait": wait,
        "own": own_queries,
        "far": far_queries,
        "joint": joint_weights,
        "back": back_joint,
        "tokens": finish_tokens,
        "unpack": unpack,
    }
    for name, *args in PLAN:
        steps[name](*args)
    sums2, d_down, d_up = ff
    d_qkv, sums1 = joint
    out, d_tokens, d_proj = values["out"], values["tokens"], proj[0]
    d_gain1 = jnp.sum(sums1, 1) / ln1_gain
    d_gain2 = jnp.sum(sums2, (0, 2)) / ln2_gain
    return out[None], d_tokens[None], d_gain1, d_qkv, d_proj, d_gain2, d_up, d_down


def layer_norm(values, gain):
    center = values - jnp.mean(values, -1, keepdims=True)
    spread = jnp.mean(center * center, -1, keepdims=True)
    return center * lax.rsqrt(spread + epsilon) * gain


def outer_product(left, right):
    return lax.dot_general(
        left, right, (((0,), (0,)), ((), ())), preferred_element_type=jnp.float32
    )


def times_transposed(left, weight):
    return lax.dot_general(
        left, weight, (((1,), (1,)), ((), ())), preferred_element_type=jnp.float32
    )


def split_blocks(keys, values):
    count = keys.shape[0]
    size = math.gcd(count, 512)
    shape = (count // size, size, HEADS, HD)
    return (keys.reshape(shape), values.reshape(shape))


def general(tokens, visible, ln1_gain, w_qkv, w_proj, ln2_gain, w_up, w_down, d_out):
    rows = tokens.shape[1]
    width = tokens.shape[2]
    factor = HD ** (-0.5)
    resid = tokens[0].astype(jnp.float32) + position_table(visible[0], width)
    normed1, back_one = jax.vjp(layer_norm, resid, ln1_gain)
    normed1 = normed1.astype(jnp.bfloat16)
    qkv = jnp.dot(normed1, w_qkv, preferred_element_type=jnp.float32).astype(jnp.bfloat16)
    query = qkv[:, :width]
    keys = qkv[:, width : 2 * width]
    values = qkv[:, 2 * width :]
    query_heads = query.reshape(rows, HEADS, HD)
    initial = (
        jnp.full((HEADS, rows), -1e30, jnp.float32),
        jnp.zeros((HEADS, rows), jnp.float32),
        jnp.zeros((HEADS, rows, HD), jnp.float32),
    )
    key_blocks, value_blocks = split_blocks(
        lax.all_gather(keys, "blk", axis=0, tiled=True),
        lax.all_gather(values, "blk", axis=0, tiled=True),
    )

    def one_block(state, block):
        running, total, accum = state
        block_keys, block_values = block
        scores = (
            jnp.einsum("qhd,khd->hqk", query_heads, block_keys, preferred_element_type=jnp.float32)
            * factor
        )
        top = jnp.maximum(running, jnp.max(scores, -1))
        weights = jnp.exp(scores - top[..., None])
        shrink = jnp.exp(running - top)
        total = total * shrink + jnp.sum(weights, -1)
        accum = accum * shrink[..., None] + jnp.einsum(
            "hqk,khd->hqd",
            weights.astype(jnp.bfloat16),
            block_values,
            preferred_element_type=jnp.float32,
        )
        return ((top, total, accum), None)

    running, total, accum = lax.scan(one_block, initial, (key_blocks, value_blocks))[0]
    log_total = running + jnp.log(total)
    attended = (accum / total[..., None]).transpose(1, 0, 2).reshape(rows, width)
    attended_low = attended.astype(jnp.bfloat16)
    resid2 = resid + jnp.dot(attended_low, w_proj, preferred_element_type=jnp.float32)
    normed2, back_two = jax.vjp(layer_norm, resid2, ln2_gain)
    normed2 = normed2.astype(jnp.bfloat16)
    hidden = jnp.dot(normed2, w_up, preferred_element_type=jnp.float32)
    activated, back_gelu = jax.vjp(jax.nn.gelu, hidden)
    activated = activated.astype(jnp.bfloat16)
    result = resid2 + jnp.dot(activated, w_down, preferred_element_type=jnp.float32)
    cotangent = d_out[0]
    grad_down = outer_product(activated, cotangent)
    (grad_hidden,) = back_gelu(times_transposed(cotangent, w_down))
    grad_hidden = grad_hidden.astype(jnp.bfloat16)
    grad_up = outer_product(normed2, grad_hidden)
    grad_resid2, grad_gain2 = back_two(times_transposed(grad_hidden, w_up))
    grad_resid2 = grad_resid2 + cotangent.astype(jnp.float32)
    grad_branch = grad_resid2.astype(jnp.bfloat16)
    grad_proj = outer_product(attended_low, grad_branch)
    grad_attended = times_transposed(grad_branch, w_proj).astype(jnp.bfloat16)
    correction = (grad_attended.astype(jnp.float32) * attended).reshape(rows, HEADS, HD)
    correction = jnp.sum(correction, -1).T
    grad_heads = grad_attended.reshape(rows, HEADS, HD)
    all_keys, all_values = (
        lax.all_gather(keys, "blk", axis=0, tiled=True),
        lax.all_gather(values, "blk", axis=0, tiled=True),
    )
    full_rows = all_keys.shape[0]
    key_blocks, value_blocks = split_blocks(all_keys, all_values)

    def back_block(grad_query, block):
        block_keys, block_values = block
        scores = (
            jnp.einsum("qhd,khd->hqk", query_heads, block_keys, preferred_element_type=jnp.float32)
            * factor
        )
        probs = jnp.exp(scores - log_total[..., None])
        grad_value = jnp.einsum(
            "hqk,qhd->khd",
            probs.astype(jnp.bfloat16),
            grad_heads,
            preferred_element_type=jnp.float32,
        )
        grad_probs = jnp.einsum(
            "qhd,khd->hqk", grad_heads, block_values, preferred_element_type=jnp.float32
        )
        grad_scores = (probs * (grad_probs - correction[..., None])).astype(jnp.bfloat16)
        grad_query = grad_query + jnp.einsum(
            "hqk,khd->qhd", grad_scores, block_keys, preferred_element_type=jnp.float32
        )
        grad_key = (
            jnp.einsum("hqk,qhd->khd", grad_scores, query_heads, preferred_element_type=jnp.float32)
            * factor
        )
        return (grad_query, (grad_key, grad_value))

    grad_query, (key_parts, value_parts) = lax.scan(
        back_block, jnp.zeros((rows, HEADS, HD), jnp.float32), (key_blocks, value_blocks)
    )
    grad_query = (grad_query * factor).reshape(rows, width)
    grad_keys, grad_values = (
        lax.psum_scatter(
            key_parts.reshape(full_rows, width).astype(jnp.bfloat16),
            "blk",
            scatter_dimension=0,
            tiled=True,
        ).astype(jnp.float32),
        lax.psum_scatter(
            value_parts.reshape(full_rows, width).astype(jnp.bfloat16),
            "blk",
            scatter_dimension=0,
            tiled=True,
        ).astype(jnp.float32),
    )
    grad_qkv = jnp.concatenate([grad_query, grad_keys, grad_values], 1).astype(jnp.bfloat16)
    grad_joint = outer_product(normed1, grad_qkv)
    grad_resid, grad_gain1 = back_one(times_transposed(grad_qkv, w_qkv))
    input_grad = grad_resid2 + grad_resid
    flats = (
        grad_joint.reshape(-1),
        grad_proj.reshape(-1),
        grad_up.reshape(-1),
        grad_down.reshape(-1),
    )
    shares = (
        lax.psum_scatter(flats[0], ("dp", "blk"), scatter_dimension=0, tiled=True),
        lax.psum_scatter(flats[1], ("dp", "blk"), scatter_dimension=0, tiled=True),
        lax.psum_scatter(flats[2], ("dp", "blk"), scatter_dimension=0, tiled=True),
        lax.psum_scatter(flats[3], ("dp", "blk"), scatter_dimension=0, tiled=True),
    )
    summed = (
        lax.all_gather(shares[0].astype(jnp.bfloat16), ("dp", "blk"), axis=0, tiled=True).astype(
            jnp.float32
        ),
        lax.all_gather(shares[1].astype(jnp.bfloat16), ("dp", "blk"), axis=0, tiled=True).astype(
            jnp.float32
        ),
        lax.all_gather(shares[2].astype(jnp.bfloat16), ("dp", "blk"), axis=0, tiled=True).astype(
            jnp.float32
        ),
        lax.all_gather(shares[3].astype(jnp.bfloat16), ("dp", "blk"), axis=0, tiled=True).astype(
            jnp.float32
        ),
    )
    gain_one, gain_two = lax.psum((grad_gain1, grad_gain2), ("dp", "blk"))
    return (
        result.astype(jnp.bfloat16)[None],
        input_grad[None],
        gain_one,
        summed[0].reshape(w_qkv.shape),
        summed[1].reshape(w_proj.shape),
        gain_two,
        summed[2].reshape(w_up.shape),
        summed[3].reshape(w_down.shape),
    )


def solution(mesh):
    split = mesh.shape["dp"] == 16 and mesh.shape["blk"] == 2
    return jax.shard_map(
        fast if split else general,
        mesh=mesh,
        in_specs=(
            P("dp", "blk", None),
            P("dp", "blk"),
            P(),
            P(),
            P(),
            P(),
            P(),
            P(),
            P("dp", "blk", None),
        ),
        out_specs=(P("dp", "blk", None), P("dp", "blk", None), P(), P(), P(), P(), P(), P()),
        check_vma=False,
    )
```

```python
import functools
import math

import jax
import jax.numpy as jnp
from jax import lax
from jax.experimental import pallas as pl
from jax.experimental.pallas import tpu as pltpu
from jax.sharding import PartitionSpec as P

HEADS = 12
HD = 64
PAIR = 2 * HD
epsilon = 1e-06
f32 = jnp.float32
bf16 = jnp.bfloat16
NN = ((1,), (0,))
NT = ((1,), (1,))
TN = ((0,), (0,))
AXES = ("dp", "blk")
MIB = 1 << 20


def dot(left, right, dims=NN):
    return lax.dot_general(left, right, (dims, ((), ())), preferred_element_type=f32)


def position_table(visible, width):
    half = width // 2
    column = jnp.arange(half, dtype=f32)
    freqs = jnp.exp(column * (-math.log(10000.0) / half))
    angles = visible.astype(f32)[..., None] * freqs
    return jnp.concatenate([jnp.sin(angles), jnp.cos(angles)], -1)


def normalize(values):
    center = values - jnp.mean(values, -1, keepdims=True)
    spread = jnp.mean(center * center, -1, keepdims=True)
    scale = lax.rsqrt(spread + epsilon)
    return center * scale, scale


def norm_backward(grad, gain, xhat, scale):
    e = grad * gain
    return scale * (
        e - jnp.mean(e, -1, keepdims=True) - xhat * jnp.mean(e * xhat, -1, keepdims=True)
    )


def call(kernel, grid, in_specs, out_specs, out_shape, args, scalars, vmem, scratch=(), aliases=None):
    return pl.pallas_call(
        kernel,
        grid_spec=pltpu.PrefetchScalarGridSpec(
            num_scalar_prefetch=1,
            grid=grid,
            in_specs=in_specs,
            out_specs=out_specs,
            scratch_shapes=list(scratch),
        ),
        out_shape=out_shape,
        input_output_aliases=aliases or {},
        compiler_params=pltpu.CompilerParams(vmem_limit_bytes=max(vmem, 28) * MIB),
        cost_estimate=pl.CostEstimate(flops=1, bytes_accessed=1, transcendentals=0),
    )(scalars, *args)


def spec(shape, index):
    return pl.BlockSpec(shape, index)


def whole(array):
    zeros = (0,) * array.ndim
    return pl.BlockSpec(array.shape, lambda i, s: zeros)


def shape(dims, dtype):
    return jax.ShapeDtypeStruct(dims, dtype)


FF_ORDERS = (
    (("x", "y", "z0", "z1"), ("y", "z0", "x", "z1")),
    (("z0", "y", "x", "z1"), ("x", "y", "z1", "z0")),
    (("y", "z0", "x", "z1"), ("x", "y", "z0", "z1")),
)
QKV_ORDER = (("x", "z0", "z1"), ("z0", "z1", "x"))
PLAN = (
    ("ff", 0), ("ff", 1), ("wait", "early"), ("wait", "e0"), ("dw", 0), ("wait", "e2"),
    ("wait", "e1"), ("wait", "branch_other"), ("own",), ("wait", "g"), ("dw", 2), ("dw", 1),
    ("go", 0), ("far",), ("go", 2), ("joint",), ("go", 0), ("go", 1), ("go", 2), ("go", 0),
    ("go", 3), ("back",), ("go", 2), ("go", 3), ("go", 1), ("go", 0), ("go", 2), ("go", 0),
    ("go", 3), ("go", 2), ("wait", "bf"), ("go", 1), ("go", 3), ("go", 0), ("go", 3), ("go", 2),
    ("tokens",), ("go", 1), ("wait", "n0"), ("go", 0), ("unpack", 0, 0), ("go", 3), ("go", 1),
    ("wait", "f0"), ("unpack", 0, 1), ("go", 2), ("wait", "n2"), ("unpack", 2, 0), ("go", 1),
    ("go", 3), ("wait", "f2"), ("wait", "n3"), ("unpack", 2, 1), ("wait", "f3"), ("unpack", 3, 0),
    ("unpack", 3, 1), ("wait", "n1"), ("go", 1), ("unpack", 1, 0), ("wait", "f1"), ("unpack", 1, 1),
)
DP_BIT = {"c": 1, "x": 2, "z0": 4, "z1": 8}


def swap(array, first, second=None):
    second = second or first
    pairs = []
    for d in range(16):
        for b in range(2):
            bit = second if d & 1 else first
            to = (d, b ^ 1) if bit == "y" else (d ^ DP_BIT[bit], b)
            pairs.append((d * 2 + b, to[0] * 2 + to[1]))
    return lax.ppermute(array, AXES, pairs)


def place(order):
    d, b = lax.axis_index("dp"), lax.axis_index("blk")
    code = jnp.int32(0)
    for bit in order:
        value = b & 1 if bit == "y" else (d // DP_BIT[bit]) & 1
        code = code * 2 + value
    return code


def places(orders):
    core = lax.axis_index("dp") & 1
    first, second = place(orders[0]), place(orders[1])
    return jnp.where(core == 0, first, second), jnp.where(core == 0, second, first)


def add(a, b):
    return (a.astype(f32) + b.astype(f32)).astype(bf16)


class Order:
    def __init__(self):
        self.last = None

    def pin(self, *arrays):
        if self.last is None:
            return arrays
        return lax.optimization_barrier((*arrays, self.last))[:-1]

    def run(self, function, *arrays):
        result = function(*self.pin(*arrays))
        self.last = result[0] if isinstance(result, (tuple, list)) else result
        return result

    def swap(self, array, first, second=None):
        return swap(self.pin(array)[0], first, second)


def total(order, keep, send, links, widen=None):
    received = order.swap(send, *links[0])
    yield
    for link in links[1:-1]:
        half = keep.shape[0] // 2
        send = order.run(lambda k, r: add(k[half:], r[half:]), keep, received)
        coming = order.swap(send, *link)
        keep = order.run(lambda k, r: add(k[:half], r[:half]), keep, received)
        received = coming
        yield
    keep = order.run(add, keep, received)
    received = order.swap(keep, *links[-1])
    yield
    block = order.run(lambda k, r: add(k, r[::-1]), keep, received)
    if widen is not None:
        received = order.swap(block, "y")
        yield
        block = order.run(widen, block, received)
    back = [link for link in links[:-1] if link[0] != "c"][::-1]
    for link in back[:-1]:
        received = order.swap(block, *link)
        yield
        block = order.run(lambda k, r: jnp.concatenate([k, r], 0), block, received)
    far = order.swap(block, *back[-1])
    other = order.swap(block, "c")
    yield block, other
    far = order.run(lambda value: value, far)
    yield far, order.swap(far, "c")


def sine_and_cosine(angle):
    turns = jnp.floor(angle * (2.0 / math.pi) + 0.5)
    rest = angle - turns * 1.5703125
    rest = rest - turns * 4.837512969970703125e-4
    rest = rest - turns * 7.54978995489188e-8
    square = rest * rest
    sine = rest + rest * square * (
        -1.6666654611e-1 + square * (8.3321608736e-3 + square * -1.9515295891e-4)
    )
    cosine = (1.0 - 0.5 * square) + square * square * (
        4.166664568298827e-2 + square * (-1.388731625493765e-3 + square * 2.443315711809948e-5)
    )
    quarter = turns.astype(jnp.int32)
    odd = (quarter & 1) == 1
    sin = jnp.where(odd, cosine, sine)
    cos = jnp.where(odd, sine, cosine)
    return (
        jnp.where((quarter & 2) == 2, -sin, sin),
        jnp.where(((quarter + 1) & 2) == 2, -cos, cos),
    )


def position_kernel(s, visible, freqs, out):
    column = jnp.broadcast_to(visible[...].astype(f32), (8, visible.shape[1])).T[:, :1]
    sin, cos = sine_and_cosine(column * freqs[...])
    half = sin.shape[1]
    out[:, :half] = sin
    out[:, half:] = cos


def positions(scalars, visible, freqs):
    rows, width = visible.shape[1], 2 * freqs.shape[1]
    out = shape((rows, width), f32)
    return call(
        position_kernel, (1,), [whole(visible), whole(freqs)], whole(out), out, (visible, freqs), scalars, 16
    )


def ln_qkv_kernel(s, tok, pos, gain, w, normed, qkv, *resid):
    @pl.when(pl.program_id(0) == 0)
    def _():
        value = tok[...].astype(f32) + pos[...]
        if resid:
            resid[0][...] = value
        xhat, _ = normalize(value)
        normed[...] = (xhat * gain[...]).astype(bf16)

    qkv[...] = dot(normed[...], w[...]).astype(bf16)


def ln_qkv(scalars, far, tok, pos, gain, w):
    rows, width = tok.shape
    full = spec((rows, width), lambda i, s: (0, 0))
    parts = 2 if far else 3
    out_shape = [shape((rows, width), bf16), shape((rows, parts * width), bf16)]
    return call(
        ln_qkv_kernel,
        (parts,),
        [full, full, whole(gain), spec((width, width), lambda i, s: (0, i + far))],
        [full, spec((rows, width), lambda i, s: (0, i))] + [full] * (not far),
        out_shape + [shape((rows, width), f32)] * (not far),
        (tok, pos, gain, w),
        scalars,
        24,
    )


def far_query_kernel(s, normed, w, out):
    out[...] = dot(normed[...], w[...]).astype(bf16)


def far_query(scalars, normed, w):
    rows, width = normed.shape
    out = shape((rows, width // 2), bf16)
    return call(
        far_query_kernel,
        (1,),
        [whole(normed), spec((width, width // 2), lambda i, s: (0, s[1]))],
        whole(out),
        out,
        (normed, w),
        scalars,
        16,
    )


def head_masks(x):
    lane = lax.broadcasted_iota(jnp.int32, x.shape, 1)
    return jnp.where(lane < HD, x, 0.0).astype(bf16), jnp.where(lane >= HD, x, 0.0).astype(bf16)


def attn_kernel(s, q, k, v, *refs):
    rows = q.shape[0]
    qs = jnp.concatenate(head_masks(q[...].astype(f32) * HD**-0.5), 0)
    scores = dot(k[...], qs, NT)
    top = jnp.max(scores, 0, keepdims=True)
    later = len(refs) == 3
    if later:
        acc_in, stat_in, out = refs
        before = stat_in[0, 0:1]
        top = jnp.maximum(top, before)
    e = jnp.exp(scores - top)
    total = jnp.sum(e, 0, keepdims=True)
    vt = v[...].T
    low = e.astype(bf16)
    parts = [dot(vt[h * HD : (h + 1) * HD], low[:, h * rows : (h + 1) * rows]) for h in range(2)]
    if not later:
        acc, stat = refs
        acc[0] = jnp.concatenate(parts, 0)
        stat[0, 0:1] = top
        stat[0, 1:2] = total
        return
    shrink = jnp.exp(before - top)
    scale = 1.0 / (total + stat_in[0, 1:2] * shrink)
    shrink = shrink * scale
    for h in range(2):
        at = slice(h * rows, (h + 1) * rows)
        held = acc_in[0, h * HD : (h + 1) * HD]
        parts[h] = parts[h] * scale[:, at] + held * shrink[:, at]
    out[...] = jnp.concatenate(parts, 0).T.astype(bf16)


def attention(scalars, qkv, keys, *so_far):
    rows, width = qkv.shape[0], qkv.shape[1] // 3
    pairs = width // PAIR

    def column(part):
        return spec((rows, PAIR), lambda i, s: (0, part * pairs + i))

    first = 0 if so_far else 1
    acc = spec((1, PAIR, rows), lambda i, s: (i, 0, 0))
    stat = spec((1, 8, 2 * rows), lambda i, s: (i, 0, 0))
    sums = [shape((pairs, PAIR, rows), f32), shape((pairs, 8, 2 * rows), f32)]
    return call(
        attn_kernel,
        (pairs,),
        [column(0), column(first), column(first + 1)] + ([acc, stat] if so_far else []),
        spec((rows, PAIR), lambda i, s: (0, i)) if so_far else [acc, stat],
        shape((rows, width), bf16) if so_far else sums,
        (qkv, keys, keys) + so_far,
        scalars,
        28,
    )


def proj_kernel(s, att, att_half, w, resid, gain, resid2, normed2, normed2_t, att_send):
    att_send[...] = att_half[...]
    value = resid[...] + dot(att[...], w[...])
    resid2[...] = value
    xhat, _ = normalize(value)
    low = (xhat * gain[...]).astype(bf16)
    normed2[...] = low
    normed2_t[...] = low.T


def project(scalars, att, w, resid, gain):
    rows, width = att.shape
    full = spec((rows, width), lambda i, s: (0, 0))
    half = spec((rows, width // 2), lambda i, s: (0, 1 - s[0]))
    return call(
        proj_kernel,
        (1,),
        [full, half, whole(w), full, whole(gain)],
        [
            full,
            full,
            spec((width, rows), lambda i, s: (0, 0)),
            spec((rows, width // 2), lambda i, s: (0, 0)),
        ],
        [
            shape((rows, width), f32),
            shape((rows, width), bf16),
            shape((width, rows), bf16),
            shape((rows, width // 2), bf16),
        ],
        (att, att, w, resid, gain),
        scalars,
        24,
    )


def gelu_and_slope(v):
    c = math.sqrt(2.0 / math.pi)
    square = v * v
    t = jnp.tanh(v * (c + (c * 0.044715) * square))
    act = 0.5 * v * (1.0 + t)
    slope = 0.5 * (1.0 + t) + (0.5 * v) * (1.0 - t * t) * (c + (3.0 * c * 0.044715) * square)
    return act, slope


def ff_kernel(count, s, normed, cot, up, down, *refs):
    step = pl.program_id(0)
    if count > 1:
        out_in, back_in, resid2, gain, w_own, w_other, *refs = refs
    pieces, refs = refs[: 2 * count], refs[2 * count :]
    if count > 1:
        out_low, grad2, branch, g_own, g_other, out, back = refs
    else:
        out, back = refs
    hidden = dot(normed[...], up[...])
    act, slope = gelu_and_slope(hidden)
    act = act.astype(bf16)
    grad = (dot(cot[...], down[...], NT) * slope).astype(bf16)
    out_part = dot(act, down[...])
    back_part = dot(grad, up[...], NT)

    @pl.when(step == 0)
    def _():
        out[...] = out_in[...] + out_part if count > 1 else out_part
        back[...] = back_in[...] + back_part if count > 1 else back_part

    @pl.when(step > 0)
    def _():
        out[...] += out_part
        back[...] += back_part

    for at, piece in enumerate(pieces):

        @pl.when(step == at)
        def _(piece=piece):
            piece[0] = act
            piece[1] = grad

    if count > 1:

        @pl.when(step == 2 * count - 1)
        def _():
            value = resid2[...]
            out_low[...] = (value + out[...]).astype(bf16)
            xhat, scale = normalize(value)
            g = cot[...].astype(f32) + norm_backward(back[...], gain[...], xhat, scale)
            grad2[...] = g
            low = g.astype(bf16)
            branch[...] = low
            g_other[...] = dot(low, w_other[...], NT).astype(bf16)
            g_own[...] = dot(low, w_own[...], NT).astype(bf16)


def ff_chunks(scalars, first, count, normed, cot, up, down, *more):
    rows, width = normed.shape
    half = width // 2
    wide = 512

    def column(i, s):
        return 2 * (first + i // 2) + (s[0] ^ (1 - (i & 1)))

    full = spec((rows, width), lambda i, s: (0, 0))
    part = spec((rows, half), lambda i, s: (0, 0))
    in_specs = [
        whole(normed),
        whole(cot),
        spec((width, wide), lambda i, s: (0, column(i, s))),
        spec((wide, width), lambda i, s: (column(i, s), 0)),
    ]
    out_specs = [spec((2, rows, wide), lambda i, s: (0, 0, 0))] * (2 * count)
    out_shape = [shape((2, rows, wide), bf16)] * (2 * count)
    scratch = []
    if count > 1:
        in_specs += [
            full,
            full,
            full,
            spec((1, width), lambda i, s: (0, 0)),
            spec((half, width), lambda i, s: (s[1], 0)),
            spec((half, width), lambda i, s: (1 - s[1], 0)),
        ]
        out_specs += [full, full, full, part, part]
        out_shape += [shape((rows, width), t) for t in (bf16, f32, bf16)]
        out_shape += [shape((rows, half), bf16)] * 2
        scratch = [pltpu.VMEM((rows, width), f32)] * 2
    else:
        out_specs += [full, full]
        out_shape += [shape((rows, width), f32)] * 2
    return call(
        functools.partial(ff_kernel, count),
        (2 * count,),
        in_specs,
        out_specs,
        out_shape,
        (normed, cot, up, down) + more,
        scalars,
        28,
        scratch,
    )


def ff_grads_kernel(at, s, act, act_o, grad, grad_o, cot, cot_o, nt, nt_o, *refs):
    keep, send = refs[-2:]
    step = pl.program_id(0)
    rows_both = jnp.concatenate([cot[...], cot_o[...]], 0)
    g_down = dot(jnp.concatenate([act[0], act_o[0]], 0), rows_both, TN).astype(bf16)
    grads = jnp.concatenate([grad[0], grad_o[0]], 0)
    g_up = dot(jnp.concatenate([nt[...], nt_o[...]], 1), grads).astype(bf16)
    g_proj = None
    if len(refs) > 2:
        att, att_o, branch, branch_o = refs[:4]
        both = jnp.concatenate([branch[...], branch_o[...]], 0)
        g_proj = dot(jnp.concatenate([att[...], att_o[...]], 0), both, TN).astype(bf16)
    code = s[at] & 7

    def store(target):
        rows_d = g_down.shape[0] // 8
        rows_u = g_up.shape[0] // 8
        half = g_up.shape[1] // 2
        for block in range(8):
            to = block ^ code
            target[to, :rows_d, :] = g_down[block * rows_d : (block + 1) * rows_d]
            part = g_up[block * rows_u : (block + 1) * rows_u]
            target[to, 32:64, : 2 * half] = part[:32]
            target[to, 32:48, 2 * half :] = part[32:, :half]
            target[to, 48:64, 2 * half :] = part[32:, half:]
            if g_proj is not None:
                part = g_proj[block * rows_u : (block + 1) * rows_u]
                wide = part.shape[1]
                target[to, 64:80, :wide] = part[:16]
                target[to, 64:80, wide:] = part[16:32]
                target[to, 80:, :wide] = part[32:]
                target[to, 80:, wide:] = jnp.zeros_like(part[32:])

    @pl.when(step == 0)
    def _():
        store(send)

    @pl.when(step == 1)
    def _():
        store(keep)


def ff_grads(scalars, chunk, mine, theirs, cot, cot_other, normed_t_other, normed_t, *proj):
    rows, width = cot.shape
    wide = mine.shape[2]
    at = 2 + 2 * chunk

    def side(i, s):
        return (1 - i) ^ (s[at] // 8)

    act = spec((1, rows, wide // 2), lambda i, s: (0, 0, side(i, s)))
    grad = spec((1, rows, wide), lambda i, s: (1, 0, 0))
    feature = spec((width // 2, rows), lambda i, s: (side(i, s), 0))
    in_specs = [act, act, grad, grad, whole(cot), whole(cot), feature, feature]
    if proj:
        half = width // 2
        column = spec((rows, half), lambda i, s: (0, side(i, s)))
        in_specs += [spec((rows, half), lambda i, s: (0, s[0])), whole(proj[1]), column, column]
    deep = 96 if proj else 64
    piece = spec((8, deep, width), lambda i, s: (0, 0, 0))
    return call(
        functools.partial(ff_grads_kernel, at),
        (2,),
        in_specs,
        [piece, piece],
        [shape((8, deep, width), bf16)] * 2,
        (mine, theirs, mine, theirs, cot, cot_other, normed_t, normed_t_other) + proj,
        scalars,
        28,
    )


def attn_back_kernel(s, q, g, k_o, k_f, v_o, v_f, *refs):
    gk_in, gv_in = refs[:2] if len(refs) == 5 else (None, None)
    gq, gk, gv = refs[-3:]
    k = jnp.concatenate([k_o[...], k_f[...]], 0)
    v = jnp.concatenate([v_o[...], v_f[...]], 0)
    kt = (k.astype(f32) * HD**-0.5).astype(bf16).T
    rows = q.shape[0]
    qs = jnp.concatenate(head_masks(q[...].astype(f32) * HD**-0.5), 0)
    gs = jnp.concatenate(head_masks(g[...].astype(f32)), 0)
    scores = dot(k, qs, NT)
    e = jnp.exp(scores - jnp.max(scores, 0, keepdims=True))
    probs = e * (1.0 / jnp.sum(e, 0, keepdims=True))
    grad_v = dot(probs.astype(bf16), gs)
    grad_p = dot(v, gs, NT)
    row = jnp.sum(probs * grad_p, 0, keepdims=True)
    grad_s = (probs * (grad_p - row)).astype(bf16)
    grad_k = dot(grad_s, qs)
    grad_q = [
        dot(kt[h * HD : (h + 1) * HD], grad_s[:, h * rows : (h + 1) * rows]) for h in range(2)
    ]
    if gk_in is not None:
        grad_k, grad_v = grad_k + gk_in[...], grad_v + gv_in[...]
    gq[...] = jnp.concatenate(grad_q, 0).T.astype(bf16)
    gk[...] = grad_k.astype(gk.dtype)
    gv[...] = grad_v.astype(gv.dtype)


def attention_back(scalars, query, grad, qkv, kv_far, *so_far):
    rows, width = qkv.shape[0], qkv.shape[1] // 3
    pairs = width // PAIR
    mine = pairs // 2

    def column(part):
        return spec((rows, PAIR), lambda i, s: (0, part * pairs + mine * s[1] + i))

    block = spec((rows, PAIR), lambda i, s: (0, i))
    both = spec((2 * rows, PAIR), lambda i, s: (0, i))
    dtype = bf16 if so_far else f32
    return call(
        attn_back_kernel,
        (mine,),
        [block if so_far else column(0), block, column(1), column(0), column(2), column(1)]
        + [both] * len(so_far),
        [block, both, both],
        [shape((rows, width // 2), bf16)] + [shape((2 * rows, width // 2), dtype)] * 2,
        (query, grad, qkv, kv_far, qkv, kv_far) + so_far,
        scalars,
        28,
    )


def joint_kernel(s, n_own, n_far, gq_o, gq_f, gk, gv, keep, send):
    step = pl.program_id(0)
    gq = jnp.concatenate([gq_o[...], gq_f[...]], 0)
    n = jnp.concatenate([n_own[...], n_far[...]], 0)
    cols = gk.shape[1]

    def fill(target, code):
        tiles = [dot(n, g, TN).astype(bf16) for g in (gq, gk[...], gv[...])]
        rows = tiles[0].shape[0] // 8
        for block in range(8):
            at = block ^ code
            for i, tile in enumerate(tiles):
                part = tile[block * rows : (block + 1) * rows]
                target[at, :, i * cols : i * cols + part.shape[1]] = part

    @pl.when(step == 0)
    def _():
        fill(send, s[9])

    @pl.when(step == 1)
    def _():
        fill(keep, s[8])


def joint_grads(scalars, n_own, n_far, gq, gq_far, gk, gv):
    rows, width = n_own.shape
    half = width // 2
    feature = spec((rows, half), lambda i, s: (0, s[0] ^ (1 - i)))
    cols = 3 * half
    piece = spec((8, half // 8, cols), lambda i, s: (0, 0, 0))
    return call(
        joint_kernel,
        (2,),
        [feature, feature, whole(gq), whole(gq), whole(gk), whole(gv)],
        [piece, piece],
        [shape((8, half // 8, cols), bf16)] * 2,
        (n_own, n_far, gq, gq_far, gk, gv),
        scalars,
        28,
    )


def back_qkv_kernel(s, gq_o, gq_f, gk, gv, wq, wk, wv, own, far):
    rows = own.shape[0]

    def part(gq, at):
        total = dot(gq[...], wq[...], NT)
        total += dot(gk[pl.ds(at, rows)], wk[...], NT)
        return total + dot(gv[pl.ds(at, rows)], wv[...], NT)

    far[...] = part(gq_f, rows).astype(bf16)
    own[...] = part(gq_o, 0)


def back_qkv(scalars, gq, gq_far, gk, gv, w):
    rows, half = gq.shape
    width = 2 * half

    def column(part):
        return spec((width, half), lambda i, s: (0, 2 * part + s[1]))

    full = spec((rows, width), lambda i, s: (0, 0))
    return call(
        back_qkv_kernel,
        (1,),
        [whole(gq), whole(gq), whole(gk), whole(gv), column(0), column(1), column(2)],
        [full, full],
        [shape((rows, width), f32), shape((rows, width), bf16)],
        (gq, gq_far, gk, gv, w, w, w),
        scalars,
        28,
    )


def last_kernel(s, own, far, resid, gain, grad2, out):
    xhat, scale = normalize(resid[...])
    grad = own[...] + far[...].astype(f32)
    out[...] = grad2[...] + norm_backward(grad, gain[...], xhat, scale)


def token_grad(scalars, own, far, resid, gain, grad2):
    args = (own, far, resid, gain, grad2)
    return call(
        last_kernel,
        (1,),
        [whole(a) for a in args],
        whole(own),
        shape(own.shape, f32),
        args,
        scalars,
        24,
    )


def row_sums(values):
    folded = sum(values[:, at : at + 128] for at in range(0, values.shape[1], 128))
    return lax.dot_general(
        jnp.ones((8, 128), f32),
        folded,
        (NT, ((), ())),
        precision=lax.Precision.HIGHEST,
        preferred_element_type=f32,
    )


def unpack_ff_kernel(at, last, s, own, other, w, gain_in, *refs):
    gain, down, up, *proj = refs[-4:] if last else refs[-3:]
    step = pl.program_id(0)

    def unpack(source, code):
        for block in range(8):
            to = block ^ (code & 7)
            down[pl.ds(pl.multiple_of(to * 32, 32), 32), :] = source[block, :32, :].astype(f32)
            row = pl.multiple_of(to * 48, 16)
            up[pl.ds(row, 32), :] = source[block, 32:64, :512].astype(f32)
            up[pl.ds(row + 32, 16), :256] = source[block, 32:48, 512:].astype(f32)
            up[pl.ds(row + 32, 16), 256:] = source[block, 48:64, 512:].astype(f32)
            if last:
                wide = source.shape[2] // 2
                proj[0][pl.ds(row, 16), :] = source[block, 64:80, :wide].astype(f32)
                proj[0][pl.ds(row + 16, 16), :] = source[block, 64:80, wide:].astype(f32)
                proj[0][pl.ds(row + 32, 16), :] = source[block, 80:, :wide].astype(f32)

    @pl.when(step == 0)
    def _():
        unpack(own, s[at])

    @pl.when(step == 1)
    def _():
        unpack(other, s[at + 1])

    gain[0, 0] = gain_in[0, 0] + row_sums(up[...] * w[...].astype(f32))


def unpack_ff(scalars, chunk, far, own, other, w, so_far):
    width, hidden = w.shape
    at = 2 + 2 * chunk
    last = own.shape[1] > 64

    def side(i, s):
        return (s[at + i] // 8) ^ far

    def half(i, s):
        return 2 * chunk + (s[0] ^ i)

    any_spec = pl.BlockSpec(memory_space=pl.ANY)
    column = spec((width // 2, 512), lambda i, s: (side(i, s), half(i, s)))
    gain = spec((1, 1, 8, width // 2), lambda i, s: (i, side(i, s), 0, 0))
    out_specs = [gain, spec((256, width), lambda i, s: (2 * half(i, s) + side(i, s), 0)), column]
    out_shape = [shape((2, 2, 8, width // 2), f32), shape((hidden, width), f32), shape((width, hidden), f32)]
    if last:
        out_specs.append(spec((width // 2, width // 2), lambda i, s: (s[0] ^ i, side(i, s))))
        out_shape.append(shape((width, width), f32))
    in_specs = [whole(own), whole(other), column]
    in_specs += [gain, any_spec, any_spec, any_spec][: len(so_far)]
    return call(
        functools.partial(unpack_ff_kernel, at, last),
        (2,),
        in_specs,
        out_specs,
        out_shape,
        (own, other, w) + tuple(so_far),
        scalars,
        28,
        aliases={4 + i: i for i in range(len(so_far))},
    )


def unpack_qkv_kernel(s, own, other, w, *refs):
    joint, gain = refs[-2:]
    step = pl.program_id(0)
    mine = s[1]

    def unpack(source, code):
        half = source.shape[2] // 6

        def place_columns(first):
            for block in range(2):
                rows = pl.ds(pl.multiple_of((block ^ (code & 1)) * 48, 16), 48)
                for part in range(3):
                    for side in range(2):
                        column = 2 * half * part + half * (first ^ side)
                        value = source[block, :, (3 * side + part) * half : (3 * side + part + 1) * half]
                        joint[rows, column : column + half] = value.astype(f32)

        for first in range(2):
            pl.when(mine == first)(functools.partial(place_columns, first))

    @pl.when(step < 2)
    def _():
        unpack(own, s[8])

    @pl.when(step >= 2)
    def _():
        unpack(other, s[9])

    gain[0] = row_sums(joint[...] * w[...].astype(f32))


def unpack_qkv(scalars, far, own, other, w, so_far):
    width = w.shape[0]

    def row(i, s):
        code = s[8 + i // 2]
        return 4 * (s[0] ^ (i // 2)) + 2 * ((code // 4) ^ far) + ((i & 1) ^ ((code // 2) & 1))

    def blocks(mine):
        return spec((2,) + own.shape[1:], lambda i, s: (jnp.clip(i - 2 * mine, 0, 1), 0, 0))

    any_spec = pl.BlockSpec(memory_space=pl.ANY)
    rows = spec((width // 8, 3 * width), lambda i, s: (row(i, s), 0))
    return call(
        unpack_qkv_kernel,
        (4,),
        [blocks(0), blocks(1), rows] + [any_spec] * len(so_far),
        [rows, spec((1, 8, width // 8), lambda i, s: (row(i, s), 0, 0))],
        [shape((width, 3 * width), f32), shape((8, 8, width // 8), f32)],
        (own, other, w) + tuple(so_far),
        scalars,
        28,
        aliases={4 + i: i for i in range(len(so_far))},
    )


def fast(tokens, visible, ln1_gain, w_qkv, w_proj, ln2_gain, w_up, w_down, d_out):
    tok, cot = tokens[0], d_out[0]
    rows, width = tok.shape
    gain1, gain2 = ln1_gain[None], ln2_gain[None]
    scalars = [lax.axis_index("dp") & 1, lax.axis_index("blk")]
    for orders in FF_ORDERS + (QKV_ORDER,):
        scalars.extend(places(orders))
    scalars = jnp.stack([jnp.int32(v) for v in scalars])

    order = Order()
    run = order.run
    vis_far = swap(visible, "y")
    tok_far = swap(tok, "y")
    half = width // 2
    freqs = jnp.exp(jnp.arange(half, dtype=f32) * (-math.log(10000.0) / half))[None]
    pos = run(functools.partial(positions, scalars), visible, freqs)
    normed1, qkv, resid = run(functools.partial(ln_qkv, scalars, False), tok, pos, gain1, w_qkv)
    sums = run(functools.partial(attention, scalars), qkv, qkv)
    pos_far = run(functools.partial(positions, scalars), vis_far, freqs)
    normed1_far, kv_far = run(functools.partial(ln_qkv, scalars, True), tok_far, pos_far, gain1, w_qkv)
    attended = run(functools.partial(attention, scalars), qkv, kv_far, *sums)
    resid2, normed2, normed2_t, att_half = run(
        functools.partial(project, scalars), attended, w_proj, resid, gain2
    )
    early = tuple(order.swap(array, "c") for array in (cot, normed2_t, att_half))

    streams, blocks, values = {}, {}, {"early": early}
    ff, proj, joint = (jnp.zeros((2, 2, 8, width // 2), f32),), (), ()

    def feed_forward(first):
        if first == 0:
            send, keep, *values["sums"] = run(
                functools.partial(ff_chunks, scalars, 0, 1), normed2, cot, w_up, w_down
            )
            values["act", 0], values["e0"] = keep, order.swap(send, "c")
            return
        more = (*values["sums"], resid2, gain2, w_proj, w_proj)
        send1, keep1, send2, keep2, out, grad2, branch, g_own, g_other = run(
            functools.partial(ff_chunks, scalars, 1, 2), normed2, cot, w_up, w_down, *more
        )
        values["act", 1], values["e1"] = keep1, order.swap(send1, "c")
        values["act", 2], values["e2"] = keep2, order.swap(send2, "c")
        values["branch"], values["branch_other"] = branch, order.swap(branch, "c")
        values["g"] = order.swap(g_other, "y")
        values.update(out=out, grad2=grad2, own=g_own)

    def weight_grads(chunk):
        early = (*values["early"][:2], normed2_t)
        more = ()
        if chunk == 2:
            more = (attended, values["early"][2], values["branch"], values["branch_other"])
        keep, send = run(
            functools.partial(ff_grads, scalars, chunk),
            values["act", chunk], values["e%d" % chunk], cot, *early, *more,
        )
        streams[chunk] = total(order, keep, send, list(zip(*FF_ORDERS[chunk])))
        advance(chunk)

    def advance(chunk):
        pair = next(streams[chunk])
        if pair is not None:
            blocks.setdefault(chunk, []).append(pair)

    def wait(key):
        if key[0] in "nf" and key[1:].isdigit():
            chunk, far = int(key[1:]), int(key[0] == "f")
            own, other = blocks[chunk][far]
            blocks[chunk][far] = own, run(lambda value: value, other)
            return
        value = values[key]
        values[key] = run(lambda *v: v if isinstance(value, tuple) else v[0], *(value if isinstance(value, tuple) else (value,)))

    def own_queries():
        values["attn"] = run(functools.partial(attention_back, scalars), qkv, values["own"], qkv, kv_far)

    def far_queries():
        gq, *sums = values["attn"]
        values["q"] = run(functools.partial(far_query, scalars), normed1_far, w_qkv)
        back = run(functools.partial(attention_back, scalars), values["q"], values["g"], qkv, kv_far, *sums)
        values["attn"] = (gq, *back)

    def joint_weights():
        keep, send = run(functools.partial(joint_grads, scalars), normed1, normed1_far, *values["attn"])
        links = [("c", "c")] + list(zip(*QKV_ORDER))
        streams[3] = total(order, keep, send, links, lambda a, b: jnp.concatenate([a, b], -1))
        advance(3)

    def back_joint():
        own, far = run(functools.partial(back_qkv, scalars), *values["attn"], w_qkv)
        values["norm"], values["bf"] = own, order.swap(far, "y")

    def finish_tokens():
        args = (values["norm"], values["bf"], resid, gain1, values["grad2"])
        values["tokens"] = run(functools.partial(token_grad, scalars), *args)

    def unpack(chunk, far):
        nonlocal ff, proj, joint
        own, other = blocks[chunk][far]
        if chunk == 3:
            joint = run(lambda a, b, *f: unpack_qkv(scalars, far, a, b, w_qkv, f), own, other, *joint)
            return
        so_far = ff + proj if chunk == 2 else ff
        weight = w_hbm if (chunk, far) == final else w_up
        result = tuple(
            run(lambda a, b, *f: unpack_ff(scalars, chunk, far, a, b, weight, f), own, other, *so_far)
        )
        ff, proj = result[:3], result[3:] or proj

    w_hbm = pltpu.with_memory_space_constraint(w_up, pltpu.HBM)
    final = [step[1:] for step in PLAN if step[0] == "unpack" and step[1] != 3][-1]
    steps = {
        "ff": feed_forward,
        "dw": weight_grads,
        "go": advance,
        "wait": wait,
        "own": own_queries,
        "far": far_queries,
        "joint": joint_weights,
        "back": back_joint,
        "tokens": finish_tokens,
        "unpack": unpack,
    }
    for name, *args in PLAN:
        steps[name](*args)
    sums2, d_down, d_up = ff
    d_qkv, sums1 = joint
    out, d_tokens, d_proj = values["out"], values["tokens"], proj[0]
    d_gain1 = sums1[:, 0].reshape(-1) / ln1_gain
    d_gain2 = (sums2[0, :, 0] + sums2[1, :, 0]).reshape(-1) / ln2_gain
    return out[None], d_tokens[None], d_gain1, d_qkv, d_proj, d_gain2, d_up, d_down


def layer_norm(values, gain):
    center = values - jnp.mean(values, -1, keepdims=True)
    spread = jnp.mean(center * center, -1, keepdims=True)
    return center * lax.rsqrt(spread + epsilon) * gain


def outer_product(left, right):
    return lax.dot_general(
        left, right, (((0,), (0,)), ((), ())), preferred_element_type=jnp.float32
    )


def times_transposed(left, weight):
    return lax.dot_general(
        left, weight, (((1,), (1,)), ((), ())), preferred_element_type=jnp.float32
    )


def split_blocks(keys, values):
    count = keys.shape[0]
    size = math.gcd(count, 512)
    shape = (count // size, size, HEADS, HD)
    return (keys.reshape(shape), values.reshape(shape))


def general(tokens, visible, ln1_gain, w_qkv, w_proj, ln2_gain, w_up, w_down, d_out):
    rows = tokens.shape[1]
    width = tokens.shape[2]
    factor = HD ** (-0.5)
    resid = tokens[0].astype(jnp.float32) + position_table(visible[0], width)
    normed1, back_one = jax.vjp(layer_norm, resid, ln1_gain)
    normed1 = normed1.astype(jnp.bfloat16)
    qkv = jnp.dot(normed1, w_qkv, preferred_element_type=jnp.float32).astype(jnp.bfloat16)
    query = qkv[:, :width]
    keys = qkv[:, width : 2 * width]
    values = qkv[:, 2 * width :]
    query_heads = query.reshape(rows, HEADS, HD)
    initial = (
        jnp.full((HEADS, rows), -1e30, jnp.float32),
        jnp.zeros((HEADS, rows), jnp.float32),
        jnp.zeros((HEADS, rows, HD), jnp.float32),
    )
    key_blocks, value_blocks = split_blocks(
        lax.all_gather(keys, "blk", axis=0, tiled=True),
        lax.all_gather(values, "blk", axis=0, tiled=True),
    )

    def one_block(state, block):
        running, total, accum = state
        block_keys, block_values = block
        scores = (
            jnp.einsum("qhd,khd->hqk", query_heads, block_keys, preferred_element_type=jnp.float32)
            * factor
        )
        top = jnp.maximum(running, jnp.max(scores, -1))
        weights = jnp.exp(scores - top[..., None])
        shrink = jnp.exp(running - top)
        total = total * shrink + jnp.sum(weights, -1)
        accum = accum * shrink[..., None] + jnp.einsum(
            "hqk,khd->hqd",
            weights.astype(jnp.bfloat16),
            block_values,
            preferred_element_type=jnp.float32,
        )
        return ((top, total, accum), None)

    running, total, accum = lax.scan(one_block, initial, (key_blocks, value_blocks))[0]
    log_total = running + jnp.log(total)
    attended = (accum / total[..., None]).transpose(1, 0, 2).reshape(rows, width)
    attended_low = attended.astype(jnp.bfloat16)
    resid2 = resid + jnp.dot(attended_low, w_proj, preferred_element_type=jnp.float32)
    normed2, back_two = jax.vjp(layer_norm, resid2, ln2_gain)
    normed2 = normed2.astype(jnp.bfloat16)
    hidden = jnp.dot(normed2, w_up, preferred_element_type=jnp.float32)
    activated, back_gelu = jax.vjp(jax.nn.gelu, hidden)
    activated = activated.astype(jnp.bfloat16)
    result = resid2 + jnp.dot(activated, w_down, preferred_element_type=jnp.float32)
    cotangent = d_out[0]
    grad_down = outer_product(activated, cotangent)
    (grad_hidden,) = back_gelu(times_transposed(cotangent, w_down))
    grad_hidden = grad_hidden.astype(jnp.bfloat16)
    grad_up = outer_product(normed2, grad_hidden)
    grad_resid2, grad_gain2 = back_two(times_transposed(grad_hidden, w_up))
    grad_resid2 = grad_resid2 + cotangent.astype(jnp.float32)
    grad_branch = grad_resid2.astype(jnp.bfloat16)
    grad_proj = outer_product(attended_low, grad_branch)
    grad_attended = times_transposed(grad_branch, w_proj).astype(jnp.bfloat16)
    correction = (grad_attended.astype(jnp.float32) * attended).reshape(rows, HEADS, HD)
    correction = jnp.sum(correction, -1).T
    grad_heads = grad_attended.reshape(rows, HEADS, HD)
    all_keys, all_values = (
        lax.all_gather(keys, "blk", axis=0, tiled=True),
        lax.all_gather(values, "blk", axis=0, tiled=True),
    )
    full_rows = all_keys.shape[0]
    key_blocks, value_blocks = split_blocks(all_keys, all_values)

    def back_block(grad_query, block):
        block_keys, block_values = block
        scores = (
            jnp.einsum("qhd,khd->hqk", query_heads, block_keys, preferred_element_type=jnp.float32)
            * factor
        )
        probs = jnp.exp(scores - log_total[..., None])
        grad_value = jnp.einsum(
            "hqk,qhd->khd",
            probs.astype(jnp.bfloat16),
            grad_heads,
            preferred_element_type=jnp.float32,
        )
        grad_probs = jnp.einsum(
            "qhd,khd->hqk", grad_heads, block_values, preferred_element_type=jnp.float32
        )
        grad_scores = (probs * (grad_probs - correction[..., None])).astype(jnp.bfloat16)
        grad_query = grad_query + jnp.einsum(
            "hqk,khd->qhd", grad_scores, block_keys, preferred_element_type=jnp.float32
        )
        grad_key = (
            jnp.einsum("hqk,qhd->khd", grad_scores, query_heads, preferred_element_type=jnp.float32)
            * factor
        )
        return (grad_query, (grad_key, grad_value))

    grad_query, (key_parts, value_parts) = lax.scan(
        back_block, jnp.zeros((rows, HEADS, HD), jnp.float32), (key_blocks, value_blocks)
    )
    grad_query = (grad_query * factor).reshape(rows, width)
    grad_keys, grad_values = (
        lax.psum_scatter(
            key_parts.reshape(full_rows, width).astype(jnp.bfloat16),
            "blk",
            scatter_dimension=0,
            tiled=True,
        ).astype(jnp.float32),
        lax.psum_scatter(
            value_parts.reshape(full_rows, width).astype(jnp.bfloat16),
            "blk",
            scatter_dimension=0,
            tiled=True,
        ).astype(jnp.float32),
    )
    grad_qkv = jnp.concatenate([grad_query, grad_keys, grad_values], 1).astype(jnp.bfloat16)
    grad_joint = outer_product(normed1, grad_qkv)
    grad_resid, grad_gain1 = back_one(times_transposed(grad_qkv, w_qkv))
    input_grad = grad_resid2 + grad_resid
    flats = (
        grad_joint.reshape(-1),
        grad_proj.reshape(-1),
        grad_up.reshape(-1),
        grad_down.reshape(-1),
    )
    shares = (
        lax.psum_scatter(flats[0], ("dp", "blk"), scatter_dimension=0, tiled=True),
        lax.psum_scatter(flats[1], ("dp", "blk"), scatter_dimension=0, tiled=True),
        lax.psum_scatter(flats[2], ("dp", "blk"), scatter_dimension=0, tiled=True),
        lax.psum_scatter(flats[3], ("dp", "blk"), scatter_dimension=0, tiled=True),
    )
    summed = (
        lax.all_gather(shares[0].astype(jnp.bfloat16), ("dp", "blk"), axis=0, tiled=True).astype(
            jnp.float32
        ),
        lax.all_gather(shares[1].astype(jnp.bfloat16), ("dp", "blk"), axis=0, tiled=True).astype(
            jnp.float32
        ),
        lax.all_gather(shares[2].astype(jnp.bfloat16), ("dp", "blk"), axis=0, tiled=True).astype(
            jnp.float32
        ),
        lax.all_gather(shares[3].astype(jnp.bfloat16), ("dp", "blk"), axis=0, tiled=True).astype(
            jnp.float32
        ),
    )
    gain_one, gain_two = lax.psum((grad_gain1, grad_gain2), ("dp", "blk"))
    return (
        result.astype(jnp.bfloat16)[None],
        input_grad[None],
        gain_one,
        summed[0].reshape(w_qkv.shape),
        summed[1].reshape(w_proj.shape),
        gain_two,
        summed[2].reshape(w_up.shape),
        summed[3].reshape(w_down.shape),
    )


def solution(mesh):
    split = mesh.shape["dp"] == 16 and mesh.shape["blk"] == 2
    return jax.shard_map(
        fast if split else general,
        mesh=mesh,
        in_specs=(
            P("dp", "blk", None),
            P("dp", "blk"),
            P(),
            P(),
            P(),
            P(),
            P(),
            P(),
            P("dp", "blk", None),
        ),
        out_specs=(P("dp", "blk", None), P("dp", "blk", None), P(), P(), P(), P(), P(), P()),
        check_vma=False,
    )
```

```python
import functools
import math

import jax
import jax.numpy as jnp
from jax import lax
from jax.experimental import pallas as pl
from jax.experimental.pallas import tpu as pltpu
from jax.sharding import PartitionSpec as P

HEADS = 12
HD = 64
PAIR = 2 * HD
epsilon = 1e-06
f32 = jnp.float32
bf16 = jnp.bfloat16
NN = ((1,), (0,))
NT = ((1,), (1,))
TN = ((0,), (0,))
AXES = ("dp", "blk")
MIB = 1 << 20


def dot(left, right, dims=NN):
    return lax.dot_general(left, right, (dims, ((), ())), preferred_element_type=f32)


def position_table(visible, width):
    half = width // 2
    column = jnp.arange(half, dtype=f32)
    freqs = jnp.exp(column * (-math.log(10000.0) / half))
    angles = visible.astype(f32)[..., None] * freqs
    return jnp.concatenate([jnp.sin(angles), jnp.cos(angles)], -1)


def normalize(values):
    center = values - jnp.mean(values, -1, keepdims=True)
    spread = jnp.mean(center * center, -1, keepdims=True)
    scale = lax.rsqrt(spread + epsilon)
    return center * scale, scale


def norm_backward(grad, gain, xhat, scale):
    e = grad * gain
    return scale * (
        e - jnp.mean(e, -1, keepdims=True) - xhat * jnp.mean(e * xhat, -1, keepdims=True)
    )


def call(kernel, grid, in_specs, out_specs, out_shape, args, scalars, vmem, scratch=(), aliases=None):
    return pl.pallas_call(
        kernel,
        grid_spec=pltpu.PrefetchScalarGridSpec(
            num_scalar_prefetch=1,
            grid=grid,
            in_specs=in_specs,
            out_specs=out_specs,
            scratch_shapes=list(scratch),
        ),
        out_shape=out_shape,
        input_output_aliases=aliases or {},
        compiler_params=pltpu.CompilerParams(vmem_limit_bytes=max(vmem, 28) * MIB),
        cost_estimate=pl.CostEstimate(flops=1, bytes_accessed=1, transcendentals=0),
    )(scalars, *args)


def spec(shape, index):
    return pl.BlockSpec(shape, index)


def whole(array):
    zeros = (0,) * array.ndim
    return pl.BlockSpec(array.shape, lambda i, s: zeros)


def shape(dims, dtype):
    return jax.ShapeDtypeStruct(dims, dtype)


FF_ORDERS = (
    (("x", "y", "z0", "z1"), ("y", "z0", "x", "z1")),
    (("z0", "y", "x", "z1"), ("x", "y", "z1", "z0")),
    (("y", "z0", "x", "z1"), ("x", "y", "z0", "z1")),
)
QKV_ORDER = (("x", "z0", "z1"), ("z0", "z1", "x"))
PLAN = (
    ("ff", 0), ("wait", "early"), ("ff", 1), ("wait", "e0"), ("dw", 0), ("own",),
    ("wait", "branch_other"), ("wait", "e2"), ("wait", "g"), ("dw", 2), ("wait", "e1"), ("dw", 1),
    ("go", 0), ("far",), ("go", 2), ("joint",), ("go", 0), ("go", 2), ("go", 1), ("go", 0),
    ("go", 3), ("go", 2), ("back",), ("go", 3), ("go", 1), ("go", 0), ("wait", "bf"), ("go", 2),
    ("go", 0), ("go", 3), ("go", 2), ("go", 1), ("go", 3), ("go", 0), ("go", 3), ("go", 2),
    ("go", 1), ("wait", "n0"), ("go", 0), ("unpack", 0, 0), ("go", 3), ("go", 1), ("wait", "f0"),
    ("tokens",), ("unpack", 0, 1), ("go", 2), ("wait", "n2"), ("unpack", 2, 0), ("go", 1),
    ("go", 3), ("wait", "f2"), ("wait", "n3"), ("unpack", 2, 1), ("unpack", 3, 0), ("wait", "f3"),
    ("unpack", 3, 1), ("go", 1), ("wait", "n1"), ("unpack", 1, 0), ("wait", "f1"), ("unpack", 1, 1),
)
DP_BIT = {"c": 1, "x": 2, "z0": 4, "z1": 8}


def swap(array, first, second=None):
    second = second or first
    pairs = []
    for d in range(16):
        for b in range(2):
            bit = second if d & 1 else first
            to = (d, b ^ 1) if bit == "y" else (d ^ DP_BIT[bit], b)
            pairs.append((d * 2 + b, to[0] * 2 + to[1]))
    return lax.ppermute(array, AXES, pairs)


def place(order):
    d, b = lax.axis_index("dp"), lax.axis_index("blk")
    code = jnp.int32(0)
    for bit in order:
        value = b & 1 if bit == "y" else (d // DP_BIT[bit]) & 1
        code = code * 2 + value
    return code


def places(orders):
    core = lax.axis_index("dp") & 1
    first, second = place(orders[0]), place(orders[1])
    return jnp.where(core == 0, first, second), jnp.where(core == 0, second, first)


def add(a, b):
    return (a.astype(f32) + b.astype(f32)).astype(bf16)


class Order:
    def __init__(self):
        self.last = None

    def pin(self, *arrays):
        if self.last is None:
            return arrays
        return lax.optimization_barrier((*arrays, self.last))[:-1]

    def run(self, function, *arrays):
        result = function(*self.pin(*arrays))
        self.last = result[0] if isinstance(result, (tuple, list)) else result
        return result

    def swap(self, array, first, second=None):
        return swap(self.pin(array)[0], first, second)


def total(order, keep, send, links, widen=None):
    received = order.swap(send, *links[0])
    yield
    for link in links[1:-1]:
        half = keep.shape[0] // 2
        send = order.run(lambda k, r: add(k[half:], r[half:]), keep, received)
        coming = order.swap(send, *link)
        keep = order.run(lambda k, r: add(k[:half], r[:half]), keep, received)
        received = coming
        yield
    keep = order.run(add, keep, received)
    received = order.swap(keep, *links[-1])
    yield
    block = order.run(lambda k, r: add(k, r[::-1]), keep, received)
    if widen is not None:
        received = order.swap(block, "y")
        yield
        block = order.run(widen, block, received)
    back = [link for link in links[:-1] if link[0] != "c"][::-1]
    for link in back[:-1]:
        received = order.swap(block, *link)
        yield
        block = order.run(lambda k, r: jnp.concatenate([k, r], 0), block, received)
    far = order.swap(block, *back[-1])
    other = order.swap(block, "c")
    yield block, other
    far = order.run(lambda value: value, far)
    yield far, order.swap(far, "c")


def sine_and_cosine(angle):
    turns = jnp.floor(angle * (2.0 / math.pi) + 0.5)
    rest = angle - turns * 1.5703125
    rest = rest - turns * 4.837512969970703125e-4
    rest = rest - turns * 7.54978995489188e-8
    square = rest * rest
    sine = rest + rest * square * (
        -1.6666654611e-1 + square * (8.3321608736e-3 + square * -1.9515295891e-4)
    )
    cosine = (1.0 - 0.5 * square) + square * square * (
        4.166664568298827e-2 + square * (-1.388731625493765e-3 + square * 2.443315711809948e-5)
    )
    quarter = turns.astype(jnp.int32)
    odd = (quarter & 1) == 1
    sin = jnp.where(odd, cosine, sine)
    cos = jnp.where(odd, sine, cosine)
    return (
        jnp.where((quarter & 2) == 2, -sin, sin),
        jnp.where(((quarter + 1) & 2) == 2, -cos, cos),
    )


def position_kernel(s, visible, freqs, out):
    column = jnp.broadcast_to(visible[...].astype(f32), (8, visible.shape[1])).T[:, :1]
    sin, cos = sine_and_cosine(column * freqs[...])
    half = sin.shape[1]
    out[:, :half] = sin
    out[:, half:] = cos


def positions(scalars, visible, freqs):
    rows, width = visible.shape[1], 2 * freqs.shape[1]
    out = shape((rows, width), f32)
    return call(
        position_kernel, (1,), [whole(visible), whole(freqs)], whole(out), out, (visible, freqs), scalars, 16
    )


def ln_qkv_kernel(s, tok, pos, gain, w, normed, qkv, *resid):
    @pl.when(pl.program_id(0) == 0)
    def _():
        value = tok[...].astype(f32) + pos[...]
        if resid:
            resid[0][...] = value
        xhat, _ = normalize(value)
        normed[...] = (xhat * gain[...]).astype(bf16)

    qkv[...] = dot(normed[...], w[...]).astype(bf16)


def ln_qkv(scalars, far, tok, pos, gain, w):
    rows, width = tok.shape
    full = spec((rows, width), lambda i, s: (0, 0))
    parts = 2 if far else 3
    out_shape = [shape((rows, width), bf16), shape((rows, parts * width), bf16)]
    return call(
        ln_qkv_kernel,
        (parts,),
        [full, full, whole(gain), spec((width, width), lambda i, s: (0, i + far))],
        [full, spec((rows, width), lambda i, s: (0, i))] + [full] * (not far),
        out_shape + [shape((rows, width), f32)] * (not far),
        (tok, pos, gain, w),
        scalars,
        24,
    )


def far_query_kernel(s, normed, w, out):
    out[...] = dot(normed[...], w[...]).astype(bf16)


def far_query(scalars, normed, w):
    rows, width = normed.shape
    out = shape((rows, width // 2), bf16)
    return call(
        far_query_kernel,
        (1,),
        [whole(normed), spec((width, width // 2), lambda i, s: (0, s[1]))],
        whole(out),
        out,
        (normed, w),
        scalars,
        16,
    )


def head_masks(x):
    lane = lax.broadcasted_iota(jnp.int32, x.shape, 1)
    return jnp.where(lane < HD, x, 0.0).astype(bf16), jnp.where(lane >= HD, x, 0.0).astype(bf16)


def attn_kernel(s, q, k, v, *refs):
    rows = q.shape[0]
    qs = jnp.concatenate(head_masks(q[...].astype(f32) * HD**-0.5), 0)
    scores = dot(k[...], qs, NT)
    top = jnp.max(scores, 0, keepdims=True)
    later = len(refs) == 3
    if later:
        acc_in, stat_in, out = refs
        before = stat_in[0, 0:1]
        top = jnp.maximum(top, before)
    e = jnp.exp(scores - top)
    total = jnp.sum(e, 0, keepdims=True)
    vt = v[...].T
    low = e.astype(bf16)
    parts = [dot(vt[h * HD : (h + 1) * HD], low[:, h * rows : (h + 1) * rows]) for h in range(2)]
    if not later:
        acc, stat = refs
        acc[0] = jnp.concatenate(parts, 0)
        stat[0, 0:1] = top
        stat[0, 1:2] = total
        return
    shrink = jnp.exp(before - top)
    scale = 1.0 / (total + stat_in[0, 1:2] * shrink)
    shrink = shrink * scale
    for h in range(2):
        at = slice(h * rows, (h + 1) * rows)
        held = acc_in[0, h * HD : (h + 1) * HD]
        parts[h] = parts[h] * scale[:, at] + held * shrink[:, at]
    out[...] = jnp.concatenate(parts, 0).T.astype(bf16)


def attention(scalars, qkv, keys, *so_far):
    rows, width = qkv.shape[0], qkv.shape[1] // 3
    pairs = width // PAIR

    def column(part):
        return spec((rows, PAIR), lambda i, s: (0, part * pairs + i))

    first = 0 if so_far else 1
    acc = spec((1, PAIR, rows), lambda i, s: (i, 0, 0))
    stat = spec((1, 8, 2 * rows), lambda i, s: (i, 0, 0))
    sums = [shape((pairs, PAIR, rows), f32), shape((pairs, 8, 2 * rows), f32)]
    return call(
        attn_kernel,
        (pairs,),
        [column(0), column(first), column(first + 1)] + ([acc, stat] if so_far else []),
        spec((rows, PAIR), lambda i, s: (0, i)) if so_far else [acc, stat],
        shape((rows, width), bf16) if so_far else sums,
        (qkv, keys, keys) + so_far,
        scalars,
        28,
    )


def proj_kernel(s, att, att_half, w, resid, gain, resid2, normed2, normed2_t, att_send):
    att_send[...] = att_half[...]
    value = resid[...] + dot(att[...], w[...])
    resid2[...] = value
    xhat, _ = normalize(value)
    low = (xhat * gain[...]).astype(bf16)
    normed2[...] = low
    normed2_t[...] = low.T


def project(scalars, att, w, resid, gain):
    rows, width = att.shape
    full = spec((rows, width), lambda i, s: (0, 0))
    half = spec((rows, width // 2), lambda i, s: (0, 1 - s[0]))
    return call(
        proj_kernel,
        (1,),
        [full, half, whole(w), full, whole(gain)],
        [
            full,
            full,
            spec((width, rows), lambda i, s: (0, 0)),
            spec((rows, width // 2), lambda i, s: (0, 0)),
        ],
        [
            shape((rows, width), f32),
            shape((rows, width), bf16),
            shape((width, rows), bf16),
            shape((rows, width // 2), bf16),
        ],
        (att, att, w, resid, gain),
        scalars,
        24,
    )


def gelu_and_slope(v):
    c = math.sqrt(2.0 / math.pi)
    square = v * v
    t = jnp.tanh(v * (c + (c * 0.044715) * square))
    act = 0.5 * v * (1.0 + t)
    slope = 0.5 * (1.0 + t) + (0.5 * v) * (1.0 - t * t) * (c + (3.0 * c * 0.044715) * square)
    return act, slope


def ff_kernel(count, s, normed, cot, up, down, *refs):
    step = pl.program_id(0)
    if count > 1:
        out_in, back_in, resid2, gain, w_own, w_other, *refs = refs
    pieces, refs = refs[: 2 * count], refs[2 * count :]
    if count > 1:
        out_low, grad2, branch, g_own, g_other, out, back = refs
    else:
        out, back = refs
    hidden = dot(normed[...], up[...])
    act, slope = gelu_and_slope(hidden)
    act = act.astype(bf16)
    grad = (dot(cot[...], down[...], NT) * slope).astype(bf16)
    out_part = dot(act, down[...])
    back_part = dot(grad, up[...], NT)

    @pl.when(step == 0)
    def _():
        out[...] = out_in[...] + out_part if count > 1 else out_part
        back[...] = back_in[...] + back_part if count > 1 else back_part

    @pl.when(step > 0)
    def _():
        out[...] += out_part
        back[...] += back_part

    for at, piece in enumerate(pieces):

        @pl.when(step == at)
        def _(piece=piece):
            piece[0] = act
            piece[1] = grad

    if count > 1:

        @pl.when(step == 2 * count - 1)
        def _():
            value = resid2[...]
            out_low[...] = (value + out[...]).astype(bf16)
            xhat, scale = normalize(value)
            g = cot[...].astype(f32) + norm_backward(back[...], gain[...], xhat, scale)
            grad2[...] = g
            low = g.astype(bf16)
            branch[...] = low
            g_other[...] = dot(low, w_other[...], NT).astype(bf16)
            g_own[...] = dot(low, w_own[...], NT).astype(bf16)


def ff_chunks(scalars, first, count, normed, cot, up, down, *more):
    rows, width = normed.shape
    half = width // 2
    wide = 512

    def column(i, s):
        return 2 * (first + i // 2) + (s[0] ^ (1 - (i & 1)))

    full = spec((rows, width), lambda i, s: (0, 0))
    part = spec((rows, half), lambda i, s: (0, 0))
    in_specs = [
        whole(normed),
        whole(cot),
        spec((width, wide), lambda i, s: (0, column(i, s))),
        spec((wide, width), lambda i, s: (column(i, s), 0)),
    ]
    out_specs = [spec((2, rows, wide), lambda i, s: (0, 0, 0))] * (2 * count)
    out_shape = [shape((2, rows, wide), bf16)] * (2 * count)
    scratch = []
    if count > 1:
        in_specs += [
            full,
            full,
            full,
            spec((1, width), lambda i, s: (0, 0)),
            spec((half, width), lambda i, s: (s[1], 0)),
            spec((half, width), lambda i, s: (1 - s[1], 0)),
        ]
        out_specs += [full, full, full, part, part]
        out_shape += [shape((rows, width), t) for t in (bf16, f32, bf16)]
        out_shape += [shape((rows, half), bf16)] * 2
        scratch = [pltpu.VMEM((rows, width), f32)] * 2
    else:
        out_specs += [full, full]
        out_shape += [shape((rows, width), f32)] * 2
    return call(
        functools.partial(ff_kernel, count),
        (2 * count,),
        in_specs,
        out_specs,
        out_shape,
        (normed, cot, up, down) + more,
        scalars,
        28,
        scratch,
    )


def ff_grads_kernel(at, s, act, act_o, grad, grad_o, cot, cot_o, nt, nt_o, *refs):
    keep, send = refs[-2:]
    step = pl.program_id(0)
    rows_both = jnp.concatenate([cot[...], cot_o[...]], 0)
    g_down = dot(jnp.concatenate([act[0], act_o[0]], 0), rows_both, TN).astype(bf16)
    grads = jnp.concatenate([grad[0], grad_o[0]], 0)
    g_up = dot(jnp.concatenate([nt[...], nt_o[...]], 1), grads).astype(bf16)
    g_proj = None
    if len(refs) > 2:
        att, att_o, branch, branch_o = refs[:4]
        both = jnp.concatenate([branch[...], branch_o[...]], 0)
        g_proj = dot(jnp.concatenate([att[...], att_o[...]], 0), both, TN).astype(bf16)
    code = s[at] & 7

    def store(target):
        rows_d = g_down.shape[0] // 8
        rows_u = g_up.shape[0] // 8
        half = g_up.shape[1] // 2
        for block in range(8):
            to = block ^ code
            target[to, :rows_d, :] = g_down[block * rows_d : (block + 1) * rows_d]
            part = g_up[block * rows_u : (block + 1) * rows_u]
            target[to, 32:64, : 2 * half] = part[:32]
            target[to, 32:48, 2 * half :] = part[32:, :half]
            target[to, 48:64, 2 * half :] = part[32:, half:]
            if g_proj is not None:
                part = g_proj[block * rows_u : (block + 1) * rows_u]
                wide = part.shape[1]
                target[to, 64:80, :wide] = part[:16]
                target[to, 64:80, wide:] = part[16:32]
                target[to, 80:, :wide] = part[32:]
                target[to, 80:, wide:] = jnp.zeros_like(part[32:])

    @pl.when(step == 0)
    def _():
        store(send)

    @pl.when(step == 1)
    def _():
        store(keep)


def ff_grads(scalars, chunk, mine, theirs, cot, cot_other, normed_t_other, normed_t, *proj):
    rows, width = cot.shape
    wide = mine.shape[2]
    at = 2 + 2 * chunk

    def side(i, s):
        return (1 - i) ^ (s[at] // 8)

    act = spec((1, rows, wide // 2), lambda i, s: (0, 0, side(i, s)))
    grad = spec((1, rows, wide), lambda i, s: (1, 0, 0))
    feature = spec((width // 2, rows), lambda i, s: (side(i, s), 0))
    in_specs = [act, act, grad, grad, whole(cot), whole(cot), feature, feature]
    if proj:
        half = width // 2
        column = spec((rows, half), lambda i, s: (0, side(i, s)))
        in_specs += [spec((rows, half), lambda i, s: (0, s[0])), whole(proj[1]), column, column]
    deep = 96 if proj else 64
    piece = spec((8, deep, width), lambda i, s: (0, 0, 0))
    return call(
        functools.partial(ff_grads_kernel, at),
        (2,),
        in_specs,
        [piece, piece],
        [shape((8, deep, width), bf16)] * 2,
        (mine, theirs, mine, theirs, cot, cot_other, normed_t, normed_t_other) + proj,
        scalars,
        28,
    )


def attn_back_kernel(s, q, g, k_o, k_f, v_o, v_f, *refs):
    gk_in, gv_in = refs[:2] if len(refs) == 5 else (None, None)
    gq, gk, gv = refs[-3:]
    k = jnp.concatenate([k_o[...], k_f[...]], 0)
    v = jnp.concatenate([v_o[...], v_f[...]], 0)
    kt = (k.astype(f32) * HD**-0.5).astype(bf16).T
    rows = q.shape[0]
    qs = jnp.concatenate(head_masks(q[...].astype(f32) * HD**-0.5), 0)
    gs = jnp.concatenate(head_masks(g[...].astype(f32)), 0)
    scores = dot(k, qs, NT)
    e = jnp.exp(scores - jnp.max(scores, 0, keepdims=True))
    probs = e * (1.0 / jnp.sum(e, 0, keepdims=True))
    grad_v = dot(probs.astype(bf16), gs)
    grad_p = dot(v, gs, NT)
    row = jnp.sum(probs * grad_p, 0, keepdims=True)
    grad_s = (probs * (grad_p - row)).astype(bf16)
    grad_k = dot(grad_s, qs)
    grad_q = [
        dot(kt[h * HD : (h + 1) * HD], grad_s[:, h * rows : (h + 1) * rows]) for h in range(2)
    ]
    if gk_in is not None:
        grad_k, grad_v = grad_k + gk_in[...], grad_v + gv_in[...]
    gq[...] = jnp.concatenate(grad_q, 0).T.astype(bf16)
    gk[...] = grad_k.astype(gk.dtype)
    gv[...] = grad_v.astype(gv.dtype)


def attention_back(scalars, query, grad, qkv, kv_far, *so_far):
    rows, width = qkv.shape[0], qkv.shape[1] // 3
    pairs = width // PAIR
    mine = pairs // 2

    def column(part):
        return spec((rows, PAIR), lambda i, s: (0, part * pairs + mine * s[1] + i))

    block = spec((rows, PAIR), lambda i, s: (0, i))
    both = spec((2 * rows, PAIR), lambda i, s: (0, i))
    dtype = bf16 if so_far else f32
    return call(
        attn_back_kernel,
        (mine,),
        [block if so_far else column(0), block, column(1), column(0), column(2), column(1)]
        + [both] * len(so_far),
        [block, both, both],
        [shape((rows, width // 2), bf16)] + [shape((2 * rows, width // 2), dtype)] * 2,
        (query, grad, qkv, kv_far, qkv, kv_far) + so_far,
        scalars,
        28,
    )


def joint_kernel(s, n_own, n_far, gq_o, gq_f, gk, gv, keep, send):
    step = pl.program_id(0)
    gq = jnp.concatenate([gq_o[...], gq_f[...]], 0)
    n = jnp.concatenate([n_own[...], n_far[...]], 0)
    cols = gk.shape[1]

    def fill(target, code):
        tiles = [dot(n, g, TN).astype(bf16) for g in (gq, gk[...], gv[...])]
        rows = tiles[0].shape[0] // 8
        for block in range(8):
            at = block ^ code
            for i, tile in enumerate(tiles):
                part = tile[block * rows : (block + 1) * rows]
                target[at, :, i * cols : i * cols + part.shape[1]] = part

    @pl.when(step == 0)
    def _():
        fill(send, s[9])

    @pl.when(step == 1)
    def _():
        fill(keep, s[8])


def joint_grads(scalars, n_own, n_far, gq, gq_far, gk, gv):
    rows, width = n_own.shape
    half = width // 2
    feature = spec((rows, half), lambda i, s: (0, s[0] ^ (1 - i)))
    cols = 3 * half
    piece = spec((8, half // 8, cols), lambda i, s: (0, 0, 0))
    return call(
        joint_kernel,
        (2,),
        [feature, feature, whole(gq), whole(gq), whole(gk), whole(gv)],
        [piece, piece],
        [shape((8, half // 8, cols), bf16)] * 2,
        (n_own, n_far, gq, gq_far, gk, gv),
        scalars,
        28,
    )


def back_qkv_kernel(s, gq_o, gq_f, gk, gv, wq, wk, wv, own, far):
    rows = own.shape[0]

    def part(gq, at):
        total = dot(gq[...], wq[...], NT)
        total += dot(gk[pl.ds(at, rows)], wk[...], NT)
        return total + dot(gv[pl.ds(at, rows)], wv[...], NT)

    far[...] = part(gq_f, rows).astype(bf16)
    own[...] = part(gq_o, 0)


def back_qkv(scalars, gq, gq_far, gk, gv, w):
    rows, half = gq.shape
    width = 2 * half

    def column(part):
        return spec((width, half), lambda i, s: (0, 2 * part + s[1]))

    full = spec((rows, width), lambda i, s: (0, 0))
    return call(
        back_qkv_kernel,
        (1,),
        [whole(gq), whole(gq), whole(gk), whole(gv), column(0), column(1), column(2)],
        [full, full],
        [shape((rows, width), f32), shape((rows, width), bf16)],
        (gq, gq_far, gk, gv, w, w, w),
        scalars,
        28,
    )


def last_kernel(s, own, far, resid, gain, grad2, out):
    xhat, scale = normalize(resid[...])
    grad = own[...] + far[...].astype(f32)
    out[...] = grad2[...] + norm_backward(grad, gain[...], xhat, scale)


def token_grad(scalars, own, far, resid, gain, grad2):
    args = (own, far, resid, gain, grad2)
    return call(
        last_kernel,
        (1,),
        [whole(a) for a in args],
        whole(own),
        shape(own.shape, f32),
        args,
        scalars,
        24,
    )


def row_sums(values):
    folded = sum(values[:, at : at + 128] for at in range(0, values.shape[1], 128))
    return lax.dot_general(
        jnp.ones((8, 128), f32),
        folded,
        (NT, ((), ())),
        precision=lax.Precision.HIGHEST,
        preferred_element_type=f32,
    )


def unpack_ff_kernel(at, last, s, own, other, w, gain_in, *refs):
    gain, down, up, *proj = refs[-4:] if last else refs[-3:]
    step = pl.program_id(0)

    def unpack(source, code):
        for block in range(8):
            to = block ^ (code & 7)
            down[pl.ds(pl.multiple_of(to * 32, 32), 32), :] = source[block, :32, :].astype(f32)
            row = pl.multiple_of(to * 48, 16)
            up[pl.ds(row, 32), :] = source[block, 32:64, :512].astype(f32)
            up[pl.ds(row + 32, 16), :256] = source[block, 32:48, 512:].astype(f32)
            up[pl.ds(row + 32, 16), 256:] = source[block, 48:64, 512:].astype(f32)
            if last:
                wide = source.shape[2] // 2
                proj[0][pl.ds(row, 16), :] = source[block, 64:80, :wide].astype(f32)
                proj[0][pl.ds(row + 16, 16), :] = source[block, 64:80, wide:].astype(f32)
                proj[0][pl.ds(row + 32, 16), :] = source[block, 80:, :wide].astype(f32)

    @pl.when(step == 0)
    def _():
        unpack(own, s[at])

    @pl.when(step == 1)
    def _():
        unpack(other, s[at + 1])

    gain[0, 0] = gain_in[0, 0] + row_sums(up[...] * w[...].astype(f32))


def unpack_ff(scalars, chunk, far, own, other, w, so_far):
    width, hidden = w.shape
    at = 2 + 2 * chunk
    last = own.shape[1] > 64

    def side(i, s):
        return (s[at + i] // 8) ^ far

    def half(i, s):
        return 2 * chunk + (s[0] ^ i)

    any_spec = pl.BlockSpec(memory_space=pl.ANY)
    column = spec((width // 2, 512), lambda i, s: (side(i, s), half(i, s)))
    gain = spec((1, 1, 8, width // 2), lambda i, s: (i, side(i, s), 0, 0))
    out_specs = [gain, spec((256, width), lambda i, s: (2 * half(i, s) + side(i, s), 0)), column]
    out_shape = [shape((2, 2, 8, width // 2), f32), shape((hidden, width), f32), shape((width, hidden), f32)]
    if last:
        out_specs.append(spec((width // 2, width // 2), lambda i, s: (s[0] ^ i, side(i, s))))
        out_shape.append(shape((width, width), f32))
    in_specs = [whole(own), whole(other), column]
    in_specs += [gain, any_spec, any_spec, any_spec][: len(so_far)]
    return call(
        functools.partial(unpack_ff_kernel, at, last),
        (2,),
        in_specs,
        out_specs,
        out_shape,
        (own, other, w) + tuple(so_far),
        scalars,
        28,
        aliases={4 + i: i for i in range(len(so_far))},
    )


def unpack_qkv_kernel(s, own, other, w, *refs):
    joint, gain = refs[-2:]
    step = pl.program_id(0)
    mine = s[1]

    def unpack(source, code):
        half = source.shape[2] // 6

        def place_columns(first):
            for block in range(2):
                rows = pl.ds(pl.multiple_of((block ^ (code & 1)) * 48, 16), 48)
                for part in range(3):
                    for side in range(2):
                        column = 2 * half * part + half * (first ^ side)
                        value = source[block, :, (3 * side + part) * half : (3 * side + part + 1) * half]
                        joint[rows, column : column + half] = value.astype(f32)

        for first in range(2):
            pl.when(mine == first)(functools.partial(place_columns, first))

    @pl.when(step < 2)
    def _():
        unpack(own, s[8])

    @pl.when(step >= 2)
    def _():
        unpack(other, s[9])

    gain[0] = row_sums(joint[...] * w[...].astype(f32))


def unpack_qkv(scalars, far, own, other, w, so_far):
    width = w.shape[0]

    def row(i, s):
        code = s[8 + i // 2]
        return 4 * (s[0] ^ (i // 2)) + 2 * ((code // 4) ^ far) + ((i & 1) ^ ((code // 2) & 1))

    def blocks(mine):
        return spec((2,) + own.shape[1:], lambda i, s: (jnp.clip(i - 2 * mine, 0, 1), 0, 0))

    any_spec = pl.BlockSpec(memory_space=pl.ANY)
    rows = spec((width // 8, 3 * width), lambda i, s: (row(i, s), 0))
    return call(
        unpack_qkv_kernel,
        (4,),
        [blocks(0), blocks(1), rows] + [any_spec] * len(so_far),
        [rows, spec((1, 8, width // 8), lambda i, s: (row(i, s), 0, 0))],
        [shape((width, 3 * width), f32), shape((8, 8, width // 8), f32)],
        (own, other, w) + tuple(so_far),
        scalars,
        28,
        aliases={4 + i: i for i in range(len(so_far))},
    )


def fast(tokens, visible, ln1_gain, w_qkv, w_proj, ln2_gain, w_up, w_down, d_out):
    tok, cot = tokens[0], d_out[0]
    rows, width = tok.shape
    gain1, gain2 = ln1_gain[None], ln2_gain[None]
    scalars = [lax.axis_index("dp") & 1, lax.axis_index("blk")]
    for orders in FF_ORDERS + (QKV_ORDER,):
        scalars.extend(places(orders))
    scalars = jnp.stack([jnp.int32(v) for v in scalars])

    order = Order()
    run = order.run
    vis_far = swap(visible, "y")
    tok_far = swap(tok, "y")
    half = width // 2
    freqs = jnp.exp(jnp.arange(half, dtype=f32) * (-math.log(10000.0) / half))[None]
    pos = run(functools.partial(positions, scalars), visible, freqs)
    normed1, qkv, resid = run(functools.partial(ln_qkv, scalars, False), tok, pos, gain1, w_qkv)
    sums = run(functools.partial(attention, scalars), qkv, qkv)
    pos_far = run(functools.partial(positions, scalars), vis_far, freqs)
    normed1_far, kv_far = run(functools.partial(ln_qkv, scalars, True), tok_far, pos_far, gain1, w_qkv)
    attended = run(functools.partial(attention, scalars), qkv, kv_far, *sums)
    resid2, normed2, normed2_t, att_half = run(
        functools.partial(project, scalars), attended, w_proj, resid, gain2
    )
    early = tuple(order.swap(array, "c") for array in (cot, normed2_t, att_half))

    streams, blocks, values = {}, {}, {"early": early}
    ff, proj, joint = (jnp.zeros((2, 2, 8, width // 2), f32),), (), ()

    def feed_forward(first):
        if first == 0:
            send, keep, *values["sums"] = run(
                functools.partial(ff_chunks, scalars, 0, 1), normed2, cot, w_up, w_down
            )
            values["act", 0], values["e0"] = keep, order.swap(send, "c")
            return
        more = (*values["sums"], resid2, gain2, w_proj, w_proj)
        send1, keep1, send2, keep2, out, grad2, branch, g_own, g_other = run(
            functools.partial(ff_chunks, scalars, 1, 2), normed2, cot, w_up, w_down, *more
        )
        values["act", 1], values["e1"] = keep1, order.swap(send1, "c")
        values["act", 2], values["e2"] = keep2, order.swap(send2, "c")
        values["branch"], values["branch_other"] = branch, order.swap(branch, "c")
        values["g"] = order.swap(g_other, "y")
        values.update(out=out, grad2=grad2, own=g_own)

    def weight_grads(chunk):
        early = (*values["early"][:2], normed2_t)
        more = ()
        if chunk == 2:
            more = (attended, values["early"][2], values["branch"], values["branch_other"])
        keep, send = run(
            functools.partial(ff_grads, scalars, chunk),
            values["act", chunk], values["e%d" % chunk], cot, *early, *more,
        )
        streams[chunk] = total(order, keep, send, list(zip(*FF_ORDERS[chunk])))
        advance(chunk)

    def advance(chunk):
        pair = next(streams[chunk])
        if pair is not None:
            blocks.setdefault(chunk, []).append(pair)

    def wait(key):
        if key[0] in "nf" and key[1:].isdigit():
            chunk, far = int(key[1:]), int(key[0] == "f")
            own, other = blocks[chunk][far]
            blocks[chunk][far] = own, run(lambda value: value, other)
            return
        value = values[key]
        values[key] = run(lambda *v: v if isinstance(value, tuple) else v[0], *(value if isinstance(value, tuple) else (value,)))

    def own_queries():
        values["attn"] = run(functools.partial(attention_back, scalars), qkv, values["own"], qkv, kv_far)

    def far_queries():
        gq, *sums = values["attn"]
        values["q"] = run(functools.partial(far_query, scalars), normed1_far, w_qkv)
        back = run(functools.partial(attention_back, scalars), values["q"], values["g"], qkv, kv_far, *sums)
        values["attn"] = (gq, *back)

    def joint_weights():
        keep, send = run(functools.partial(joint_grads, scalars), normed1, normed1_far, *values["attn"])
        links = [("c", "c")] + list(zip(*QKV_ORDER))
        streams[3] = total(order, keep, send, links, lambda a, b: jnp.concatenate([a, b], -1))
        advance(3)

    def back_joint():
        own, far = run(functools.partial(back_qkv, scalars), *values["attn"], w_qkv)
        values["norm"], values["bf"] = own, order.swap(far, "y")

    def finish_tokens():
        args = (values["norm"], values["bf"], resid, gain1, values["grad2"])
        values["tokens"] = run(functools.partial(token_grad, scalars), *args)

    def unpack(chunk, far):
        nonlocal ff, proj, joint
        own, other = blocks[chunk][far]
        if chunk == 3:
            joint = run(lambda a, b, *f: unpack_qkv(scalars, far, a, b, w_qkv, f), own, other, *joint)
            return
        so_far = ff + proj if chunk == 2 else ff
        weight = w_hbm if (chunk, far) == final else w_up
        result = tuple(
            run(lambda a, b, *f: unpack_ff(scalars, chunk, far, a, b, weight, f), own, other, *so_far)
        )
        ff, proj = result[:3], result[3:] or proj

    w_hbm = pltpu.with_memory_space_constraint(w_up, pltpu.HBM)
    final = [step[1:] for step in PLAN if step[0] == "unpack" and step[1] != 3][-1]
    steps = {
        "ff": feed_forward,
        "dw": weight_grads,
        "go": advance,
        "wait": wait,
        "own": own_queries,
        "far": far_queries,
        "joint": joint_weights,
        "back": back_joint,
        "tokens": finish_tokens,
        "unpack": unpack,
    }
    for name, *args in PLAN:
        steps[name](*args)
    sums2, d_down, d_up = ff
    d_qkv, sums1 = joint
    out, d_tokens, d_proj = values["out"], values["tokens"], proj[0]
    d_gain1 = sums1[:, 0].reshape(-1) / ln1_gain
    d_gain2 = (sums2[0, :, 0] + sums2[1, :, 0]).reshape(-1) / ln2_gain
    return out[None], d_tokens[None], d_gain1, d_qkv, d_proj, d_gain2, d_up, d_down


def layer_norm(values, gain):
    center = values - jnp.mean(values, -1, keepdims=True)
    spread = jnp.mean(center * center, -1, keepdims=True)
    return center * lax.rsqrt(spread + epsilon) * gain


def outer_product(left, right):
    return lax.dot_general(
        left, right, (((0,), (0,)), ((), ())), preferred_element_type=jnp.float32
    )


def times_transposed(left, weight):
    return lax.dot_general(
        left, weight, (((1,), (1,)), ((), ())), preferred_element_type=jnp.float32
    )


def split_blocks(keys, values):
    count = keys.shape[0]
    size = math.gcd(count, 512)
    shape = (count // size, size, HEADS, HD)
    return (keys.reshape(shape), values.reshape(shape))


def general(tokens, visible, ln1_gain, w_qkv, w_proj, ln2_gain, w_up, w_down, d_out):
    rows = tokens.shape[1]
    width = tokens.shape[2]
    factor = HD ** (-0.5)
    resid = tokens[0].astype(jnp.float32) + position_table(visible[0], width)
    normed1, back_one = jax.vjp(layer_norm, resid, ln1_gain)
    normed1 = normed1.astype(jnp.bfloat16)
    qkv = jnp.dot(normed1, w_qkv, preferred_element_type=jnp.float32).astype(jnp.bfloat16)
    query = qkv[:, :width]
    keys = qkv[:, width : 2 * width]
    values = qkv[:, 2 * width :]
    query_heads = query.reshape(rows, HEADS, HD)
    initial = (
        jnp.full((HEADS, rows), -1e30, jnp.float32),
        jnp.zeros((HEADS, rows), jnp.float32),
        jnp.zeros((HEADS, rows, HD), jnp.float32),
    )
    key_blocks, value_blocks = split_blocks(
        lax.all_gather(keys, "blk", axis=0, tiled=True),
        lax.all_gather(values, "blk", axis=0, tiled=True),
    )

    def one_block(state, block):
        running, total, accum = state
        block_keys, block_values = block
        scores = (
            jnp.einsum("qhd,khd->hqk", query_heads, block_keys, preferred_element_type=jnp.float32)
            * factor
        )
        top = jnp.maximum(running, jnp.max(scores, -1))
        weights = jnp.exp(scores - top[..., None])
        shrink = jnp.exp(running - top)
        total = total * shrink + jnp.sum(weights, -1)
        accum = accum * shrink[..., None] + jnp.einsum(
            "hqk,khd->hqd",
            weights.astype(jnp.bfloat16),
            block_values,
            preferred_element_type=jnp.float32,
        )
        return ((top, total, accum), None)

    running, total, accum = lax.scan(one_block, initial, (key_blocks, value_blocks))[0]
    log_total = running + jnp.log(total)
    attended = (accum / total[..., None]).transpose(1, 0, 2).reshape(rows, width)
    attended_low = attended.astype(jnp.bfloat16)
    resid2 = resid + jnp.dot(attended_low, w_proj, preferred_element_type=jnp.float32)
    normed2, back_two = jax.vjp(layer_norm, resid2, ln2_gain)
    normed2 = normed2.astype(jnp.bfloat16)
    hidden = jnp.dot(normed2, w_up, preferred_element_type=jnp.float32)
    activated, back_gelu = jax.vjp(jax.nn.gelu, hidden)
    activated = activated.astype(jnp.bfloat16)
    result = resid2 + jnp.dot(activated, w_down, preferred_element_type=jnp.float32)
    cotangent = d_out[0]
    grad_down = outer_product(activated, cotangent)
    (grad_hidden,) = back_gelu(times_transposed(cotangent, w_down))
    grad_hidden = grad_hidden.astype(jnp.bfloat16)
    grad_up = outer_product(normed2, grad_hidden)
    grad_resid2, grad_gain2 = back_two(times_transposed(grad_hidden, w_up))
    grad_resid2 = grad_resid2 + cotangent.astype(jnp.float32)
    grad_branch = grad_resid2.astype(jnp.bfloat16)
    grad_proj = outer_product(attended_low, grad_branch)
    grad_attended = times_transposed(grad_branch, w_proj).astype(jnp.bfloat16)
    correction = (grad_attended.astype(jnp.float32) * attended).reshape(rows, HEADS, HD)
    correction = jnp.sum(correction, -1).T
    grad_heads = grad_attended.reshape(rows, HEADS, HD)
    all_keys, all_values = (
        lax.all_gather(keys, "blk", axis=0, tiled=True),
        lax.all_gather(values, "blk", axis=0, tiled=True),
    )
    full_rows = all_keys.shape[0]
    key_blocks, value_blocks = split_blocks(all_keys, all_values)

    def back_block(grad_query, block):
        block_keys, block_values = block
        scores = (
            jnp.einsum("qhd,khd->hqk", query_heads, block_keys, preferred_element_type=jnp.float32)
            * factor
        )
        probs = jnp.exp(scores - log_total[..., None])
        grad_value = jnp.einsum(
            "hqk,qhd->khd",
            probs.astype(jnp.bfloat16),
            grad_heads,
            preferred_element_type=jnp.float32,
        )
        grad_probs = jnp.einsum(
            "qhd,khd->hqk", grad_heads, block_values, preferred_element_type=jnp.float32
        )
        grad_scores = (probs * (grad_probs - correction[..., None])).astype(jnp.bfloat16)
        grad_query = grad_query + jnp.einsum(
            "hqk,khd->qhd", grad_scores, block_keys, preferred_element_type=jnp.float32
        )
        grad_key = (
            jnp.einsum("hqk,qhd->khd", grad_scores, query_heads, preferred_element_type=jnp.float32)
            * factor
        )
        return (grad_query, (grad_key, grad_value))

    grad_query, (key_parts, value_parts) = lax.scan(
        back_block, jnp.zeros((rows, HEADS, HD), jnp.float32), (key_blocks, value_blocks)
    )
    grad_query = (grad_query * factor).reshape(rows, width)
    grad_keys, grad_values = (
        lax.psum_scatter(
            key_parts.reshape(full_rows, width).astype(jnp.bfloat16),
            "blk",
            scatter_dimension=0,
            tiled=True,
        ).astype(jnp.float32),
        lax.psum_scatter(
            value_parts.reshape(full_rows, width).astype(jnp.bfloat16),
            "blk",
            scatter_dimension=0,
            tiled=True,
        ).astype(jnp.float32),
    )
    grad_qkv = jnp.concatenate([grad_query, grad_keys, grad_values], 1).astype(jnp.bfloat16)
    grad_joint = outer_product(normed1, grad_qkv)
    grad_resid, grad_gain1 = back_one(times_transposed(grad_qkv, w_qkv))
    input_grad = grad_resid2 + grad_resid
    flats = (
        grad_joint.reshape(-1),
        grad_proj.reshape(-1),
        grad_up.reshape(-1),
        grad_down.reshape(-1),
    )
    shares = (
        lax.psum_scatter(flats[0], ("dp", "blk"), scatter_dimension=0, tiled=True),
        lax.psum_scatter(flats[1], ("dp", "blk"), scatter_dimension=0, tiled=True),
        lax.psum_scatter(flats[2], ("dp", "blk"), scatter_dimension=0, tiled=True),
        lax.psum_scatter(flats[3], ("dp", "blk"), scatter_dimension=0, tiled=True),
    )
    summed = (
        lax.all_gather(shares[0].astype(jnp.bfloat16), ("dp", "blk"), axis=0, tiled=True).astype(
            jnp.float32
        ),
        lax.all_gather(shares[1].astype(jnp.bfloat16), ("dp", "blk"), axis=0, tiled=True).astype(
            jnp.float32
        ),
        lax.all_gather(shares[2].astype(jnp.bfloat16), ("dp", "blk"), axis=0, tiled=True).astype(
            jnp.float32
        ),
        lax.all_gather(shares[3].astype(jnp.bfloat16), ("dp", "blk"), axis=0, tiled=True).astype(
            jnp.float32
        ),
    )
    gain_one, gain_two = lax.psum((grad_gain1, grad_gain2), ("dp", "blk"))
    return (
        result.astype(jnp.bfloat16)[None],
        input_grad[None],
        gain_one,
        summed[0].reshape(w_qkv.shape),
        summed[1].reshape(w_proj.shape),
        gain_two,
        summed[2].reshape(w_up.shape),
        summed[3].reshape(w_down.shape),
    )


def solution(mesh):
    split = mesh.shape["dp"] == 16 and mesh.shape["blk"] == 2
    return jax.shard_map(
        fast if split else general,
        mesh=mesh,
        in_specs=(
            P("dp", "blk", None),
            P("dp", "blk"),
            P(),
            P(),
            P(),
            P(),
            P(),
            P(),
            P("dp", "blk", None),
        ),
        out_specs=(P("dp", "blk", None), P("dp", "blk", None), P(), P(), P(), P(), P(), P()),
        check_vma=False,
    )
```

```python
import functools
import math

import jax
import jax.numpy as jnp
from jax import lax
from jax.experimental import pallas as pl
from jax.experimental.pallas import tpu as pltpu
from jax.sharding import PartitionSpec as P

HEADS = 12
HD = 64
PAIR = 2 * HD
GROUP = 2
BACK_GROUP = 3
BACK_LIMIT = 28
epsilon = 1e-06
f32 = jnp.float32
bf16 = jnp.bfloat16
NN = ((1,), (0,))
NT = ((1,), (1,))
TN = ((0,), (0,))
AXES = ("dp", "blk")
MIB = 1 << 20


def dot(left, right, dims=NN):
    return lax.dot_general(left, right, (dims, ((), ())), preferred_element_type=f32)


def position_table(visible, width):
    half = width // 2
    column = jnp.arange(half, dtype=f32)
    freqs = jnp.exp(column * (-math.log(10000.0) / half))
    angles = visible.astype(f32)[..., None] * freqs
    return jnp.concatenate([jnp.sin(angles), jnp.cos(angles)], -1)


def normalize(values):
    center = values - jnp.mean(values, -1, keepdims=True)
    spread = jnp.mean(center * center, -1, keepdims=True)
    scale = lax.rsqrt(spread + epsilon)
    return center * scale, scale


def norm_backward(grad, gain, xhat, scale):
    e = grad * gain
    return scale * (
        e - jnp.mean(e, -1, keepdims=True) - xhat * jnp.mean(e * xhat, -1, keepdims=True)
    )


def call(kernel, grid, in_specs, out_specs, out_shape, args, scalars, vmem, scratch=(), aliases=None):
    return pl.pallas_call(
        kernel,
        grid_spec=pltpu.PrefetchScalarGridSpec(
            num_scalar_prefetch=1,
            grid=grid,
            in_specs=in_specs,
            out_specs=out_specs,
            scratch_shapes=list(scratch),
        ),
        out_shape=out_shape,
        input_output_aliases=aliases or {},
        compiler_params=pltpu.CompilerParams(vmem_limit_bytes=max(vmem, 28) * MIB),
        cost_estimate=pl.CostEstimate(flops=1, bytes_accessed=1, transcendentals=0),
    )(scalars, *args)


def spec(shape, index):
    return pl.BlockSpec(shape, index)


def whole(array):
    zeros = (0,) * array.ndim
    return pl.BlockSpec(array.shape, lambda i, s: zeros)


def shape(dims, dtype):
    return jax.ShapeDtypeStruct(dims, dtype)


FF_ORDERS = (
    (("x", "y", "z0", "z1"), ("y", "z0", "x", "z1")),
    (("z0", "y", "x", "z1"), ("x", "y", "z1", "z0")),
    (("y", "z0", "x", "z1"), ("x", "y", "z0", "z1")),
)
QKV_ORDER = (("x", "z0", "z1"), ("z0", "z1", "x"))
PLAN = (
    ("ff", 0), ("wait", "early"), ("ff", 1), ("wait", "e0"), ("dw", 0), ("own",),
    ("wait", "branch_other"), ("wait", "e2"), ("wait", "g"), ("dw", 2), ("wait", "e1"), ("dw", 1),
    ("go", 0), ("far",), ("go", 2), ("joint",), ("go", 0), ("go", 2), ("go", 1), ("go", 0),
    ("go", 3), ("go", 2), ("back",), ("go", 3), ("go", 1), ("go", 0), ("wait", "bf"), ("go", 2),
    ("go", 0), ("go", 3), ("go", 2), ("go", 1), ("go", 3), ("go", 0), ("go", 3), ("go", 2),
    ("go", 1), ("wait", "n0"), ("go", 0), ("unpack", 0, 0), ("go", 3), ("go", 1), ("wait", "f0"),
    ("tokens",), ("unpack", 0, 1), ("go", 2), ("wait", "n2"), ("unpack", 2, 0), ("go", 1),
    ("go", 3), ("wait", "f2"), ("wait", "n3"), ("unpack", 2, 1), ("unpack", 3, 0), ("wait", "f3"),
    ("unpack", 3, 1), ("go", 1), ("wait", "n1"), ("unpack", 1, 0), ("wait", "f1"), ("unpack", 1, 1),
)
DP_BIT = {"c": 1, "x": 2, "z0": 4, "z1": 8}


def swap(array, first, second=None):
    second = second or first
    pairs = []
    for d in range(16):
        for b in range(2):
            bit = second if d & 1 else first
            to = (d, b ^ 1) if bit == "y" else (d ^ DP_BIT[bit], b)
            pairs.append((d * 2 + b, to[0] * 2 + to[1]))
    return lax.ppermute(array, AXES, pairs)


def place(order):
    d, b = lax.axis_index("dp"), lax.axis_index("blk")
    code = jnp.int32(0)
    for bit in order:
        value = b & 1 if bit == "y" else (d // DP_BIT[bit]) & 1
        code = code * 2 + value
    return code


def places(orders):
    core = lax.axis_index("dp") & 1
    first, second = place(orders[0]), place(orders[1])
    return jnp.where(core == 0, first, second), jnp.where(core == 0, second, first)


def add(a, b):
    return (a.astype(f32) + b.astype(f32)).astype(bf16)


class Order:
    def __init__(self):
        self.last = None

    def pin(self, *arrays):
        if self.last is None:
            return arrays
        return lax.optimization_barrier((*arrays, self.last))[:-1]

    def run(self, function, *arrays):
        result = function(*self.pin(*arrays))
        self.last = result[0] if isinstance(result, (tuple, list)) else result
        return result

    def swap(self, array, first, second=None):
        return swap(self.pin(array)[0], first, second)


def total(order, keep, send, links, widen=None):
    received = order.swap(send, *links[0])
    yield
    for link in links[1:-1]:
        half = keep.shape[0] // 2
        send = order.run(lambda k, r: add(k[half:], r[half:]), keep, received)
        coming = order.swap(send, *link)
        keep = order.run(lambda k, r: add(k[:half], r[:half]), keep, received)
        received = coming
        yield
    keep = order.run(add, keep, received)
    received = order.swap(keep, *links[-1])
    yield
    block = order.run(lambda k, r: add(k, r[::-1]), keep, received)
    if widen is not None:
        received = order.swap(block, "y")
        yield
        block = order.run(widen, block, received)
    back = [link for link in links[:-1] if link[0] != "c"][::-1]
    for link in back[:-1]:
        received = order.swap(block, *link)
        yield
        block = order.run(lambda k, r: jnp.concatenate([k, r], 0), block, received)
    far = order.swap(block, *back[-1])
    other = order.swap(block, "c")
    yield block, other
    far = order.run(lambda value: value, far)
    yield far, order.swap(far, "c")


def sine_and_cosine(angle):
    turns = jnp.floor(angle * (2.0 / math.pi) + 0.5)
    rest = angle - turns * 1.5703125
    rest = rest - turns * 4.837512969970703125e-4
    rest = rest - turns * 7.54978995489188e-8
    square = rest * rest
    sine = rest + rest * square * (
        -1.6666654611e-1 + square * (8.3321608736e-3 + square * -1.9515295891e-4)
    )
    cosine = (1.0 - 0.5 * square) + square * square * (
        4.166664568298827e-2 + square * (-1.388731625493765e-3 + square * 2.443315711809948e-5)
    )
    quarter = turns.astype(jnp.int32)
    odd = (quarter & 1) == 1
    sin = jnp.where(odd, cosine, sine)
    cos = jnp.where(odd, sine, cosine)
    return (
        jnp.where((quarter & 2) == 2, -sin, sin),
        jnp.where(((quarter + 1) & 2) == 2, -cos, cos),
    )


def position_kernel(s, visible, freqs, out):
    column = jnp.broadcast_to(visible[...].astype(f32), (8, visible.shape[1])).T[:, :1]
    sin, cos = sine_and_cosine(column * freqs[...])
    half = sin.shape[1]
    out[:, :half] = sin
    out[:, half:] = cos


def positions(scalars, visible, freqs):
    rows, width = visible.shape[1], 2 * freqs.shape[1]
    out = shape((rows, width), f32)
    return call(
        position_kernel, (1,), [whole(visible), whole(freqs)], whole(out), out, (visible, freqs), scalars, 16
    )


def ln_qkv_kernel(s, tok, pos, gain, w, normed, qkv, *resid):
    @pl.when(pl.program_id(0) == 0)
    def _():
        value = tok[...].astype(f32) + pos[...]
        if resid:
            resid[0][...] = value
        xhat, _ = normalize(value)
        normed[...] = (xhat * gain[...]).astype(bf16)

    qkv[...] = dot(normed[...], w[...]).astype(bf16)


def ln_qkv(scalars, far, tok, pos, gain, w):
    rows, width = tok.shape
    full = spec((rows, width), lambda i, s: (0, 0))
    parts = 2 if far else 3
    out_shape = [shape((rows, width), bf16), shape((rows, parts * width), bf16)]
    return call(
        ln_qkv_kernel,
        (parts,),
        [full, full, whole(gain), spec((width, width), lambda i, s: (0, i + far))],
        [full, spec((rows, width), lambda i, s: (0, i))] + [full] * (not far),
        out_shape + [shape((rows, width), f32)] * (not far),
        (tok, pos, gain, w),
        scalars,
        24,
    )


def far_query_kernel(s, normed, w, out):
    out[...] = dot(normed[...], w[...]).astype(bf16)


def far_query(scalars, normed, w):
    rows, width = normed.shape
    out = shape((rows, width // 2), bf16)
    return call(
        far_query_kernel,
        (1,),
        [whole(normed), spec((width, width // 2), lambda i, s: (0, s[1]))],
        whole(out),
        out,
        (normed, w),
        scalars,
        16,
    )


def head_masks(x):
    lane = lax.broadcasted_iota(jnp.int32, x.shape, 1)
    return jnp.where(lane < HD, x, 0.0).astype(bf16), jnp.where(lane >= HD, x, 0.0).astype(bf16)


def attn_kernel(group, s, q, k, v, *refs):
    rows = q.shape[0]
    later = len(refs) == 3
    if later:
        acc_in, stat_in, out = refs
    else:
        acc, stat = refs
    for pair in range(group):
        lanes = slice(pair * PAIR, (pair + 1) * PAIR)
        qs = jnp.concatenate(head_masks(q[:, lanes].astype(f32) * HD**-0.5), 0)
        scores = dot(k[:, lanes], qs, NT)
        top = jnp.max(scores, 0, keepdims=True)
        if later:
            before = stat_in[pair, 0:1]
            top = jnp.maximum(top, before)
        e = jnp.exp(scores - top)
        total = jnp.sum(e, 0, keepdims=True)
        vt = v[:, lanes].T
        low = e.astype(bf16)
        parts = [dot(vt[h * HD : (h + 1) * HD], low[:, h * rows : (h + 1) * rows]) for h in range(2)]
        if not later:
            acc[pair] = jnp.concatenate(parts, 0)
            stat[pair, 0:1] = top
            stat[pair, 1:2] = total
            continue
        shrink = jnp.exp(before - top)
        scale = 1.0 / (total + stat_in[pair, 1:2] * shrink)
        shrink = shrink * scale
        for h in range(2):
            at = slice(h * rows, (h + 1) * rows)
            held = acc_in[pair, h * HD : (h + 1) * HD]
            parts[h] = parts[h] * scale[:, at] + held * shrink[:, at]
        out[:, lanes] = jnp.concatenate(parts, 0).T.astype(bf16)


def attention(scalars, qkv, keys, *so_far):
    rows, width = qkv.shape[0], qkv.shape[1] // 3
    pairs = width // PAIR
    group = GROUP
    steps = pairs // group

    def column(part):
        return spec((rows, group * PAIR), lambda i, s: (0, part * steps + i))

    first = 0 if so_far else 1
    acc = spec((group, PAIR, rows), lambda i, s: (i, 0, 0))
    stat = spec((group, 8, 2 * rows), lambda i, s: (i, 0, 0))
    sums = [shape((pairs, PAIR, rows), f32), shape((pairs, 8, 2 * rows), f32)]
    return call(
        functools.partial(attn_kernel, group),
        (steps,),
        [column(0), column(first), column(first + 1)] + ([acc, stat] if so_far else []),
        spec((rows, group * PAIR), lambda i, s: (0, i)) if so_far else [acc, stat],
        shape((rows, width), bf16) if so_far else sums,
        (qkv, keys, keys) + so_far,
        scalars,
        28,
    )


def low_rows(packed):
    return packed.shape[0] - packed.shape[1]


def proj_kernel(s, att, att_half, w, resid, gain, resid2, normed2, packed):
    packed[low_rows(packed) :] = att_half[...]
    value = resid[...] + dot(att[...], w[...])
    resid2[...] = value
    xhat, _ = normalize(value)
    low = (xhat * gain[...]).astype(bf16)
    normed2[...] = low
    packed[: low_rows(packed)] = low.T


def project(scalars, att, w, resid, gain):
    rows, width = att.shape
    full = spec((rows, width), lambda i, s: (0, 0))
    half = spec((rows, width // 2), lambda i, s: (0, 1 - s[0]))
    return call(
        proj_kernel,
        (1,),
        [full, half, whole(w), full, whole(gain)],
        [
            full,
            full,
            spec((width + rows, rows), lambda i, s: (0, 0)),
        ],
        [
            shape((rows, width), f32),
            shape((rows, width), bf16),
            shape((width + rows, rows), bf16),
        ],
        (att, att, w, resid, gain),
        scalars,
        24,
    )


def gelu_and_slope(v):
    c = math.sqrt(2.0 / math.pi)
    square = v * v
    t = jnp.tanh(v * (c + (c * 0.044715) * square))
    act = 0.5 * v * (1.0 + t)
    slope = 0.5 * (1.0 + t) + (0.5 * v) * (1.0 - t * t) * (c + (3.0 * c * 0.044715) * square)
    return act, slope


def ff_kernel(count, s, normed, cot, up, down, *refs):
    step = pl.program_id(0)
    if count > 1:
        out_in, back_in, resid2, gain, w_own, w_other, *refs = refs
    pieces, refs = refs[: 2 * count], refs[2 * count :]
    if count > 1:
        out_low, grad2, branch, g_own, g_other, out, back = refs
    else:
        out, back = refs
    hidden = dot(normed[...], up[...])
    act, slope = gelu_and_slope(hidden)
    act = act.astype(bf16)
    grad = (dot(cot[...], down[...], NT) * slope).astype(bf16)
    out_part = dot(act, down[...])
    back_part = dot(grad, up[...], NT)

    @pl.when(step == 0)
    def _():
        out[...] = out_in[...] + out_part if count > 1 else out_part
        back[...] = back_in[...] + back_part if count > 1 else back_part

    @pl.when(step > 0)
    def _():
        out[...] += out_part
        back[...] += back_part

    for at, piece in enumerate(pieces):

        @pl.when(step == at)
        def _(piece=piece):
            piece[0] = act
            piece[1] = grad

    if count > 1:

        @pl.when(step == 2 * count - 1)
        def _():
            value = resid2[...]
            out_low[...] = (value + out[...]).astype(bf16)
            xhat, scale = normalize(value)
            g = cot[...].astype(f32) + norm_backward(back[...], gain[...], xhat, scale)
            grad2[...] = g
            low = g.astype(bf16)
            branch[...] = low
            g_other[...] = dot(low, w_other[...], NT).astype(bf16)
            g_own[...] = dot(low, w_own[...], NT).astype(bf16)


def ff_chunks(scalars, first, count, normed, cot, up, down, *more):
    rows, width = normed.shape
    half = width // 2
    wide = 512

    def column(i, s):
        return 2 * (first + i // 2) + (s[0] ^ (1 - (i & 1)))

    full = spec((rows, width), lambda i, s: (0, 0))
    part = spec((rows, half), lambda i, s: (0, 0))
    in_specs = [
        whole(normed),
        whole(cot),
        spec((width, wide), lambda i, s: (0, column(i, s))),
        spec((wide, width), lambda i, s: (column(i, s), 0)),
    ]
    out_specs = [spec((2, rows, wide), lambda i, s: (0, 0, 0))] * (2 * count)
    out_shape = [shape((2, rows, wide), bf16)] * (2 * count)
    scratch = []
    if count > 1:
        in_specs += [
            full,
            full,
            full,
            spec((1, width), lambda i, s: (0, 0)),
            spec((half, width), lambda i, s: (s[1], 0)),
            spec((half, width), lambda i, s: (1 - s[1], 0)),
        ]
        out_specs += [full, full, full, part, part]
        out_shape += [shape((rows, width), t) for t in (bf16, f32, bf16)]
        out_shape += [shape((rows, half), bf16)] * 2
        scratch = [pltpu.VMEM((rows, width), f32)] * 2
    else:
        out_specs += [full, full]
        out_shape += [shape((rows, width), f32)] * 2
    return call(
        functools.partial(ff_kernel, count),
        (2 * count,),
        in_specs,
        out_specs,
        out_shape,
        (normed, cot, up, down) + more,
        scalars,
        28,
        scratch,
    )


def ff_grads_kernel(at, s, act, act_o, grad, grad_o, cot, cot_o, nt, nt_o, *refs):
    keep, send = refs[-2:]
    step = pl.program_id(0)
    rows_both = jnp.concatenate([cot[...], cot_o[...]], 0)
    g_down = dot(jnp.concatenate([act[0], act_o[0]], 0), rows_both, TN).astype(bf16)
    grads = jnp.concatenate([grad[0], grad_o[0]], 0)
    g_up = dot(jnp.concatenate([nt[...], nt_o[...]], 1), grads).astype(bf16)
    g_proj = None
    if len(refs) > 2:
        att, att_o, branch, branch_o = refs[:4]
        both = jnp.concatenate([branch[...], branch_o[...]], 0)
        g_proj = dot(jnp.concatenate([att[...], att_o[...]], 0), both, TN).astype(bf16)
    code = s[at] & 7

    def store(target):
        rows_d = g_down.shape[0] // 8
        rows_u = g_up.shape[0] // 8
        half = g_up.shape[1] // 2
        for block in range(8):
            to = block ^ code
            target[to, :rows_d, :] = g_down[block * rows_d : (block + 1) * rows_d]
            part = g_up[block * rows_u : (block + 1) * rows_u]
            target[to, 32:64, : 2 * half] = part[:32]
            target[to, 32:48, 2 * half :] = part[32:, :half]
            target[to, 48:64, 2 * half :] = part[32:, half:]
            if g_proj is not None:
                part = g_proj[block * rows_u : (block + 1) * rows_u]
                wide = part.shape[1]
                target[to, 64:80, :wide] = part[:16]
                target[to, 64:80, wide:] = part[16:32]
                target[to, 80:, :wide] = part[32:]
                target[to, 80:, wide:] = jnp.zeros_like(part[32:])

    @pl.when(step == 0)
    def _():
        store(send)

    @pl.when(step == 1)
    def _():
        store(keep)


def ff_grads(scalars, chunk, mine, theirs, cot, cot_other, normed_t_other, normed_t, *proj):
    rows, width = cot.shape
    wide = mine.shape[2]
    at = 2 + 2 * chunk

    def side(i, s):
        return (1 - i) ^ (s[at] // 8)

    act = spec((1, rows, wide // 2), lambda i, s: (0, 0, side(i, s)))
    grad = spec((1, rows, wide), lambda i, s: (1, 0, 0))
    feature = spec((width // 2, rows), lambda i, s: (side(i, s), 0))
    in_specs = [act, act, grad, grad, whole(cot), whole(cot), feature, feature]
    if proj:
        half = width // 2
        column = spec((rows, half), lambda i, s: (0, side(i, s)))
        packed = spec((rows, half), lambda i, s: (2, 0))
        in_specs += [spec((rows, half), lambda i, s: (0, s[0])), packed, column, column]
    deep = 96 if proj else 64
    piece = spec((8, deep, width), lambda i, s: (0, 0, 0))
    return call(
        functools.partial(ff_grads_kernel, at),
        (2,),
        in_specs,
        [piece, piece],
        [shape((8, deep, width), bf16)] * 2,
        (mine, theirs, mine, theirs, cot, cot_other, normed_t, normed_t_other) + proj,
        scalars,
        28,
    )


def attn_back_kernel(group, s, q, g, k_o, k_f, v_o, v_f, *refs):
    gk_in, gv_in = refs[:2] if len(refs) == 5 else (None, None)
    gq, gk, gv = refs[-3:]
    rows = q.shape[0]
    for pair in range(group):
        lanes = slice(pair * PAIR, (pair + 1) * PAIR)
        k = jnp.concatenate([k_o[:, lanes], k_f[:, lanes]], 0)
        v = jnp.concatenate([v_o[:, lanes], v_f[:, lanes]], 0)
        kt = (k.astype(f32) * HD**-0.5).astype(bf16).T
        qs = jnp.concatenate(head_masks(q[:, lanes].astype(f32) * HD**-0.5), 0)
        gs = jnp.concatenate(head_masks(g[:, lanes].astype(f32)), 0)
        scores = dot(k, qs, NT)
        e = jnp.exp(scores - jnp.max(scores, 0, keepdims=True))
        probs = e * (1.0 / jnp.sum(e, 0, keepdims=True))
        grad_v = dot(probs.astype(bf16), gs)
        grad_p = dot(v, gs, NT)
        row = jnp.sum(probs * grad_p, 0, keepdims=True)
        grad_s = (probs * (grad_p - row)).astype(bf16)
        grad_k = dot(grad_s, qs)
        grad_q = [
            dot(kt[h * HD : (h + 1) * HD], grad_s[:, h * rows : (h + 1) * rows]) for h in range(2)
        ]
        if gk_in is not None:
            grad_k, grad_v = grad_k + gk_in[:, lanes], grad_v + gv_in[:, lanes]
        gq[:, lanes] = jnp.concatenate(grad_q, 0).T.astype(bf16)
        gk[:, lanes] = grad_k.astype(gk.dtype)
        gv[:, lanes] = grad_v.astype(gv.dtype)


def attention_back(scalars, query, grad, qkv, kv_far, *so_far):
    rows, width = qkv.shape[0], qkv.shape[1] // 3
    mine = width // PAIR // 2
    group = BACK_GROUP
    steps = mine // group

    def column(part):
        return spec((rows, group * PAIR), lambda i, s: (0, (2 * part + s[1]) * steps + i))

    block = spec((rows, group * PAIR), lambda i, s: (0, i))
    both = spec((2 * rows, group * PAIR), lambda i, s: (0, i))
    dtype = bf16 if so_far else f32
    return call(
        functools.partial(attn_back_kernel, group),
        (steps,),
        [block if so_far else column(0), block, column(1), column(0), column(2), column(1)]
        + [both] * len(so_far),
        [block, both, both],
        [shape((rows, width // 2), bf16)] + [shape((2 * rows, width // 2), dtype)] * 2,
        (query, grad, qkv, kv_far, qkv, kv_far) + so_far,
        scalars,
        BACK_LIMIT,
    )


def joint_kernel(s, n_own, n_far, gq_o, gq_f, gk, gv, keep, send):
    step = pl.program_id(0)
    gq = jnp.concatenate([gq_o[...], gq_f[...]], 0)
    n = jnp.concatenate([n_own[...], n_far[...]], 0)
    cols = gk.shape[1]

    def fill(target, code):
        tiles = [dot(n, g, TN).astype(bf16) for g in (gq, gk[...], gv[...])]
        rows = tiles[0].shape[0] // 8
        for block in range(8):
            at = block ^ code
            for i, tile in enumerate(tiles):
                part = tile[block * rows : (block + 1) * rows]
                target[at, :, i * cols : i * cols + part.shape[1]] = part

    @pl.when(step == 0)
    def _():
        fill(send, s[9])

    @pl.when(step == 1)
    def _():
        fill(keep, s[8])


def joint_grads(scalars, n_own, n_far, gq, gq_far, gk, gv):
    rows, width = n_own.shape
    half = width // 2
    feature = spec((rows, half), lambda i, s: (0, s[0] ^ (1 - i)))
    cols = 3 * half
    piece = spec((8, half // 8, cols), lambda i, s: (0, 0, 0))
    return call(
        joint_kernel,
        (2,),
        [feature, feature, whole(gq), whole(gq), whole(gk), whole(gv)],
        [piece, piece],
        [shape((8, half // 8, cols), bf16)] * 2,
        (n_own, n_far, gq, gq_far, gk, gv),
        scalars,
        28,
    )


def back_qkv_kernel(s, gq_o, gq_f, gk, gv, wq, wk, wv, own, far):
    rows = own.shape[0]

    def part(gq, at):
        total = dot(gq[...], wq[...], NT)
        total += dot(gk[pl.ds(at, rows)], wk[...], NT)
        return total + dot(gv[pl.ds(at, rows)], wv[...], NT)

    far[...] = part(gq_f, rows).astype(bf16)
    own[...] = part(gq_o, 0)


def back_qkv(scalars, gq, gq_far, gk, gv, w):
    rows, half = gq.shape
    width = 2 * half

    def column(part):
        return spec((width, half), lambda i, s: (0, 2 * part + s[1]))

    full = spec((rows, width), lambda i, s: (0, 0))
    return call(
        back_qkv_kernel,
        (1,),
        [whole(gq), whole(gq), whole(gk), whole(gv), column(0), column(1), column(2)],
        [full, full],
        [shape((rows, width), f32), shape((rows, width), bf16)],
        (gq, gq_far, gk, gv, w, w, w),
        scalars,
        28,
    )


def last_kernel(s, own, far, resid, gain, grad2, out):
    xhat, scale = normalize(resid[...])
    grad = own[...] + far[...].astype(f32)
    out[...] = grad2[...] + norm_backward(grad, gain[...], xhat, scale)


def token_grad(scalars, own, far, resid, gain, grad2):
    args = (own, far, resid, gain, grad2)
    return call(
        last_kernel,
        (1,),
        [whole(a) for a in args],
        whole(own),
        shape(own.shape, f32),
        args,
        scalars,
        24,
    )


def row_sums(values):
    folded = sum(values[:, at : at + 128] for at in range(0, values.shape[1], 128))
    return lax.dot_general(
        jnp.ones((8, 128), f32),
        folded,
        (NT, ((), ())),
        precision=lax.Precision.HIGHEST,
        preferred_element_type=f32,
    )


def unpack_ff_kernel(at, last, s, own, other, w, gain_in, *refs):
    gain, down, up, *proj = refs[-4:] if last else refs[-3:]
    step = pl.program_id(0)

    def unpack(source, code):
        for block in range(8):
            to = block ^ (code & 7)
            down[pl.ds(pl.multiple_of(to * 32, 32), 32), :] = source[block, :32, :].astype(f32)
            row = pl.multiple_of(to * 48, 16)
            up[pl.ds(row, 32), :] = source[block, 32:64, :512].astype(f32)
            up[pl.ds(row + 32, 16), :256] = source[block, 32:48, 512:].astype(f32)
            up[pl.ds(row + 32, 16), 256:] = source[block, 48:64, 512:].astype(f32)
            if last:
                wide = source.shape[2] // 2
                proj[0][pl.ds(row, 16), :] = source[block, 64:80, :wide].astype(f32)
                proj[0][pl.ds(row + 16, 16), :] = source[block, 64:80, wide:].astype(f32)
                proj[0][pl.ds(row + 32, 16), :] = source[block, 80:, :wide].astype(f32)

    @pl.when(step == 0)
    def _():
        unpack(own, s[at])

    @pl.when(step == 1)
    def _():
        unpack(other, s[at + 1])

    gain[0, 0] = gain_in[0, 0] + row_sums(up[...] * w[...].astype(f32))


def unpack_ff(scalars, chunk, far, own, other, w, so_far):
    width, hidden = w.shape
    at = 2 + 2 * chunk
    last = own.shape[1] > 64

    def side(i, s):
        return (s[at + i] // 8) ^ far

    def half(i, s):
        return 2 * chunk + (s[0] ^ i)

    any_spec = pl.BlockSpec(memory_space=pl.ANY)
    column = spec((width // 2, 512), lambda i, s: (side(i, s), half(i, s)))
    gain = spec((1, 1, 8, width // 2), lambda i, s: (i, side(i, s), 0, 0))
    out_specs = [gain, spec((256, width), lambda i, s: (2 * half(i, s) + side(i, s), 0)), column]
    out_shape = [shape((2, 2, 8, width // 2), f32), shape((hidden, width), f32), shape((width, hidden), f32)]
    if last:
        out_specs.append(spec((width // 2, width // 2), lambda i, s: (s[0] ^ i, side(i, s))))
        out_shape.append(shape((width, width), f32))
    in_specs = [whole(own), whole(other), column]
    in_specs += [gain, any_spec, any_spec, any_spec][: len(so_far)]
    return call(
        functools.partial(unpack_ff_kernel, at, last),
        (2,),
        in_specs,
        out_specs,
        out_shape,
        (own, other, w) + tuple(so_far),
        scalars,
        28,
        aliases={4 + i: i for i in range(len(so_far))},
    )


def unpack_qkv_kernel(s, own, other, w, *refs):
    joint, gain = refs[-2:]
    step = pl.program_id(0)
    mine = s[1]

    def unpack(source, code):
        half = source.shape[2] // 6

        def place_columns(first):
            for block in range(2):
                rows = pl.ds(pl.multiple_of((block ^ (code & 1)) * 48, 16), 48)
                for part in range(3):
                    for side in range(2):
                        column = 2 * half * part + half * (first ^ side)
                        value = source[block, :, (3 * side + part) * half : (3 * side + part + 1) * half]
                        joint[rows, column : column + half] = value.astype(f32)

        for first in range(2):
            pl.when(mine == first)(functools.partial(place_columns, first))

    @pl.when(step < 2)
    def _():
        unpack(own, s[8])

    @pl.when(step >= 2)
    def _():
        unpack(other, s[9])

    gain[0] = row_sums(joint[...] * w[...].astype(f32))


def unpack_qkv(scalars, far, own, other, w, so_far):
    width = w.shape[0]

    def row(i, s):
        code = s[8 + i // 2]
        return 4 * (s[0] ^ (i // 2)) + 2 * ((code // 4) ^ far) + ((i & 1) ^ ((code // 2) & 1))

    def blocks(mine):
        return spec((2,) + own.shape[1:], lambda i, s: (jnp.clip(i - 2 * mine, 0, 1), 0, 0))

    any_spec = pl.BlockSpec(memory_space=pl.ANY)
    rows = spec((width // 8, 3 * width), lambda i, s: (row(i, s), 0))
    return call(
        unpack_qkv_kernel,
        (4,),
        [blocks(0), blocks(1), rows] + [any_spec] * len(so_far),
        [rows, spec((1, 8, width // 8), lambda i, s: (row(i, s), 0, 0))],
        [shape((width, 3 * width), f32), shape((8, 8, width // 8), f32)],
        (own, other, w) + tuple(so_far),
        scalars,
        28,
        aliases={4 + i: i for i in range(len(so_far))},
    )


def fast(tokens, visible, ln1_gain, w_qkv, w_proj, ln2_gain, w_up, w_down, d_out):
    tok, cot = tokens[0], d_out[0]
    rows, width = tok.shape
    gain1, gain2 = ln1_gain[None], ln2_gain[None]
    scalars = [lax.axis_index("dp") & 1, lax.axis_index("blk")]
    for orders in FF_ORDERS + (QKV_ORDER,):
        scalars.extend(places(orders))
    scalars = jnp.stack([jnp.int32(v) for v in scalars])

    order = Order()
    run = order.run
    vis_far = swap(visible, "y")
    tok_far = swap(tok, "y")
    half = width // 2
    freqs = jnp.exp(jnp.arange(half, dtype=f32) * (-math.log(10000.0) / half))[None]
    pos = run(functools.partial(positions, scalars), visible, freqs)
    normed1, qkv, resid = run(functools.partial(ln_qkv, scalars, False), tok, pos, gain1, w_qkv)
    sums = run(functools.partial(attention, scalars), qkv, qkv)
    pos_far = run(functools.partial(positions, scalars), vis_far, freqs)
    normed1_far, kv_far = run(functools.partial(ln_qkv, scalars, True), tok_far, pos_far, gain1, w_qkv)
    attended = run(functools.partial(attention, scalars), qkv, kv_far, *sums)
    resid2, normed2, packed = run(
        functools.partial(project, scalars), attended, w_proj, resid, gain2
    )
    early = tuple(order.swap(array, "c") for array in (cot, packed))

    streams, blocks, values = {}, {}, {"early": early}
    ff, proj, joint = (jnp.zeros((2, 2, 8, width // 2), f32),), (), ()

    def feed_forward(first):
        if first == 0:
            send, keep, *values["sums"] = run(
                functools.partial(ff_chunks, scalars, 0, 1), normed2, cot, w_up, w_down
            )
            values["act", 0], values["e0"] = keep, order.swap(send, "c")
            return
        more = (*values["sums"], resid2, gain2, w_proj, w_proj)
        send1, keep1, send2, keep2, out, grad2, branch, g_own, g_other = run(
            functools.partial(ff_chunks, scalars, 1, 2), normed2, cot, w_up, w_down, *more
        )
        values["act", 1], values["e1"] = keep1, order.swap(send1, "c")
        values["act", 2], values["e2"] = keep2, order.swap(send2, "c")
        values["branch"], values["branch_other"] = branch, order.swap(branch, "c")
        values["g"] = order.swap(g_other, "y")
        values.update(out=out, grad2=grad2, own=g_own)

    def weight_grads(chunk):
        early = (*values["early"], packed)
        more = ()
        if chunk == 2:
            more = (attended, values["early"][1], values["branch"], values["branch_other"])
        keep, send = run(
            functools.partial(ff_grads, scalars, chunk),
            values["act", chunk], values["e%d" % chunk], cot, *early, *more,
        )
        streams[chunk] = total(order, keep, send, list(zip(*FF_ORDERS[chunk])))
        advance(chunk)

    def advance(chunk):
        pair = next(streams[chunk])
        if pair is not None:
            blocks.setdefault(chunk, []).append(pair)

    def wait(key):
        if key[0] in "nf" and key[1:].isdigit():
            chunk, far = int(key[1:]), int(key[0] == "f")
            own, other = blocks[chunk][far]
            blocks[chunk][far] = own, run(lambda value: value, other)
            return
        value = values[key]
        values[key] = run(lambda *v: v if isinstance(value, tuple) else v[0], *(value if isinstance(value, tuple) else (value,)))

    def own_queries():
        values["attn"] = run(functools.partial(attention_back, scalars), qkv, values["own"], qkv, kv_far)

    def far_queries():
        gq, *sums = values["attn"]
        values["q"] = run(functools.partial(far_query, scalars), normed1_far, w_qkv)
        back = run(functools.partial(attention_back, scalars), values["q"], values["g"], qkv, kv_far, *sums)
        values["attn"] = (gq, *back)

    def joint_weights():
        keep, send = run(functools.partial(joint_grads, scalars), normed1, normed1_far, *values["attn"])
        links = [("c", "c")] + list(zip(*QKV_ORDER))
        streams[3] = total(order, keep, send, links, lambda a, b: jnp.concatenate([a, b], -1))
        advance(3)

    def back_joint():
        own, far = run(functools.partial(back_qkv, scalars), *values["attn"], w_qkv)
        values["norm"], values["bf"] = own, order.swap(far, "y")

    def finish_tokens():
        args = (values["norm"], values["bf"], resid, gain1, values["grad2"])
        values["tokens"] = run(functools.partial(token_grad, scalars), *args)

    def unpack(chunk, far):
        nonlocal ff, proj, joint
        own, other = blocks[chunk][far]
        if chunk == 3:
            joint = run(lambda a, b, *f: unpack_qkv(scalars, far, a, b, w_qkv, f), own, other, *joint)
            return
        so_far = ff + proj if chunk == 2 else ff
        weight = w_hbm if (chunk, far) == final else w_up
        result = tuple(
            run(lambda a, b, *f: unpack_ff(scalars, chunk, far, a, b, weight, f), own, other, *so_far)
        )
        ff, proj = result[:3], result[3:] or proj

    w_hbm = pltpu.with_memory_space_constraint(w_up, pltpu.HBM)
    final = [step[1:] for step in PLAN if step[0] == "unpack" and step[1] != 3][-1]
    steps = {
        "ff": feed_forward,
        "dw": weight_grads,
        "go": advance,
        "wait": wait,
        "own": own_queries,
        "far": far_queries,
        "joint": joint_weights,
        "back": back_joint,
        "tokens": finish_tokens,
        "unpack": unpack,
    }
    for name, *args in PLAN:
        steps[name](*args)
    sums2, d_down, d_up = ff
    d_qkv, sums1 = joint
    out, d_tokens, d_proj = values["out"], values["tokens"], proj[0]
    d_gain1 = sums1[:, 0].reshape(-1) / ln1_gain
    d_gain2 = (sums2[0, :, 0] + sums2[1, :, 0]).reshape(-1) / ln2_gain
    return out[None], d_tokens[None], d_gain1, d_qkv, d_proj, d_gain2, d_up, d_down


def layer_norm(values, gain):
    center = values - jnp.mean(values, -1, keepdims=True)
    spread = jnp.mean(center * center, -1, keepdims=True)
    return center * lax.rsqrt(spread + epsilon) * gain


def outer_product(left, right):
    return lax.dot_general(
        left, right, (((0,), (0,)), ((), ())), preferred_element_type=jnp.float32
    )


def times_transposed(left, weight):
    return lax.dot_general(
        left, weight, (((1,), (1,)), ((), ())), preferred_element_type=jnp.float32
    )


def split_blocks(keys, values):
    count = keys.shape[0]
    size = math.gcd(count, 512)
    shape = (count // size, size, HEADS, HD)
    return (keys.reshape(shape), values.reshape(shape))


def general(tokens, visible, ln1_gain, w_qkv, w_proj, ln2_gain, w_up, w_down, d_out):
    rows = tokens.shape[1]
    width = tokens.shape[2]
    factor = HD ** (-0.5)
    resid = tokens[0].astype(jnp.float32) + position_table(visible[0], width)
    normed1, back_one = jax.vjp(layer_norm, resid, ln1_gain)
    normed1 = normed1.astype(jnp.bfloat16)
    qkv = jnp.dot(normed1, w_qkv, preferred_element_type=jnp.float32).astype(jnp.bfloat16)
    query = qkv[:, :width]
    keys = qkv[:, width : 2 * width]
    values = qkv[:, 2 * width :]
    query_heads = query.reshape(rows, HEADS, HD)
    initial = (
        jnp.full((HEADS, rows), -1e30, jnp.float32),
        jnp.zeros((HEADS, rows), jnp.float32),
        jnp.zeros((HEADS, rows, HD), jnp.float32),
    )
    key_blocks, value_blocks = split_blocks(
        lax.all_gather(keys, "blk", axis=0, tiled=True),
        lax.all_gather(values, "blk", axis=0, tiled=True),
    )

    def one_block(state, block):
        running, total, accum = state
        block_keys, block_values = block
        scores = (
            jnp.einsum("qhd,khd->hqk", query_heads, block_keys, preferred_element_type=jnp.float32)
            * factor
        )
        top = jnp.maximum(running, jnp.max(scores, -1))
        weights = jnp.exp(scores - top[..., None])
        shrink = jnp.exp(running - top)
        total = total * shrink + jnp.sum(weights, -1)
        accum = accum * shrink[..., None] + jnp.einsum(
            "hqk,khd->hqd",
            weights.astype(jnp.bfloat16),
            block_values,
            preferred_element_type=jnp.float32,
        )
        return ((top, total, accum), None)

    running, total, accum = lax.scan(one_block, initial, (key_blocks, value_blocks))[0]
    log_total = running + jnp.log(total)
    attended = (accum / total[..., None]).transpose(1, 0, 2).reshape(rows, width)
    attended_low = attended.astype(jnp.bfloat16)
    resid2 = resid + jnp.dot(attended_low, w_proj, preferred_element_type=jnp.float32)
    normed2, back_two = jax.vjp(layer_norm, resid2, ln2_gain)
    normed2 = normed2.astype(jnp.bfloat16)
    hidden = jnp.dot(normed2, w_up, preferred_element_type=jnp.float32)
    activated, back_gelu = jax.vjp(jax.nn.gelu, hidden)
    activated = activated.astype(jnp.bfloat16)
    result = resid2 + jnp.dot(activated, w_down, preferred_element_type=jnp.float32)
    cotangent = d_out[0]
    grad_down = outer_product(activated, cotangent)
    (grad_hidden,) = back_gelu(times_transposed(cotangent, w_down))
    grad_hidden = grad_hidden.astype(jnp.bfloat16)
    grad_up = outer_product(normed2, grad_hidden)
    grad_resid2, grad_gain2 = back_two(times_transposed(grad_hidden, w_up))
    grad_resid2 = grad_resid2 + cotangent.astype(jnp.float32)
    grad_branch = grad_resid2.astype(jnp.bfloat16)
    grad_proj = outer_product(attended_low, grad_branch)
    grad_attended = times_transposed(grad_branch, w_proj).astype(jnp.bfloat16)
    correction = (grad_attended.astype(jnp.float32) * attended).reshape(rows, HEADS, HD)
    correction = jnp.sum(correction, -1).T
    grad_heads = grad_attended.reshape(rows, HEADS, HD)
    all_keys, all_values = (
        lax.all_gather(keys, "blk", axis=0, tiled=True),
        lax.all_gather(values, "blk", axis=0, tiled=True),
    )
    full_rows = all_keys.shape[0]
    key_blocks, value_blocks = split_blocks(all_keys, all_values)

    def back_block(grad_query, block):
        block_keys, block_values = block
        scores = (
            jnp.einsum("qhd,khd->hqk", query_heads, block_keys, preferred_element_type=jnp.float32)
            * factor
        )
        probs = jnp.exp(scores - log_total[..., None])
        grad_value = jnp.einsum(
            "hqk,qhd->khd",
            probs.astype(jnp.bfloat16),
            grad_heads,
            preferred_element_type=jnp.float32,
        )
        grad_probs = jnp.einsum(
            "qhd,khd->hqk", grad_heads, block_values, preferred_element_type=jnp.float32
        )
        grad_scores = (probs * (grad_probs - correction[..., None])).astype(jnp.bfloat16)
        grad_query = grad_query + jnp.einsum(
            "hqk,khd->qhd", grad_scores, block_keys, preferred_element_type=jnp.float32
        )
        grad_key = (
            jnp.einsum("hqk,qhd->khd", grad_scores, query_heads, preferred_element_type=jnp.float32)
            * factor
        )
        return (grad_query, (grad_key, grad_value))

    grad_query, (key_parts, value_parts) = lax.scan(
        back_block, jnp.zeros((rows, HEADS, HD), jnp.float32), (key_blocks, value_blocks)
    )
    grad_query = (grad_query * factor).reshape(rows, width)
    grad_keys, grad_values = (
        lax.psum_scatter(
            key_parts.reshape(full_rows, width).astype(jnp.bfloat16),
            "blk",
            scatter_dimension=0,
            tiled=True,
        ).astype(jnp.float32),
        lax.psum_scatter(
            value_parts.reshape(full_rows, width).astype(jnp.bfloat16),
            "blk",
            scatter_dimension=0,
            tiled=True,
        ).astype(jnp.float32),
    )
    grad_qkv = jnp.concatenate([grad_query, grad_keys, grad_values], 1).astype(jnp.bfloat16)
    grad_joint = outer_product(normed1, grad_qkv)
    grad_resid, grad_gain1 = back_one(times_transposed(grad_qkv, w_qkv))
    input_grad = grad_resid2 + grad_resid
    flats = (
        grad_joint.reshape(-1),
        grad_proj.reshape(-1),
        grad_up.reshape(-1),
        grad_down.reshape(-1),
    )
    shares = (
        lax.psum_scatter(flats[0], ("dp", "blk"), scatter_dimension=0, tiled=True),
        lax.psum_scatter(flats[1], ("dp", "blk"), scatter_dimension=0, tiled=True),
        lax.psum_scatter(flats[2], ("dp", "blk"), scatter_dimension=0, tiled=True),
        lax.psum_scatter(flats[3], ("dp", "blk"), scatter_dimension=0, tiled=True),
    )
    summed = (
        lax.all_gather(shares[0].astype(jnp.bfloat16), ("dp", "blk"), axis=0, tiled=True).astype(
            jnp.float32
        ),
        lax.all_gather(shares[1].astype(jnp.bfloat16), ("dp", "blk"), axis=0, tiled=True).astype(
            jnp.float32
        ),
        lax.all_gather(shares[2].astype(jnp.bfloat16), ("dp", "blk"), axis=0, tiled=True).astype(
            jnp.float32
        ),
        lax.all_gather(shares[3].astype(jnp.bfloat16), ("dp", "blk"), axis=0, tiled=True).astype(
            jnp.float32
        ),
    )
    gain_one, gain_two = lax.psum((grad_gain1, grad_gain2), ("dp", "blk"))
    return (
        result.astype(jnp.bfloat16)[None],
        input_grad[None],
        gain_one,
        summed[0].reshape(w_qkv.shape),
        summed[1].reshape(w_proj.shape),
        gain_two,
        summed[2].reshape(w_up.shape),
        summed[3].reshape(w_down.shape),
    )


def solution(mesh):
    split = mesh.shape["dp"] == 16 and mesh.shape["blk"] == 2

    def local(tokens, *others):
        fits = split and 2 * tokens.shape[1] == tokens.shape[2]
        return (fast if fits else general)(tokens, *others)

    return jax.shard_map(
        local,
        mesh=mesh,
        in_specs=(
            P("dp", "blk", None),
            P("dp", "blk"),
            P(),
            P(),
            P(),
            P(),
            P(),
            P(),
            P("dp", "blk", None),
        ),
        out_specs=(P("dp", "blk", None), P("dp", "blk", None), P(), P(), P(), P(), P(), P()),
        check_vma=False,
    )
```

```python
import functools
import math

import jax
import jax.numpy as jnp
from jax import lax
from jax.experimental import pallas as pl
from jax.experimental.pallas import tpu as pltpu
from jax.sharding import PartitionSpec as P

HEADS = 12
HD = 64
PAIR = 2 * HD
GROUP = 2
BACK_GROUP = 1
BACK_LIMIT = 28
epsilon = 1e-06
f32 = jnp.float32
bf16 = jnp.bfloat16
NN = ((1,), (0,))
NT = ((1,), (1,))
TN = ((0,), (0,))
AXES = ("dp", "blk")
MIB = 1 << 20


def dot(left, right, dims=NN):
    return lax.dot_general(left, right, (dims, ((), ())), preferred_element_type=f32)


def position_table(visible, width):
    half = width // 2
    column = jnp.arange(half, dtype=f32)
    freqs = jnp.exp(column * (-math.log(10000.0) / half))
    angles = visible.astype(f32)[..., None] * freqs
    return jnp.concatenate([jnp.sin(angles), jnp.cos(angles)], -1)


def normalize(values):
    center = values - jnp.mean(values, -1, keepdims=True)
    spread = jnp.mean(center * center, -1, keepdims=True)
    scale = lax.rsqrt(spread + epsilon)
    return center * scale, scale


def norm_backward(grad, gain, xhat, scale):
    e = grad * gain
    return scale * (
        e - jnp.mean(e, -1, keepdims=True) - xhat * jnp.mean(e * xhat, -1, keepdims=True)
    )


def call(kernel, grid, in_specs, out_specs, out_shape, args, scalars, vmem, scratch=(), aliases=None):
    return pl.pallas_call(
        kernel,
        grid_spec=pltpu.PrefetchScalarGridSpec(
            num_scalar_prefetch=1,
            grid=grid,
            in_specs=in_specs,
            out_specs=out_specs,
            scratch_shapes=list(scratch),
        ),
        out_shape=out_shape,
        input_output_aliases=aliases or {},
        compiler_params=pltpu.CompilerParams(vmem_limit_bytes=max(vmem, 28) * MIB),
        cost_estimate=pl.CostEstimate(flops=1, bytes_accessed=1, transcendentals=0),
    )(scalars, *args)


def spec(shape, index):
    return pl.BlockSpec(shape, index)


def whole(array):
    zeros = (0,) * array.ndim
    return pl.BlockSpec(array.shape, lambda i, s: zeros)


def shape(dims, dtype):
    return jax.ShapeDtypeStruct(dims, dtype)


FF_ORDERS = (
    (("x", "y", "z0", "z1"), ("y", "z0", "x", "z1")),
    (("z0", "y", "x", "z1"), ("x", "y", "z1", "z0")),
    (("y", "z0", "x", "z1"), ("x", "y", "z0", "z1")),
)
QKV_ORDER = (("x", "z0", "z1"), ("z0", "z1", "x"))
PLAN = (
    ("ff", 0), ("wait", "early"), ("ff", 1), ("wait", "e0"), ("dw", 0), ("own",),
    ("wait", "branch_other"), ("wait", "e2"), ("wait", "g"), ("dw", 2), ("wait", "e1"), ("dw", 1),
    ("go", 0), ("far",), ("go", 2), ("joint",), ("go", 0), ("go", 2), ("go", 1), ("go", 0),
    ("go", 3), ("go", 2), ("back",), ("go", 3), ("go", 1), ("go", 0), ("wait", "bf"), ("go", 2),
    ("go", 0), ("go", 3), ("go", 2), ("go", 1), ("go", 3), ("go", 0), ("go", 3), ("go", 2),
    ("go", 1), ("wait", "n0"), ("go", 0), ("unpack", 0, 0), ("go", 3), ("go", 1), ("wait", "f0"),
    ("tokens",), ("unpack", 0, 1), ("go", 2), ("wait", "n2"), ("unpack", 2, 0), ("go", 1),
    ("go", 3), ("wait", "f2"), ("wait", "n3"), ("unpack", 2, 1), ("unpack", 3, 0), ("wait", "f3"),
    ("unpack", 3, 1), ("go", 1), ("wait", "n1"), ("unpack", 1, 0), ("wait", "f1"), ("unpack", 1, 1),
)
DP_BIT = {"c": 1, "x": 2, "z0": 4, "z1": 8}


def swap(array, first, second=None):
    second = second or first
    pairs = []
    for d in range(16):
        for b in range(2):
            bit = second if d & 1 else first
            to = (d, b ^ 1) if bit == "y" else (d ^ DP_BIT[bit], b)
            pairs.append((d * 2 + b, to[0] * 2 + to[1]))
    return lax.ppermute(array, AXES, pairs)


def place(order):
    d, b = lax.axis_index("dp"), lax.axis_index("blk")
    code = jnp.int32(0)
    for bit in order:
        value = b & 1 if bit == "y" else (d // DP_BIT[bit]) & 1
        code = code * 2 + value
    return code


def places(orders):
    core = lax.axis_index("dp") & 1
    first, second = place(orders[0]), place(orders[1])
    return jnp.where(core == 0, first, second), jnp.where(core == 0, second, first)


def add(a, b):
    return (a.astype(f32) + b.astype(f32)).astype(bf16)


class Order:
    def __init__(self):
        self.last = None

    def pin(self, *arrays):
        if self.last is None:
            return arrays
        return lax.optimization_barrier((*arrays, self.last))[:-1]

    def run(self, function, *arrays):
        result = function(*self.pin(*arrays))
        self.last = result[0] if isinstance(result, (tuple, list)) else result
        return result

    def swap(self, array, first, second=None):
        return swap(self.pin(array)[0], first, second)


def total(order, keep, send, links, widen=None):
    received = order.swap(send, *links[0])
    yield
    for link in links[1:-1]:
        half = keep.shape[0] // 2
        send = order.run(lambda k, r: add(k[half:], r[half:]), keep, received)
        coming = order.swap(send, *link)
        keep = order.run(lambda k, r: add(k[:half], r[:half]), keep, received)
        received = coming
        yield
    keep = order.run(add, keep, received)
    received = order.swap(keep, *links[-1])
    yield
    block = order.run(lambda k, r: add(k, r[::-1]), keep, received)
    if widen is not None:
        received = order.swap(block, "y")
        yield
        block = order.run(widen, block, received)
    back = [link for link in links[:-1] if link[0] != "c"][::-1]
    for link in back[:-1]:
        received = order.swap(block, *link)
        yield
        block = order.run(lambda k, r: jnp.concatenate([k, r], 0), block, received)
    far = order.swap(block, *back[-1])
    other = order.swap(block, "c")
    yield block, other
    far = order.run(lambda value: value, far)
    yield far, order.swap(far, "c")


def sine_and_cosine(angle):
    turns = jnp.floor(angle * (2.0 / math.pi) + 0.5)
    rest = angle - turns * 1.5703125
    rest = rest - turns * 4.837512969970703125e-4
    rest = rest - turns * 7.54978995489188e-8
    square = rest * rest
    sine = rest + rest * square * (
        -1.6666654611e-1 + square * (8.3321608736e-3 + square * -1.9515295891e-4)
    )
    cosine = (1.0 - 0.5 * square) + square * square * (
        4.166664568298827e-2 + square * (-1.388731625493765e-3 + square * 2.443315711809948e-5)
    )
    quarter = turns.astype(jnp.int32)
    odd = (quarter & 1) == 1
    sin = jnp.where(odd, cosine, sine)
    cos = jnp.where(odd, sine, cosine)
    return (
        jnp.where((quarter & 2) == 2, -sin, sin),
        jnp.where(((quarter + 1) & 2) == 2, -cos, cos),
    )


def position_kernel(s, visible, freqs, out):
    column = jnp.broadcast_to(visible[...].astype(f32), (8, visible.shape[1])).T[:, :1]
    sin, cos = sine_and_cosine(column * freqs[...])
    half = sin.shape[1]
    out[:, :half] = sin
    out[:, half:] = cos


def positions(scalars, visible, freqs):
    rows, width = visible.shape[1], 2 * freqs.shape[1]
    out = shape((rows, width), f32)
    return call(
        position_kernel, (1,), [whole(visible), whole(freqs)], whole(out), out, (visible, freqs), scalars, 16
    )


def ln_qkv_kernel(s, tok, pos, gain, w, normed, qkv, *resid):
    @pl.when(pl.program_id(0) == 0)
    def _():
        value = tok[...].astype(f32) + pos[...]
        if resid:
            resid[0][...] = value
        xhat, _ = normalize(value)
        normed[...] = (xhat * gain[...]).astype(bf16)

    qkv[...] = dot(normed[...], w[...]).astype(bf16)


def ln_qkv(scalars, far, tok, pos, gain, w):
    rows, width = tok.shape
    full = spec((rows, width), lambda i, s: (0, 0))
    parts = 2 if far else 3
    out_shape = [shape((rows, width), bf16), shape((rows, parts * width), bf16)]
    return call(
        ln_qkv_kernel,
        (parts,),
        [full, full, whole(gain), spec((width, width), lambda i, s: (0, i + far))],
        [full, spec((rows, width), lambda i, s: (0, i))] + [full] * (not far),
        out_shape + [shape((rows, width), f32)] * (not far),
        (tok, pos, gain, w),
        scalars,
        24,
    )


def far_query_kernel(s, normed, w, out):
    out[...] = dot(normed[...], w[...]).astype(bf16)


def far_query(scalars, normed, w):
    rows, width = normed.shape
    out = shape((rows, width // 2), bf16)
    return call(
        far_query_kernel,
        (1,),
        [whole(normed), spec((width, width // 2), lambda i, s: (0, s[1]))],
        whole(out),
        out,
        (normed, w),
        scalars,
        16,
    )


def head_masks(x):
    lane = lax.broadcasted_iota(jnp.int32, x.shape, 1)
    return jnp.where(lane < HD, x, 0.0).astype(bf16), jnp.where(lane >= HD, x, 0.0).astype(bf16)


def attn_kernel(group, s, q, k, v, *refs):
    rows = q.shape[0]
    later = len(refs) == 3
    if later:
        acc_in, stat_in, out = refs
    else:
        acc, stat = refs
    for pair in range(group):
        lanes = slice(pair * PAIR, (pair + 1) * PAIR)
        qs = jnp.concatenate(head_masks(q[:, lanes].astype(f32) * HD**-0.5), 0)
        scores = dot(k[:, lanes], qs, NT)
        top = jnp.max(scores, 0, keepdims=True)
        if later:
            before = stat_in[pair, 0:1]
            top = jnp.maximum(top, before)
        e = jnp.exp(scores - top)
        total = jnp.sum(e, 0, keepdims=True)
        vt = v[:, lanes].T
        low = e.astype(bf16)
        parts = [dot(vt[h * HD : (h + 1) * HD], low[:, h * rows : (h + 1) * rows]) for h in range(2)]
        if not later:
            acc[pair] = jnp.concatenate(parts, 0)
            stat[pair, 0:1] = top
            stat[pair, 1:2] = total
            continue
        shrink = jnp.exp(before - top)
        scale = 1.0 / (total + stat_in[pair, 1:2] * shrink)
        shrink = shrink * scale
        for h in range(2):
            at = slice(h * rows, (h + 1) * rows)
            held = acc_in[pair, h * HD : (h + 1) * HD]
            parts[h] = parts[h] * scale[:, at] + held * shrink[:, at]
        out[:, lanes] = jnp.concatenate(parts, 0).T.astype(bf16)


def attention(scalars, qkv, keys, *so_far):
    rows, width = qkv.shape[0], qkv.shape[1] // 3
    pairs = width // PAIR
    group = GROUP
    steps = pairs // group

    def column(part):
        return spec((rows, group * PAIR), lambda i, s: (0, part * steps + i))

    first = 0 if so_far else 1
    acc = spec((group, PAIR, rows), lambda i, s: (i, 0, 0))
    stat = spec((group, 8, 2 * rows), lambda i, s: (i, 0, 0))
    sums = [shape((pairs, PAIR, rows), f32), shape((pairs, 8, 2 * rows), f32)]
    return call(
        functools.partial(attn_kernel, group),
        (steps,),
        [column(0), column(first), column(first + 1)] + ([acc, stat] if so_far else []),
        spec((rows, group * PAIR), lambda i, s: (0, i)) if so_far else [acc, stat],
        shape((rows, width), bf16) if so_far else sums,
        (qkv, keys, keys) + so_far,
        scalars,
        28,
    )


def low_rows(packed):
    return packed.shape[0] - packed.shape[1]


def proj_kernel(s, att, att_half, w, resid, gain, resid2, normed2, packed):
    packed[low_rows(packed) :] = att_half[...]
    value = resid[...] + dot(att[...], w[...])
    resid2[...] = value
    xhat, _ = normalize(value)
    low = (xhat * gain[...]).astype(bf16)
    normed2[...] = low
    packed[: low_rows(packed)] = low.T


def project(scalars, att, w, resid, gain):
    rows, width = att.shape
    full = spec((rows, width), lambda i, s: (0, 0))
    half = spec((rows, width // 2), lambda i, s: (0, 1 - s[0]))
    return call(
        proj_kernel,
        (1,),
        [full, half, whole(w), full, whole(gain)],
        [
            full,
            full,
            spec((width + rows, rows), lambda i, s: (0, 0)),
        ],
        [
            shape((rows, width), f32),
            shape((rows, width), bf16),
            shape((width + rows, rows), bf16),
        ],
        (att, att, w, resid, gain),
        scalars,
        24,
    )


def gelu_and_slope(v):
    c = math.sqrt(2.0 / math.pi)
    square = v * v
    t = jnp.tanh(v * (c + (c * 0.044715) * square))
    act = 0.5 * v * (1.0 + t)
    slope = 0.5 * (1.0 + t) + (0.5 * v) * (1.0 - t * t) * (c + (3.0 * c * 0.044715) * square)
    return act, slope


def ff_kernel(count, s, normed, cot, up, down, *refs):
    step = pl.program_id(0)
    if count > 1:
        out_in, back_in, resid2, gain, w_own, w_other, *refs = refs
    pieces, refs = refs[: 2 * count], refs[2 * count :]
    if count > 1:
        out_low, grad2, branch, g_own, g_other, out, back = refs
    else:
        out, back = refs
    hidden = dot(normed[...], up[...])
    act, slope = gelu_and_slope(hidden)
    act = act.astype(bf16)
    grad = (dot(cot[...], down[...], NT) * slope).astype(bf16)
    out_part = dot(act, down[...])
    back_part = dot(grad, up[...], NT)

    @pl.when(step == 0)
    def _():
        out[...] = out_in[...] + out_part if count > 1 else out_part
        back[...] = back_in[...] + back_part if count > 1 else back_part

    @pl.when(step > 0)
    def _():
        out[...] += out_part
        back[...] += back_part

    for at, piece in enumerate(pieces):

        @pl.when(step == at)
        def _(piece=piece):
            piece[0] = act
            piece[1] = grad

    if count > 1:

        @pl.when(step == 2 * count - 1)
        def _():
            value = resid2[...]
            out_low[...] = (value + out[...]).astype(bf16)
            xhat, scale = normalize(value)
            g = cot[...].astype(f32) + norm_backward(back[...], gain[...], xhat, scale)
            grad2[...] = g
            low = g.astype(bf16)
            branch[...] = low
            g_other[...] = dot(low, w_other[...], NT).astype(bf16)
            g_own[...] = dot(low, w_own[...], NT).astype(bf16)


def ff_chunks(scalars, first, count, normed, cot, up, down, *more):
    rows, width = normed.shape
    half = width // 2
    wide = 512

    def column(i, s):
        return 2 * (first + i // 2) + (s[0] ^ (1 - (i & 1)))

    full = spec((rows, width), lambda i, s: (0, 0))
    part = spec((rows, half), lambda i, s: (0, 0))
    in_specs = [
        whole(normed),
        whole(cot),
        spec((width, wide), lambda i, s: (0, column(i, s))),
        spec((wide, width), lambda i, s: (column(i, s), 0)),
    ]
    out_specs = [spec((2, rows, wide), lambda i, s: (0, 0, 0))] * (2 * count)
    out_shape = [shape((2, rows, wide), bf16)] * (2 * count)
    scratch = []
    if count > 1:
        in_specs += [
            full,
            full,
            full,
            spec((1, width), lambda i, s: (0, 0)),
            spec((half, width), lambda i, s: (s[1], 0)),
            spec((half, width), lambda i, s: (1 - s[1], 0)),
        ]
        out_specs += [full, full, full, part, part]
        out_shape += [shape((rows, width), t) for t in (bf16, f32, bf16)]
        out_shape += [shape((rows, half), bf16)] * 2
        scratch = [pltpu.VMEM((rows, width), f32)] * 2
    else:
        out_specs += [full, full]
        out_shape += [shape((rows, width), f32)] * 2
    return call(
        functools.partial(ff_kernel, count),
        (2 * count,),
        in_specs,
        out_specs,
        out_shape,
        (normed, cot, up, down) + more,
        scalars,
        28,
        scratch,
    )


def ff_grads_kernel(at, s, act, act_o, grad, grad_o, cot, cot_o, nt, nt_o, *refs):
    keep, send = refs[-2:]
    step = pl.program_id(0)
    rows_both = jnp.concatenate([cot[...], cot_o[...]], 0)
    g_down = dot(jnp.concatenate([act[0], act_o[0]], 0), rows_both, TN).astype(bf16)
    grads = jnp.concatenate([grad[0], grad_o[0]], 0)
    g_up = dot(jnp.concatenate([nt[...], nt_o[...]], 1), grads).astype(bf16)
    g_proj = None
    if len(refs) > 2:
        att, att_o, branch, branch_o = refs[:4]
        both = jnp.concatenate([branch[...], branch_o[...]], 0)
        g_proj = dot(jnp.concatenate([att[...], att_o[...]], 0), both, TN).astype(bf16)
    code = s[at] & 7

    def store(target):
        rows_d = g_down.shape[0] // 8
        rows_u = g_up.shape[0] // 8
        half = g_up.shape[1] // 2
        for block in range(8):
            to = block ^ code
            target[to, :rows_d, :] = g_down[block * rows_d : (block + 1) * rows_d]
            part = g_up[block * rows_u : (block + 1) * rows_u]
            target[to, 32:64, : 2 * half] = part[:32]
            target[to, 32:48, 2 * half :] = part[32:, :half]
            target[to, 48:64, 2 * half :] = part[32:, half:]
            if g_proj is not None:
                part = g_proj[block * rows_u : (block + 1) * rows_u]
                wide = part.shape[1]
                target[to, 64:80, :wide] = part[:16]
                target[to, 64:80, wide:] = part[16:32]
                target[to, 80:, :wide] = part[32:]
                target[to, 80:, wide:] = jnp.zeros_like(part[32:])

    @pl.when(step == 0)
    def _():
        store(send)

    @pl.when(step == 1)
    def _():
        store(keep)


def ff_grads(scalars, chunk, mine, theirs, cot, cot_other, normed_t_other, normed_t, *proj):
    rows, width = cot.shape
    wide = mine.shape[2]
    at = 2 + 2 * chunk

    def side(i, s):
        return (1 - i) ^ (s[at] // 8)

    act = spec((1, rows, wide // 2), lambda i, s: (0, 0, side(i, s)))
    grad = spec((1, rows, wide), lambda i, s: (1, 0, 0))
    feature = spec((width // 2, rows), lambda i, s: (side(i, s), 0))
    in_specs = [act, act, grad, grad, whole(cot), whole(cot), feature, feature]
    if proj:
        half = width // 2
        column = spec((rows, half), lambda i, s: (0, side(i, s)))
        packed = spec((rows, half), lambda i, s: (2, 0))
        in_specs += [spec((rows, half), lambda i, s: (0, s[0])), packed, column, column]
    deep = 96 if proj else 64
    piece = spec((8, deep, width), lambda i, s: (0, 0, 0))
    return call(
        functools.partial(ff_grads_kernel, at),
        (2,),
        in_specs,
        [piece, piece],
        [shape((8, deep, width), bf16)] * 2,
        (mine, theirs, mine, theirs, cot, cot_other, normed_t, normed_t_other) + proj,
        scalars,
        28,
    )


def attn_back_kernel(group, s, q, g, k_o, k_f, v_o, v_f, *refs):
    gk_in, gv_in = refs[:2] if len(refs) == 5 else (None, None)
    gq, gk, gv = refs[-3:]
    rows = q.shape[0]
    for pair in range(group):
        lanes = slice(pair * PAIR, (pair + 1) * PAIR)
        k = jnp.concatenate([k_o[:, lanes], k_f[:, lanes]], 0)
        v = jnp.concatenate([v_o[:, lanes], v_f[:, lanes]], 0)
        kt = (k.astype(f32) * HD**-0.5).astype(bf16).T
        qs = jnp.concatenate(head_masks(q[:, lanes].astype(f32) * HD**-0.5), 0)
        gs = jnp.concatenate(head_masks(g[:, lanes].astype(f32)), 0)
        scores = dot(k, qs, NT)
        e = jnp.exp(scores - jnp.max(scores, 0, keepdims=True))
        probs = e * (1.0 / jnp.sum(e, 0, keepdims=True))
        grad_v = dot(probs.astype(bf16), gs)
        grad_p = dot(v, gs, NT)
        row = jnp.sum(probs * grad_p, 0, keepdims=True)
        grad_s = (probs * (grad_p - row)).astype(bf16)
        grad_k = dot(grad_s, qs)
        grad_q = [
            dot(kt[h * HD : (h + 1) * HD], grad_s[:, h * rows : (h + 1) * rows]) for h in range(2)
        ]
        if gk_in is not None:
            grad_k, grad_v = grad_k + gk_in[:, lanes], grad_v + gv_in[:, lanes]
        gq[:, lanes] = jnp.concatenate(grad_q, 0).T.astype(bf16)
        gk[:, lanes] = grad_k.astype(gk.dtype)
        gv[:, lanes] = grad_v.astype(gv.dtype)


def attention_back(scalars, query, grad, qkv, kv_far, *so_far):
    rows, width = qkv.shape[0], qkv.shape[1] // 3
    mine = width // PAIR // 2
    group = BACK_GROUP
    steps = mine // group

    def column(part):
        return spec((rows, group * PAIR), lambda i, s: (0, (2 * part + s[1]) * steps + i))

    block = spec((rows, group * PAIR), lambda i, s: (0, i))
    both = spec((2 * rows, group * PAIR), lambda i, s: (0, i))
    dtype = bf16 if so_far else f32
    return call(
        functools.partial(attn_back_kernel, group),
        (steps,),
        [block if so_far else column(0), block, column(1), column(0), column(2), column(1)]
        + [both] * len(so_far),
        [block, both, both],
        [shape((rows, width // 2), bf16)] + [shape((2 * rows, width // 2), dtype)] * 2,
        (query, grad, qkv, kv_far, qkv, kv_far) + so_far,
        scalars,
        BACK_LIMIT,
    )


def joint_kernel(s, n_own, n_far, gq_o, gq_f, gk, gv, keep, send):
    step = pl.program_id(0)
    gq = jnp.concatenate([gq_o[...], gq_f[...]], 0)
    n = jnp.concatenate([n_own[...], n_far[...]], 0)
    cols = gk.shape[1]

    def fill(target, code):
        tiles = [dot(n, g, TN).astype(bf16) for g in (gq, gk[...], gv[...])]
        rows = tiles[0].shape[0] // 8
        for block in range(8):
            at = block ^ code
            for i, tile in enumerate(tiles):
                part = tile[block * rows : (block + 1) * rows]
                target[at, :, i * cols : i * cols + part.shape[1]] = part

    @pl.when(step == 0)
    def _():
        fill(send, s[9])

    @pl.when(step == 1)
    def _():
        fill(keep, s[8])


def joint_grads(scalars, n_own, n_far, gq, gq_far, gk, gv):
    rows, width = n_own.shape
    half = width // 2
    feature = spec((rows, half), lambda i, s: (0, s[0] ^ (1 - i)))
    cols = 3 * half
    piece = spec((8, half // 8, cols), lambda i, s: (0, 0, 0))
    return call(
        joint_kernel,
        (2,),
        [feature, feature, whole(gq), whole(gq), whole(gk), whole(gv)],
        [piece, piece],
        [shape((8, half // 8, cols), bf16)] * 2,
        (n_own, n_far, gq, gq_far, gk, gv),
        scalars,
        28,
    )


def back_qkv_kernel(s, gq_o, gq_f, gk, gv, wq, wk, wv, own, far):
    rows = own.shape[0]

    def part(gq, at):
        total = dot(gq[...], wq[...], NT)
        total += dot(gk[pl.ds(at, rows)], wk[...], NT)
        return total + dot(gv[pl.ds(at, rows)], wv[...], NT)

    far[...] = part(gq_f, rows).astype(bf16)
    own[...] = part(gq_o, 0)


def back_qkv(scalars, gq, gq_far, gk, gv, w):
    rows, half = gq.shape
    width = 2 * half

    def column(part):
        return spec((width, half), lambda i, s: (0, 2 * part + s[1]))

    full = spec((rows, width), lambda i, s: (0, 0))
    return call(
        back_qkv_kernel,
        (1,),
        [whole(gq), whole(gq), whole(gk), whole(gv), column(0), column(1), column(2)],
        [full, full],
        [shape((rows, width), f32), shape((rows, width), bf16)],
        (gq, gq_far, gk, gv, w, w, w),
        scalars,
        28,
    )


def last_kernel(s, own, far, resid, gain, grad2, out):
    xhat, scale = normalize(resid[...])
    grad = own[...] + far[...].astype(f32)
    out[...] = grad2[...] + norm_backward(grad, gain[...], xhat, scale)


def token_grad(scalars, own, far, resid, gain, grad2):
    args = (own, far, resid, gain, grad2)
    return call(
        last_kernel,
        (1,),
        [whole(a) for a in args],
        whole(own),
        shape(own.shape, f32),
        args,
        scalars,
        24,
    )


def row_sums(values):
    folded = sum(values[:, at : at + 128] for at in range(0, values.shape[1], 128))
    return lax.dot_general(
        jnp.ones((8, 128), f32),
        folded,
        (NT, ((), ())),
        precision=lax.Precision.HIGHEST,
        preferred_element_type=f32,
    )


def unpack_ff_kernel(at, last, s, own, other, w, gain_in, *refs):
    gain, down, up, *proj = refs[-4:] if last else refs[-3:]
    step = pl.program_id(0)

    def unpack(source, code):
        for block in range(8):
            to = block ^ (code & 7)
            down[pl.ds(pl.multiple_of(to * 32, 32), 32), :] = source[block, :32, :].astype(f32)
            row = pl.multiple_of(to * 48, 16)
            up[pl.ds(row, 32), :] = source[block, 32:64, :512].astype(f32)
            up[pl.ds(row + 32, 16), :256] = source[block, 32:48, 512:].astype(f32)
            up[pl.ds(row + 32, 16), 256:] = source[block, 48:64, 512:].astype(f32)
            if last:
                wide = source.shape[2] // 2
                proj[0][pl.ds(row, 16), :] = source[block, 64:80, :wide].astype(f32)
                proj[0][pl.ds(row + 16, 16), :] = source[block, 64:80, wide:].astype(f32)
                proj[0][pl.ds(row + 32, 16), :] = source[block, 80:, :wide].astype(f32)

    @pl.when(step == 0)
    def _():
        unpack(own, s[at])

    @pl.when(step == 1)
    def _():
        unpack(other, s[at + 1])

    gain[0, 0] = gain_in[0, 0] + row_sums(up[...] * w[...].astype(f32))


def unpack_ff(scalars, chunk, far, own, other, w, so_far):
    width, hidden = w.shape
    at = 2 + 2 * chunk
    last = own.shape[1] > 64

    def side(i, s):
        return (s[at + i] // 8) ^ far

    def half(i, s):
        return 2 * chunk + (s[0] ^ i)

    any_spec = pl.BlockSpec(memory_space=pl.ANY)
    column = spec((width // 2, 512), lambda i, s: (side(i, s), half(i, s)))
    gain = spec((1, 1, 8, width // 2), lambda i, s: (i, side(i, s), 0, 0))
    out_specs = [gain, spec((256, width), lambda i, s: (2 * half(i, s) + side(i, s), 0)), column]
    out_shape = [shape((2, 2, 8, width // 2), f32), shape((hidden, width), f32), shape((width, hidden), f32)]
    if last:
        out_specs.append(spec((width // 2, width // 2), lambda i, s: (s[0] ^ i, side(i, s))))
        out_shape.append(shape((width, width), f32))
    in_specs = [whole(own), whole(other), column]
    in_specs += [gain, any_spec, any_spec, any_spec][: len(so_far)]
    return call(
        functools.partial(unpack_ff_kernel, at, last),
        (2,),
        in_specs,
        out_specs,
        out_shape,
        (own, other, w) + tuple(so_far),
        scalars,
        28,
        aliases={4 + i: i for i in range(len(so_far))},
    )


def unpack_qkv_kernel(s, own, other, w, *refs):
    joint, gain = refs[-2:]
    step = pl.program_id(0)
    mine = s[1]

    def unpack(source, code):
        half = source.shape[2] // 6

        def place_columns(first):
            for block in range(2):
                rows = pl.ds(pl.multiple_of((block ^ (code & 1)) * 48, 16), 48)
                for part in range(3):
                    for side in range(2):
                        column = 2 * half * part + half * (first ^ side)
                        value = source[block, :, (3 * side + part) * half : (3 * side + part + 1) * half]
                        joint[rows, column : column + half] = value.astype(f32)

        for first in range(2):
            pl.when(mine == first)(functools.partial(place_columns, first))

    @pl.when(step < 2)
    def _():
        unpack(own, s[8])

    @pl.when(step >= 2)
    def _():
        unpack(other, s[9])

    gain[0] = row_sums(joint[...] * w[...].astype(f32))


def unpack_qkv(scalars, far, own, other, w, so_far):
    width = w.shape[0]

    def row(i, s):
        code = s[8 + i // 2]
        return 4 * (s[0] ^ (i // 2)) + 2 * ((code // 4) ^ far) + ((i & 1) ^ ((code // 2) & 1))

    def blocks(mine):
        return spec((2,) + own.shape[1:], lambda i, s: (jnp.clip(i - 2 * mine, 0, 1), 0, 0))

    any_spec = pl.BlockSpec(memory_space=pl.ANY)
    rows = spec((width // 8, 3 * width), lambda i, s: (row(i, s), 0))
    return call(
        unpack_qkv_kernel,
        (4,),
        [blocks(0), blocks(1), rows] + [any_spec] * len(so_far),
        [rows, spec((1, 8, width // 8), lambda i, s: (row(i, s), 0, 0))],
        [shape((width, 3 * width), f32), shape((8, 8, width // 8), f32)],
        (own, other, w) + tuple(so_far),
        scalars,
        28,
        aliases={4 + i: i for i in range(len(so_far))},
    )


def fast(tokens, visible, ln1_gain, w_qkv, w_proj, ln2_gain, w_up, w_down, d_out):
    tok, cot = tokens[0], d_out[0]
    rows, width = tok.shape
    gain1, gain2 = ln1_gain[None], ln2_gain[None]
    scalars = [lax.axis_index("dp") & 1, lax.axis_index("blk")]
    for orders in FF_ORDERS + (QKV_ORDER,):
        scalars.extend(places(orders))
    scalars = jnp.stack([jnp.int32(v) for v in scalars])

    order = Order()
    run = order.run
    vis_far = swap(visible, "y")
    tok_far = swap(tok, "y")
    half = width // 2
    freqs = jnp.exp(jnp.arange(half, dtype=f32) * (-math.log(10000.0) / half))[None]
    pos = run(functools.partial(positions, scalars), visible, freqs)
    normed1, qkv, resid = run(functools.partial(ln_qkv, scalars, False), tok, pos, gain1, w_qkv)
    sums = run(functools.partial(attention, scalars), qkv, qkv)
    pos_far = run(functools.partial(positions, scalars), vis_far, freqs)
    normed1_far, kv_far = run(functools.partial(ln_qkv, scalars, True), tok_far, pos_far, gain1, w_qkv)
    attended = run(functools.partial(attention, scalars), qkv, kv_far, *sums)
    resid2, normed2, packed = run(
        functools.partial(project, scalars), attended, w_proj, resid, gain2
    )
    early = tuple(order.swap(array, "c") for array in (cot, packed))

    streams, blocks, values = {}, {}, {"early": early}
    ff, proj, joint = (jnp.zeros((2, 2, 8, width // 2), f32),), (), ()

    def feed_forward(first):
        if first == 0:
            send, keep, *values["sums"] = run(
                functools.partial(ff_chunks, scalars, 0, 1), normed2, cot, w_up, w_down
            )
            values["act", 0], values["e0"] = keep, order.swap(send, "c")
            return
        more = (*values["sums"], resid2, gain2, w_proj, w_proj)
        send1, keep1, send2, keep2, out, grad2, branch, g_own, g_other = run(
            functools.partial(ff_chunks, scalars, 1, 2), normed2, cot, w_up, w_down, *more
        )
        values["act", 1], values["e1"] = keep1, order.swap(send1, "c")
        values["act", 2], values["e2"] = keep2, order.swap(send2, "c")
        values["branch"], values["branch_other"] = branch, order.swap(branch, "c")
        values["g"] = order.swap(g_other, "y")
        values.update(out=out, grad2=grad2, own=g_own)

    def weight_grads(chunk):
        early = (*values["early"], packed)
        more = ()
        if chunk == 2:
            more = (attended, values["early"][1], values["branch"], values["branch_other"])
        keep, send = run(
            functools.partial(ff_grads, scalars, chunk),
            values["act", chunk], values["e%d" % chunk], cot, *early, *more,
        )
        streams[chunk] = total(order, keep, send, list(zip(*FF_ORDERS[chunk])))
        advance(chunk)

    def advance(chunk):
        pair = next(streams[chunk])
        if pair is not None:
            blocks.setdefault(chunk, []).append(pair)

    def wait(key):
        if key[0] in "nf" and key[1:].isdigit():
            chunk, far = int(key[1:]), int(key[0] == "f")
            own, other = blocks[chunk][far]
            blocks[chunk][far] = own, run(lambda value: value, other)
            return
        value = values[key]
        values[key] = run(lambda *v: v if isinstance(value, tuple) else v[0], *(value if isinstance(value, tuple) else (value,)))

    def own_queries():
        values["attn"] = run(functools.partial(attention_back, scalars), qkv, values["own"], qkv, kv_far)

    def far_queries():
        gq, *sums = values["attn"]
        values["q"] = run(functools.partial(far_query, scalars), normed1_far, w_qkv)
        back = run(functools.partial(attention_back, scalars), values["q"], values["g"], qkv, kv_far, *sums)
        values["attn"] = (gq, *back)

    def joint_weights():
        keep, send = run(functools.partial(joint_grads, scalars), normed1, normed1_far, *values["attn"])
        links = [("c", "c")] + list(zip(*QKV_ORDER))
        streams[3] = total(order, keep, send, links, lambda a, b: jnp.concatenate([a, b], -1))
        advance(3)

    def back_joint():
        own, far = run(functools.partial(back_qkv, scalars), *values["attn"], w_qkv)
        values["norm"], values["bf"] = own, order.swap(far, "y")

    def finish_tokens():
        args = (values["norm"], values["bf"], resid, gain1, values["grad2"])
        values["tokens"] = run(functools.partial(token_grad, scalars), *args)

    def unpack(chunk, far):
        nonlocal ff, proj, joint
        own, other = blocks[chunk][far]
        if chunk == 3:
            joint = run(lambda a, b, *f: unpack_qkv(scalars, far, a, b, w_qkv, f), own, other, *joint)
            return
        so_far = ff + proj if chunk == 2 else ff
        weight = w_hbm if (chunk, far) == final else w_up
        result = tuple(
            run(lambda a, b, *f: unpack_ff(scalars, chunk, far, a, b, weight, f), own, other, *so_far)
        )
        ff, proj = result[:3], result[3:] or proj

    w_hbm = pltpu.with_memory_space_constraint(w_up, pltpu.HBM)
    final = [step[1:] for step in PLAN if step[0] == "unpack" and step[1] != 3][-1]
    steps = {
        "ff": feed_forward,
        "dw": weight_grads,
        "go": advance,
        "wait": wait,
        "own": own_queries,
        "far": far_queries,
        "joint": joint_weights,
        "back": back_joint,
        "tokens": finish_tokens,
        "unpack": unpack,
    }
    for name, *args in PLAN:
        steps[name](*args)
    sums2, d_down, d_up = ff
    d_qkv, sums1 = joint
    out, d_tokens, d_proj = values["out"], values["tokens"], proj[0]
    d_gain1 = sums1[:, 0].reshape(-1) / ln1_gain
    d_gain2 = (sums2[0, :, 0] + sums2[1, :, 0]).reshape(-1) / ln2_gain
    return out[None], d_tokens[None], d_gain1, d_qkv, d_proj, d_gain2, d_up, d_down


def layer_norm(values, gain):
    center = values - jnp.mean(values, -1, keepdims=True)
    spread = jnp.mean(center * center, -1, keepdims=True)
    return center * lax.rsqrt(spread + epsilon) * gain


def outer_product(left, right):
    return lax.dot_general(
        left, right, (((0,), (0,)), ((), ())), preferred_element_type=jnp.float32
    )


def times_transposed(left, weight):
    return lax.dot_general(
        left, weight, (((1,), (1,)), ((), ())), preferred_element_type=jnp.float32
    )


def split_blocks(keys, values):
    count = keys.shape[0]
    size = math.gcd(count, 512)
    shape = (count // size, size, HEADS, HD)
    return (keys.reshape(shape), values.reshape(shape))


def general(tokens, visible, ln1_gain, w_qkv, w_proj, ln2_gain, w_up, w_down, d_out):
    rows = tokens.shape[1]
    width = tokens.shape[2]
    factor = HD ** (-0.5)
    resid = tokens[0].astype(jnp.float32) + position_table(visible[0], width)
    normed1, back_one = jax.vjp(layer_norm, resid, ln1_gain)
    normed1 = normed1.astype(jnp.bfloat16)
    qkv = jnp.dot(normed1, w_qkv, preferred_element_type=jnp.float32).astype(jnp.bfloat16)
    query = qkv[:, :width]
    keys = qkv[:, width : 2 * width]
    values = qkv[:, 2 * width :]
    query_heads = query.reshape(rows, HEADS, HD)
    initial = (
        jnp.full((HEADS, rows), -1e30, jnp.float32),
        jnp.zeros((HEADS, rows), jnp.float32),
        jnp.zeros((HEADS, rows, HD), jnp.float32),
    )
    key_blocks, value_blocks = split_blocks(
        lax.all_gather(keys, "blk", axis=0, tiled=True),
        lax.all_gather(values, "blk", axis=0, tiled=True),
    )

    def one_block(state, block):
        running, total, accum = state
        block_keys, block_values = block
        scores = (
            jnp.einsum("qhd,khd->hqk", query_heads, block_keys, preferred_element_type=jnp.float32)
            * factor
        )
        top = jnp.maximum(running, jnp.max(scores, -1))
        weights = jnp.exp(scores - top[..., None])
        shrink = jnp.exp(running - top)
        total = total * shrink + jnp.sum(weights, -1)
        accum = accum * shrink[..., None] + jnp.einsum(
            "hqk,khd->hqd",
            weights.astype(jnp.bfloat16),
            block_values,
            preferred_element_type=jnp.float32,
        )
        return ((top, total, accum), None)

    running, total, accum = lax.scan(one_block, initial, (key_blocks, value_blocks))[0]
    log_total = running + jnp.log(total)
    attended = (accum / total[..., None]).transpose(1, 0, 2).reshape(rows, width)
    attended_low = attended.astype(jnp.bfloat16)
    resid2 = resid + jnp.dot(attended_low, w_proj, preferred_element_type=jnp.float32)
    normed2, back_two = jax.vjp(layer_norm, resid2, ln2_gain)
    normed2 = normed2.astype(jnp.bfloat16)
    hidden = jnp.dot(normed2, w_up, preferred_element_type=jnp.float32)
    activated, back_gelu = jax.vjp(jax.nn.gelu, hidden)
    activated = activated.astype(jnp.bfloat16)
    result = resid2 + jnp.dot(activated, w_down, preferred_element_type=jnp.float32)
    cotangent = d_out[0]
    grad_down = outer_product(activated, cotangent)
    (grad_hidden,) = back_gelu(times_transposed(cotangent, w_down))
    grad_hidden = grad_hidden.astype(jnp.bfloat16)
    grad_up = outer_product(normed2, grad_hidden)
    grad_resid2, grad_gain2 = back_two(times_transposed(grad_hidden, w_up))
    grad_resid2 = grad_resid2 + cotangent.astype(jnp.float32)
    grad_branch = grad_resid2.astype(jnp.bfloat16)
    grad_proj = outer_product(attended_low, grad_branch)
    grad_attended = times_transposed(grad_branch, w_proj).astype(jnp.bfloat16)
    correction = (grad_attended.astype(jnp.float32) * attended).reshape(rows, HEADS, HD)
    correction = jnp.sum(correction, -1).T
    grad_heads = grad_attended.reshape(rows, HEADS, HD)
    all_keys, all_values = (
        lax.all_gather(keys, "blk", axis=0, tiled=True),
        lax.all_gather(values, "blk", axis=0, tiled=True),
    )
    full_rows = all_keys.shape[0]
    key_blocks, value_blocks = split_blocks(all_keys, all_values)

    def back_block(grad_query, block):
        block_keys, block_values = block
        scores = (
            jnp.einsum("qhd,khd->hqk", query_heads, block_keys, preferred_element_type=jnp.float32)
            * factor
        )
        probs = jnp.exp(scores - log_total[..., None])
        grad_value = jnp.einsum(
            "hqk,qhd->khd",
            probs.astype(jnp.bfloat16),
            grad_heads,
            preferred_element_type=jnp.float32,
        )
        grad_probs = jnp.einsum(
            "qhd,khd->hqk", grad_heads, block_values, preferred_element_type=jnp.float32
        )
        grad_scores = (probs * (grad_probs - correction[..., None])).astype(jnp.bfloat16)
        grad_query = grad_query + jnp.einsum(
            "hqk,khd->qhd", grad_scores, block_keys, preferred_element_type=jnp.float32
        )
        grad_key = (
            jnp.einsum("hqk,qhd->khd", grad_scores, query_heads, preferred_element_type=jnp.float32)
            * factor
        )
        return (grad_query, (grad_key, grad_value))

    grad_query, (key_parts, value_parts) = lax.scan(
        back_block, jnp.zeros((rows, HEADS, HD), jnp.float32), (key_blocks, value_blocks)
    )
    grad_query = (grad_query * factor).reshape(rows, width)
    grad_keys, grad_values = (
        lax.psum_scatter(
            key_parts.reshape(full_rows, width).astype(jnp.bfloat16),
            "blk",
            scatter_dimension=0,
            tiled=True,
        ).astype(jnp.float32),
        lax.psum_scatter(
            value_parts.reshape(full_rows, width).astype(jnp.bfloat16),
            "blk",
            scatter_dimension=0,
            tiled=True,
        ).astype(jnp.float32),
    )
    grad_qkv = jnp.concatenate([grad_query, grad_keys, grad_values], 1).astype(jnp.bfloat16)
    grad_joint = outer_product(normed1, grad_qkv)
    grad_resid, grad_gain1 = back_one(times_transposed(grad_qkv, w_qkv))
    input_grad = grad_resid2 + grad_resid
    flats = (
        grad_joint.reshape(-1),
        grad_proj.reshape(-1),
        grad_up.reshape(-1),
        grad_down.reshape(-1),
    )
    shares = (
        lax.psum_scatter(flats[0], ("dp", "blk"), scatter_dimension=0, tiled=True),
        lax.psum_scatter(flats[1], ("dp", "blk"), scatter_dimension=0, tiled=True),
        lax.psum_scatter(flats[2], ("dp", "blk"), scatter_dimension=0, tiled=True),
        lax.psum_scatter(flats[3], ("dp", "blk"), scatter_dimension=0, tiled=True),
    )
    summed = (
        lax.all_gather(shares[0].astype(jnp.bfloat16), ("dp", "blk"), axis=0, tiled=True).astype(
            jnp.float32
        ),
        lax.all_gather(shares[1].astype(jnp.bfloat16), ("dp", "blk"), axis=0, tiled=True).astype(
            jnp.float32
        ),
        lax.all_gather(shares[2].astype(jnp.bfloat16), ("dp", "blk"), axis=0, tiled=True).astype(
            jnp.float32
        ),
        lax.all_gather(shares[3].astype(jnp.bfloat16), ("dp", "blk"), axis=0, tiled=True).astype(
            jnp.float32
        ),
    )
    gain_one, gain_two = lax.psum((grad_gain1, grad_gain2), ("dp", "blk"))
    return (
        result.astype(jnp.bfloat16)[None],
        input_grad[None],
        gain_one,
        summed[0].reshape(w_qkv.shape),
        summed[1].reshape(w_proj.shape),
        gain_two,
        summed[2].reshape(w_up.shape),
        summed[3].reshape(w_down.shape),
    )


def solution(mesh):
    split = mesh.shape["dp"] == 16 and mesh.shape["blk"] == 2

    def local(tokens, *others):
        fits = split and 2 * tokens.shape[1] == tokens.shape[2]
        return (fast if fits else general)(tokens, *others)

    return jax.shard_map(
        local,
        mesh=mesh,
        in_specs=(
            P("dp", "blk", None),
            P("dp", "blk"),
            P(),
            P(),
            P(),
            P(),
            P(),
            P(),
            P("dp", "blk", None),
        ),
        out_specs=(P("dp", "blk", None), P("dp", "blk", None), P(), P(), P(), P(), P(), P()),
        check_vma=False,
    )
```

```python
import functools
import math

import jax
import jax.numpy as jnp
from jax import lax
from jax.experimental import pallas as pl
from jax.experimental.pallas import tpu as pltpu
from jax.sharding import PartitionSpec as P

HEADS = 12
HD = 64
PAIR = 2 * HD
GROUP = 2
BACK_GROUP = 1
BACK_LIMIT = 28
epsilon = 1e-06
f32 = jnp.float32
bf16 = jnp.bfloat16
NN = ((1,), (0,))
NT = ((1,), (1,))
TN = ((0,), (0,))
AXES = ("dp", "blk")
MIB = 1 << 20


def dot(left, right, dims=NN):
    return lax.dot_general(left, right, (dims, ((), ())), preferred_element_type=f32)


def position_table(visible, width):
    half = width // 2
    column = jnp.arange(half, dtype=f32)
    freqs = jnp.exp(column * (-math.log(10000.0) / half))
    angles = visible.astype(f32)[..., None] * freqs
    return jnp.concatenate([jnp.sin(angles), jnp.cos(angles)], -1)


def normalize(values):
    center = values - jnp.mean(values, -1, keepdims=True)
    spread = jnp.mean(center * center, -1, keepdims=True)
    scale = lax.rsqrt(spread + epsilon)
    return center * scale, scale


def norm_backward(grad, gain, xhat, scale):
    e = grad * gain
    return scale * (
        e - jnp.mean(e, -1, keepdims=True) - xhat * jnp.mean(e * xhat, -1, keepdims=True)
    )


def call(kernel, grid, in_specs, out_specs, out_shape, args, scalars, vmem, scratch=(), aliases=None):
    return pl.pallas_call(
        kernel,
        grid_spec=pltpu.PrefetchScalarGridSpec(
            num_scalar_prefetch=1,
            grid=grid,
            in_specs=in_specs,
            out_specs=out_specs,
            scratch_shapes=list(scratch),
        ),
        out_shape=out_shape,
        input_output_aliases=aliases or {},
        compiler_params=pltpu.CompilerParams(vmem_limit_bytes=max(vmem, 28) * MIB),
        cost_estimate=pl.CostEstimate(flops=1, bytes_accessed=1, transcendentals=0),
    )(scalars, *args)


def spec(shape, index):
    return pl.BlockSpec(shape, index)


def whole(array):
    zeros = (0,) * array.ndim
    return pl.BlockSpec(array.shape, lambda i, s: zeros)


def shape(dims, dtype):
    return jax.ShapeDtypeStruct(dims, dtype)


FF_ORDERS = (
    (("x", "y", "z0", "z1"), ("y", "z0", "x", "z1")),
    (("z0", "y", "x", "z1"), ("x", "y", "z1", "z0")),
    (("y", "z0", "x", "z1"), ("x", "y", "z0", "z1")),
)
QKV_ORDER = (("x", "z0", "z1"), ("z0", "z1", "x"))
PLAN = (
    ("ff", 0), ("wait", "early"), ("ff", 1), ("wait", "e0"), ("dw", 0), ("own",),
    ("wait", "branch_other"), ("wait", "e2"), ("wait", "g"), ("dw", 2), ("wait", "e1"), ("dw", 1),
    ("go", 0), ("far",), ("go", 2), ("joint",), ("go", 0), ("go", 2), ("go", 1), ("go", 0),
    ("go", 3), ("go", 2), ("back",), ("go", 3), ("go", 1), ("go", 0), ("wait", "bf"), ("go", 2),
    ("go", 0), ("go", 3), ("go", 2), ("go", 1), ("go", 3), ("go", 0), ("go", 3), ("go", 2),
    ("go", 1), ("wait", "n0"), ("go", 0), ("unpack", 0, 0), ("go", 3), ("go", 1), ("wait", "f0"),
    ("tokens",), ("unpack", 0, 1), ("go", 2), ("wait", "n2"), ("unpack", 2, 0), ("go", 1),
    ("go", 3), ("wait", "f2"), ("wait", "n3"), ("unpack", 2, 1), ("unpack", 3, 0), ("wait", "f3"),
    ("unpack", 3, 1), ("go", 1), ("wait", "n1"), ("unpack", 1, 0), ("wait", "f1"), ("unpack", 1, 1),
)
DP_BIT = {"c": 1, "x": 2, "z0": 4, "z1": 8}


def swap(array, first, second=None):
    second = second or first
    pairs = []
    for d in range(16):
        for b in range(2):
            bit = second if d & 1 else first
            to = (d, b ^ 1) if bit == "y" else (d ^ DP_BIT[bit], b)
            pairs.append((d * 2 + b, to[0] * 2 + to[1]))
    return lax.ppermute(array, AXES, pairs)


def place(order):
    d, b = lax.axis_index("dp"), lax.axis_index("blk")
    code = jnp.int32(0)
    for bit in order:
        value = b & 1 if bit == "y" else (d // DP_BIT[bit]) & 1
        code = code * 2 + value
    return code


def places(orders):
    core = lax.axis_index("dp") & 1
    first, second = place(orders[0]), place(orders[1])
    return jnp.where(core == 0, first, second), jnp.where(core == 0, second, first)


def add(a, b):
    return (a.astype(f32) + b.astype(f32)).astype(bf16)


class Order:
    def __init__(self):
        self.last = None

    def pin(self, *arrays):
        if self.last is None:
            return arrays
        return lax.optimization_barrier((*arrays, self.last))[:-1]

    def run(self, function, *arrays):
        result = function(*self.pin(*arrays))
        self.last = result[0] if isinstance(result, (tuple, list)) else result
        return result

    def swap(self, array, first, second=None):
        return swap(self.pin(array)[0], first, second)


def total(order, keep, send, links, widen=None):
    received = order.swap(send, *links[0])
    yield
    for link in links[1:-1]:
        half = keep.shape[0] // 2
        send = order.run(lambda k, r: add(k[half:], r[half:]), keep, received)
        coming = order.swap(send, *link)
        keep = order.run(lambda k, r: add(k[:half], r[:half]), keep, received)
        received = coming
        yield
    keep = order.run(add, keep, received)
    received = order.swap(keep, *links[-1])
    yield
    block = order.run(lambda k, r: add(k, r[::-1]), keep, received)
    if widen is not None:
        received = order.swap(block, "y")
        yield
        block = order.run(widen, block, received)
    back = [link for link in links[:-1] if link[0] != "c"][::-1]
    for link in back[:-1]:
        received = order.swap(block, *link)
        yield
        block = order.run(lambda k, r: jnp.concatenate([k, r], 0), block, received)
    far = order.swap(block, *back[-1])
    other = order.swap(block, "c")
    yield block, other
    far = order.run(lambda value: value, far)
    yield far, order.swap(far, "c")


def sine_and_cosine(angle):
    turns = jnp.floor(angle * (2.0 / math.pi) + 0.5)
    rest = angle - turns * 1.5703125
    rest = rest - turns * 4.837512969970703125e-4
    rest = rest - turns * 7.54978995489188e-8
    square = rest * rest
    sine = rest + rest * square * (
        -1.6666654611e-1 + square * (8.3321608736e-3 + square * -1.9515295891e-4)
    )
    cosine = (1.0 - 0.5 * square) + square * square * (
        4.166664568298827e-2 + square * (-1.388731625493765e-3 + square * 2.443315711809948e-5)
    )
    quarter = turns.astype(jnp.int32)
    odd = (quarter & 1) == 1
    sin = jnp.where(odd, cosine, sine)
    cos = jnp.where(odd, sine, cosine)
    return (
        jnp.where((quarter & 2) == 2, -sin, sin),
        jnp.where(((quarter + 1) & 2) == 2, -cos, cos),
    )


def position_kernel(s, visible, freqs, out):
    column = jnp.broadcast_to(visible[...].astype(f32), (8, visible.shape[1])).T[:, :1]
    sin, cos = sine_and_cosine(column * freqs[...])
    half = sin.shape[1]
    out[:, :half] = sin
    out[:, half:] = cos


def positions(scalars, visible, freqs):
    rows, width = visible.shape[1], 2 * freqs.shape[1]
    out = shape((rows, width), f32)
    return call(
        position_kernel, (1,), [whole(visible), whole(freqs)], whole(out), out, (visible, freqs), scalars, 16
    )


def ln_qkv_kernel(s, tok, pos, gain, w, normed, qkv, *resid):
    @pl.when(pl.program_id(0) == 0)
    def _():
        value = tok[...].astype(f32) + pos[...]
        if resid:
            resid[0][...] = value
        xhat, _ = normalize(value)
        normed[...] = (xhat * gain[...]).astype(bf16)

    qkv[...] = dot(normed[...], w[...]).astype(bf16)


def ln_qkv(scalars, far, tok, pos, gain, w):
    rows, width = tok.shape
    full = spec((rows, width), lambda i, s: (0, 0))
    parts = 2 if far else 3
    out_shape = [shape((rows, width), bf16), shape((rows, parts * width), bf16)]
    return call(
        ln_qkv_kernel,
        (parts,),
        [full, full, whole(gain), spec((width, width), lambda i, s: (0, i + far))],
        [full, spec((rows, width), lambda i, s: (0, i))] + [full] * (not far),
        out_shape + [shape((rows, width), f32)] * (not far),
        (tok, pos, gain, w),
        scalars,
        24,
    )


def far_query_kernel(s, normed, w, out):
    out[...] = dot(normed[...], w[...]).astype(bf16)


def far_query(scalars, normed, w):
    rows, width = normed.shape
    out = shape((rows, width // 2), bf16)
    return call(
        far_query_kernel,
        (1,),
        [whole(normed), spec((width, width // 2), lambda i, s: (0, s[1]))],
        whole(out),
        out,
        (normed, w),
        scalars,
        16,
    )


def head_masks(x):
    lane = lax.broadcasted_iota(jnp.int32, x.shape, 1)
    return jnp.where(lane < HD, x, 0.0).astype(bf16), jnp.where(lane >= HD, x, 0.0).astype(bf16)


def attn_kernel(group, s, q, k, v, *refs):
    rows = q.shape[0]
    later = len(refs) == 3
    if later:
        acc_in, stat_in, out = refs
    else:
        acc, stat = refs
    for pair in range(group):
        lanes = slice(pair * PAIR, (pair + 1) * PAIR)
        qs = jnp.concatenate(head_masks(q[:, lanes].astype(f32) * HD**-0.5), 0)
        scores = dot(k[:, lanes], qs, NT)
        top = jnp.max(scores, 0, keepdims=True)
        if later:
            before = stat_in[pair, 0:1]
            top = jnp.maximum(top, before)
        e = jnp.exp(scores - top)
        total = jnp.sum(e, 0, keepdims=True)
        vt = v[:, lanes].T
        low = e.astype(bf16)
        parts = [dot(vt[h * HD : (h + 1) * HD], low[:, h * rows : (h + 1) * rows]) for h in range(2)]
        if not later:
            acc[pair] = jnp.concatenate(parts, 0)
            stat[pair, 0:1] = top
            stat[pair, 1:2] = total
            continue
        shrink = jnp.exp(before - top)
        scale = 1.0 / (total + stat_in[pair, 1:2] * shrink)
        shrink = shrink * scale
        for h in range(2):
            at = slice(h * rows, (h + 1) * rows)
            held = acc_in[pair, h * HD : (h + 1) * HD]
            parts[h] = parts[h] * scale[:, at] + held * shrink[:, at]
        out[:, lanes] = jnp.concatenate(parts, 0).T.astype(bf16)


def attention(scalars, qkv, keys, *so_far):
    rows, width = qkv.shape[0], qkv.shape[1] // 3
    pairs = width // PAIR
    group = GROUP
    steps = pairs // group

    def column(part):
        return spec((rows, group * PAIR), lambda i, s: (0, part * steps + i))

    first = 0 if so_far else 1
    acc = spec((group, PAIR, rows), lambda i, s: (i, 0, 0))
    stat = spec((group, 8, 2 * rows), lambda i, s: (i, 0, 0))
    sums = [shape((pairs, PAIR, rows), f32), shape((pairs, 8, 2 * rows), f32)]
    return call(
        functools.partial(attn_kernel, group),
        (steps,),
        [column(0), column(first), column(first + 1)] + ([acc, stat] if so_far else []),
        spec((rows, group * PAIR), lambda i, s: (0, i)) if so_far else [acc, stat],
        shape((rows, width), bf16) if so_far else sums,
        (qkv, keys, keys) + so_far,
        scalars,
        28,
    )


def low_rows(packed):
    return packed.shape[0] - packed.shape[1]


def proj_kernel(s, att, att_half, w, resid, gain, resid2, normed2, packed):
    packed[low_rows(packed) :] = att_half[...]
    value = resid[...] + dot(att[...], w[...])
    resid2[...] = value
    xhat, _ = normalize(value)
    low = (xhat * gain[...]).astype(bf16)
    normed2[...] = low
    packed[: low_rows(packed)] = low.T


def project(scalars, att, w, resid, gain):
    rows, width = att.shape
    full = spec((rows, width), lambda i, s: (0, 0))
    half = spec((rows, width // 2), lambda i, s: (0, 1 - s[0]))
    return call(
        proj_kernel,
        (1,),
        [full, half, whole(w), full, whole(gain)],
        [
            full,
            full,
            spec((width + rows, rows), lambda i, s: (0, 0)),
        ],
        [
            shape((rows, width), f32),
            shape((rows, width), bf16),
            shape((width + rows, rows), bf16),
        ],
        (att, att, w, resid, gain),
        scalars,
        24,
    )


def gelu_and_slope(v):
    c = math.sqrt(2.0 / math.pi)
    square = v * v
    t = jnp.tanh(v * (c + (c * 0.044715) * square))
    act = 0.5 * v * (1.0 + t)
    slope = 0.5 * (1.0 + t) + (0.5 * v) * (1.0 - t * t) * (c + (3.0 * c * 0.044715) * square)
    return act, slope


def ff_kernel(count, s, normed, cot, up, down, *refs):
    step = pl.program_id(0)
    if count > 1:
        out_in, back_in, resid2, gain, w_own, w_other, *refs = refs
    pieces, refs = refs[: 2 * count], refs[2 * count :]
    if count > 1:
        out_low, grad2, branch, g_own, g_other, out, back = refs
    else:
        out, back = refs
    hidden = dot(normed[...], up[...])
    act, slope = gelu_and_slope(hidden)
    act = act.astype(bf16)
    grad = (dot(cot[...], down[...], NT) * slope).astype(bf16)
    out_part = dot(act, down[...])
    back_part = dot(grad, up[...], NT)

    @pl.when(step == 0)
    def _():
        out[...] = out_in[...] + out_part if count > 1 else out_part
        back[...] = back_in[...] + back_part if count > 1 else back_part

    @pl.when(step > 0)
    def _():
        out[...] += out_part
        back[...] += back_part

    for at, piece in enumerate(pieces):

        @pl.when(step == at)
        def _(piece=piece):
            piece[0] = act
            piece[1] = grad

    if count > 1:

        @pl.when(step == 2 * count - 1)
        def _():
            value = resid2[...]
            out_low[...] = (value + out[...]).astype(bf16)
            xhat, scale = normalize(value)
            g = cot[...].astype(f32) + norm_backward(back[...], gain[...], xhat, scale)
            grad2[...] = g
            low = g.astype(bf16)
            branch[...] = low
            g_other[...] = dot(low, w_other[...], NT).astype(bf16)
            g_own[...] = dot(low, w_own[...], NT).astype(bf16)


def ff_chunks(scalars, first, count, normed, cot, up, down, *more):
    rows, width = normed.shape
    half = width // 2
    wide = 512

    def column(i, s):
        return 2 * (first + i // 2) + (s[0] ^ (1 - (i & 1)))

    full = spec((rows, width), lambda i, s: (0, 0))
    part = spec((rows, half), lambda i, s: (0, 0))
    in_specs = [
        whole(normed),
        whole(cot),
        spec((width, wide), lambda i, s: (0, column(i, s))),
        spec((wide, width), lambda i, s: (column(i, s), 0)),
    ]
    out_specs = [spec((2, rows, wide), lambda i, s: (0, 0, 0))] * (2 * count)
    out_shape = [shape((2, rows, wide), bf16)] * (2 * count)
    scratch = []
    if count > 1:
        in_specs += [
            full,
            full,
            full,
            spec((1, width), lambda i, s: (0, 0)),
            spec((half, width), lambda i, s: (s[1], 0)),
            spec((half, width), lambda i, s: (1 - s[1], 0)),
        ]
        out_specs += [full, full, full, part, part]
        out_shape += [shape((rows, width), t) for t in (bf16, f32, bf16)]
        out_shape += [shape((rows, half), bf16)] * 2
        scratch = [pltpu.VMEM((rows, width), f32)] * 2
    else:
        out_specs += [full, full]
        out_shape += [shape((rows, width), f32)] * 2
    return call(
        functools.partial(ff_kernel, count),
        (2 * count,),
        in_specs,
        out_specs,
        out_shape,
        (normed, cot, up, down) + more,
        scalars,
        28,
        scratch,
    )


def ff_grads_kernel(at, s, act, act_o, grad, grad_o, cot, cot_o, nt, nt_o, *refs):
    keep, send = refs[-2:]
    step = pl.program_id(0)
    rows_both = jnp.concatenate([cot[...], cot_o[...]], 0)
    g_down = dot(jnp.concatenate([act[0], act_o[0]], 0), rows_both, TN).astype(bf16)
    grads = jnp.concatenate([grad[0], grad_o[0]], 0)
    g_up = dot(jnp.concatenate([nt[...], nt_o[...]], 1), grads).astype(bf16)
    g_proj = None
    if len(refs) > 2:
        att, att_o, branch, branch_o = refs[:4]
        both = jnp.concatenate([branch[...], branch_o[...]], 0)
        g_proj = dot(jnp.concatenate([att[...], att_o[...]], 0), both, TN).astype(bf16)
    code = s[at] & 7

    def store(target):
        rows_d = g_down.shape[0] // 8
        rows_u = g_up.shape[0] // 8
        half = g_up.shape[1] // 2
        for block in range(8):
            to = block ^ code
            target[to, :rows_d, :] = g_down[block * rows_d : (block + 1) * rows_d]
            part = g_up[block * rows_u : (block + 1) * rows_u]
            target[to, 32:64, : 2 * half] = part[:32]
            target[to, 32:48, 2 * half :] = part[32:, :half]
            target[to, 48:64, 2 * half :] = part[32:, half:]
            if g_proj is not None:
                part = g_proj[block * rows_u : (block + 1) * rows_u]
                wide = part.shape[1]
                target[to, 64:80, :wide] = part[:16]
                target[to, 64:80, wide:] = part[16:32]
                target[to, 80:, :wide] = part[32:]
                target[to, 80:, wide:] = jnp.zeros_like(part[32:])

    @pl.when(step == 0)
    def _():
        store(send)

    @pl.when(step == 1)
    def _():
        store(keep)


def ff_grads(scalars, chunk, mine, theirs, cot, cot_other, normed_t_other, normed_t, *proj):
    rows, width = cot.shape
    wide = mine.shape[2]
    at = 2 + 2 * chunk

    def side(i, s):
        return (1 - i) ^ (s[at] // 8)

    act = spec((1, rows, wide // 2), lambda i, s: (0, 0, side(i, s)))
    grad = spec((1, rows, wide), lambda i, s: (1, 0, 0))
    feature = spec((width // 2, rows), lambda i, s: (side(i, s), 0))
    in_specs = [act, act, grad, grad, whole(cot), whole(cot), feature, feature]
    if proj:
        half = width // 2
        column = spec((rows, half), lambda i, s: (0, side(i, s)))
        packed = spec((rows, half), lambda i, s: (2, 0))
        in_specs += [spec((rows, half), lambda i, s: (0, s[0])), packed, column, column]
    deep = 96 if proj else 64
    piece = spec((8, deep, width), lambda i, s: (0, 0, 0))
    return call(
        functools.partial(ff_grads_kernel, at),
        (2,),
        in_specs,
        [piece, piece],
        [shape((8, deep, width), bf16)] * 2,
        (mine, theirs, mine, theirs, cot, cot_other, normed_t, normed_t_other) + proj,
        scalars,
        28,
    )


def attn_back_kernel(group, s, q, g, k_o, k_f, v_o, v_f, *refs):
    gk_in, gv_in = refs[:2] if len(refs) == 5 else (None, None)
    gq, gk, gv = refs[-3:]
    rows = q.shape[0]
    for pair in range(group):
        lanes = slice(pair * PAIR, (pair + 1) * PAIR)
        k = jnp.concatenate([k_o[:, lanes], k_f[:, lanes]], 0)
        v = jnp.concatenate([v_o[:, lanes], v_f[:, lanes]], 0)
        kt = (k.astype(f32) * HD**-0.5).astype(bf16).T
        qs = jnp.concatenate(head_masks(q[:, lanes].astype(f32) * HD**-0.5), 0)
        gs = jnp.concatenate(head_masks(g[:, lanes].astype(f32)), 0)
        scores = dot(k, qs, NT)
        e = jnp.exp(scores - jnp.max(scores, 0, keepdims=True))
        probs = e * (1.0 / jnp.sum(e, 0, keepdims=True))
        grad_v = dot(probs.astype(bf16), gs)
        grad_p = dot(v, gs, NT)
        row = jnp.sum(probs * grad_p, 0, keepdims=True)
        grad_s = (probs * (grad_p - row)).astype(bf16)
        grad_k = dot(grad_s, qs)
        grad_q = [
            dot(kt[h * HD : (h + 1) * HD], grad_s[:, h * rows : (h + 1) * rows]) for h in range(2)
        ]
        if gk_in is not None:
            grad_k, grad_v = grad_k + gk_in[:, lanes], grad_v + gv_in[:, lanes]
        gq[:, lanes] = jnp.concatenate(grad_q, 0).T.astype(bf16)
        gk[:, lanes] = grad_k.astype(gk.dtype)
        gv[:, lanes] = grad_v.astype(gv.dtype)


def attention_back(scalars, query, grad, qkv, kv_far, *so_far):
    rows, width = qkv.shape[0], qkv.shape[1] // 3
    mine = width // PAIR // 2
    group = BACK_GROUP
    steps = mine // group

    def column(part):
        return spec((rows, group * PAIR), lambda i, s: (0, (2 * part + s[1]) * steps + i))

    block = spec((rows, group * PAIR), lambda i, s: (0, i))
    both = spec((2 * rows, group * PAIR), lambda i, s: (0, i))
    dtype = bf16 if so_far else f32
    return call(
        functools.partial(attn_back_kernel, group),
        (steps,),
        [block if so_far else column(0), block, column(1), column(0), column(2), column(1)]
        + [both] * len(so_far),
        [block, both, both],
        [shape((rows, width // 2), bf16)] + [shape((2 * rows, width // 2), dtype)] * 2,
        (query, grad, qkv, kv_far, qkv, kv_far) + so_far,
        scalars,
        BACK_LIMIT,
    )


def joint_kernel(s, n_own, n_far, gq_o, gq_f, gk, gv, keep, send):
    step = pl.program_id(0)
    gq = jnp.concatenate([gq_o[...], gq_f[...]], 0)
    n = jnp.concatenate([n_own[...], n_far[...]], 0)
    cols = gk.shape[1]

    def fill(target, code):
        tiles = [dot(n, g, TN).astype(bf16) for g in (gq, gk[...], gv[...])]
        rows = tiles[0].shape[0] // 8
        for block in range(8):
            at = block ^ code
            for i, tile in enumerate(tiles):
                part = tile[block * rows : (block + 1) * rows]
                target[at, :, i * cols : i * cols + part.shape[1]] = part

    @pl.when(step == 0)
    def _():
        fill(send, s[9])

    @pl.when(step == 1)
    def _():
        fill(keep, s[8])


def joint_grads(scalars, n_own, n_far, gq, gq_far, gk, gv):
    rows, width = n_own.shape
    half = width // 2
    feature = spec((rows, half), lambda i, s: (0, s[0] ^ (1 - i)))
    cols = 3 * half
    piece = spec((8, half // 8, cols), lambda i, s: (0, 0, 0))
    return call(
        joint_kernel,
        (2,),
        [feature, feature, whole(gq), whole(gq), whole(gk), whole(gv)],
        [piece, piece],
        [shape((8, half // 8, cols), bf16)] * 2,
        (n_own, n_far, gq, gq_far, gk, gv),
        scalars,
        28,
    )


def back_qkv_kernel(s, gq_o, gq_f, gk, gv, wq, wk, wv, own, far):
    rows = own.shape[0]

    def part(gq, at):
        total = dot(gq[...], wq[...], NT)
        total += dot(gk[pl.ds(at, rows)], wk[...], NT)
        return total + dot(gv[pl.ds(at, rows)], wv[...], NT)

    far[...] = part(gq_f, rows).astype(bf16)
    own[...] = part(gq_o, 0)


def back_qkv(scalars, gq, gq_far, gk, gv, w):
    rows, half = gq.shape
    width = 2 * half

    def column(part):
        return spec((width, half), lambda i, s: (0, 2 * part + s[1]))

    full = spec((rows, width), lambda i, s: (0, 0))
    return call(
        back_qkv_kernel,
        (1,),
        [whole(gq), whole(gq), whole(gk), whole(gv), column(0), column(1), column(2)],
        [full, full],
        [shape((rows, width), f32), shape((rows, width), bf16)],
        (gq, gq_far, gk, gv, w, w, w),
        scalars,
        28,
    )


def last_kernel(s, own, far, resid, gain, grad2, out):
    xhat, scale = normalize(resid[...])
    grad = own[...] + far[...].astype(f32)
    out[...] = grad2[...] + norm_backward(grad, gain[...], xhat, scale)


def token_grad(scalars, own, far, resid, gain, grad2):
    args = (own, far, resid, gain, grad2)
    return call(
        last_kernel,
        (1,),
        [whole(a) for a in args],
        whole(own),
        shape(own.shape, f32),
        args,
        scalars,
        24,
    )


def row_sums(values):
    folded = sum(values[:, at : at + 128] for at in range(0, values.shape[1], 128))
    return lax.dot_general(
        jnp.ones((8, 128), f32),
        folded,
        (NT, ((), ())),
        precision=lax.Precision.HIGHEST,
        preferred_element_type=f32,
    )


def unpack_ff_kernel(at, last, s, own, other, w, gain_in, *refs):
    gain, down, up, *proj = refs[-4:] if last else refs[-3:]
    step = pl.program_id(0)

    def unpack(source, code):
        for block in range(8):
            to = block ^ (code & 7)
            down[pl.ds(pl.multiple_of(to * 32, 32), 32), :] = source[block, :32, :].astype(f32)
            row = pl.multiple_of(to * 48, 16)
            up[pl.ds(row, 32), :] = source[block, 32:64, :512].astype(f32)
            up[pl.ds(row + 32, 16), :256] = source[block, 32:48, 512:].astype(f32)
            up[pl.ds(row + 32, 16), 256:] = source[block, 48:64, 512:].astype(f32)
            if last:
                wide = source.shape[2] // 2
                proj[0][pl.ds(row, 16), :] = source[block, 64:80, :wide].astype(f32)
                proj[0][pl.ds(row + 16, 16), :] = source[block, 64:80, wide:].astype(f32)
                proj[0][pl.ds(row + 32, 16), :] = source[block, 80:, :wide].astype(f32)

    @pl.when(step == 0)
    def _():
        unpack(own, s[at])

    @pl.when(step == 1)
    def _():
        unpack(other, s[at + 1])

    gain[0, 0] = gain_in[0, 0] + row_sums(up[...] * w[...].astype(f32))


def unpack_ff(scalars, chunk, far, own, other, w, so_far):
    width, hidden = w.shape
    at = 2 + 2 * chunk
    last = own.shape[1] > 64

    def side(i, s):
        return (s[at + i] // 8) ^ far

    def half(i, s):
        return 2 * chunk + (s[0] ^ i)

    any_spec = pl.BlockSpec(memory_space=pl.ANY)
    column = spec((width // 2, 512), lambda i, s: (side(i, s), half(i, s)))
    gain = spec((1, 1, 8, width // 2), lambda i, s: (i, side(i, s), 0, 0))
    out_specs = [gain, spec((256, width), lambda i, s: (2 * half(i, s) + side(i, s), 0)), column]
    out_shape = [shape((2, 2, 8, width // 2), f32), shape((hidden, width), f32), shape((width, hidden), f32)]
    if last:
        out_specs.append(spec((width // 2, width // 2), lambda i, s: (s[0] ^ i, side(i, s))))
        out_shape.append(shape((width, width), f32))
    in_specs = [whole(own), whole(other), column]
    in_specs += [gain, any_spec, any_spec, any_spec][: len(so_far)]
    return call(
        functools.partial(unpack_ff_kernel, at, last),
        (2,),
        in_specs,
        out_specs,
        out_shape,
        (own, other, w) + tuple(so_far),
        scalars,
        28,
        aliases={4 + i: i for i in range(len(so_far))},
    )


def unpack_qkv_kernel(s, own, other, w, *refs):
    joint, gain = refs[-2:]
    step = pl.program_id(0)
    mine = s[1]

    def unpack(source, code):
        half = source.shape[2] // 6

        def place_columns(first):
            for block in range(2):
                rows = pl.ds(pl.multiple_of((block ^ (code & 1)) * 48, 16), 48)
                for part in range(3):
                    for side in range(2):
                        column = 2 * half * part + half * (first ^ side)
                        value = source[block, :, (3 * side + part) * half : (3 * side + part + 1) * half]
                        joint[rows, column : column + half] = value.astype(f32)

        for first in range(2):
            pl.when(mine == first)(functools.partial(place_columns, first))

    @pl.when(step < 2)
    def _():
        unpack(own, s[8])

    @pl.when(step >= 2)
    def _():
        unpack(other, s[9])

    gain[0] = row_sums(joint[...] * w[...].astype(f32))


def unpack_qkv(scalars, far, own, other, w, so_far):
    width = w.shape[0]

    def row(i, s):
        code = s[8 + i // 2]
        return 4 * (s[0] ^ (i // 2)) + 2 * ((code // 4) ^ far) + ((i & 1) ^ ((code // 2) & 1))

    def blocks(mine):
        return spec((2,) + own.shape[1:], lambda i, s: (jnp.clip(i - 2 * mine, 0, 1), 0, 0))

    any_spec = pl.BlockSpec(memory_space=pl.ANY)
    rows = spec((width // 8, 3 * width), lambda i, s: (row(i, s), 0))
    return call(
        unpack_qkv_kernel,
        (4,),
        [blocks(0), blocks(1), rows] + [any_spec] * len(so_far),
        [rows, spec((1, 8, width // 8), lambda i, s: (row(i, s), 0, 0))],
        [shape((width, 3 * width), f32), shape((8, 8, width // 8), f32)],
        (own, other, w) + tuple(so_far),
        scalars,
        28,
        aliases={4 + i: i for i in range(len(so_far))},
    )


def fast(tokens, visible, ln1_gain, w_qkv, w_proj, ln2_gain, w_up, w_down, d_out):
    tok, cot = tokens[0], d_out[0]
    rows, width = tok.shape
    gain1, gain2 = ln1_gain[None], ln2_gain[None]
    scalars = [lax.axis_index("dp") & 1, lax.axis_index("blk")]
    for orders in FF_ORDERS + (QKV_ORDER,):
        scalars.extend(places(orders))
    scalars = jnp.stack([jnp.int32(v) for v in scalars])

    order = Order()
    run = order.run
    vis_far = swap(visible, "y")
    tok_far = swap(tok, "y")
    half = width // 2
    freqs = jnp.exp(jnp.arange(half, dtype=f32) * (-math.log(10000.0) / half))[None]
    pos = run(functools.partial(positions, scalars), visible, freqs)
    w_first = pltpu.with_memory_space_constraint(w_qkv, pltpu.HBM)
    normed1, qkv, resid = run(functools.partial(ln_qkv, scalars, False), tok, pos, gain1, w_first)
    sums = run(functools.partial(attention, scalars), qkv, qkv)
    pos_far = run(functools.partial(positions, scalars), vis_far, freqs)
    normed1_far, kv_far = run(functools.partial(ln_qkv, scalars, True), tok_far, pos_far, gain1, w_qkv)
    attended = run(functools.partial(attention, scalars), qkv, kv_far, *sums)
    resid2, normed2, packed = run(
        functools.partial(project, scalars), attended, w_proj, resid, gain2
    )
    early = tuple(order.swap(array, "c") for array in (cot, packed))

    streams, blocks, values = {}, {}, {"early": early}
    ff, proj, joint = (jnp.zeros((2, 2, 8, width // 2), f32),), (), ()

    def feed_forward(first):
        if first == 0:
            send, keep, *values["sums"] = run(
                functools.partial(ff_chunks, scalars, 0, 1), normed2, cot, w_up, w_down
            )
            values["act", 0], values["e0"] = keep, order.swap(send, "c")
            return
        more = (*values["sums"], resid2, gain2, w_proj, w_proj)
        send1, keep1, send2, keep2, out, grad2, branch, g_own, g_other = run(
            functools.partial(ff_chunks, scalars, 1, 2), normed2, cot, w_up, w_down, *more
        )
        values["act", 1], values["e1"] = keep1, order.swap(send1, "c")
        values["act", 2], values["e2"] = keep2, order.swap(send2, "c")
        values["branch"], values["branch_other"] = branch, order.swap(branch, "c")
        values["g"] = order.swap(g_other, "y")
        values.update(out=out, grad2=grad2, own=g_own)

    def weight_grads(chunk):
        early = (*values["early"], packed)
        more = ()
        if chunk == 2:
            more = (attended, values["early"][1], values["branch"], values["branch_other"])
        keep, send = run(
            functools.partial(ff_grads, scalars, chunk),
            values["act", chunk], values["e%d" % chunk], cot, *early, *more,
        )
        streams[chunk] = total(order, keep, send, list(zip(*FF_ORDERS[chunk])))
        advance(chunk)

    def advance(chunk):
        pair = next(streams[chunk])
        if pair is not None:
            blocks.setdefault(chunk, []).append(pair)

    def wait(key):
        if key[0] in "nf" and key[1:].isdigit():
            chunk, far = int(key[1:]), int(key[0] == "f")
            own, other = blocks[chunk][far]
            blocks[chunk][far] = own, run(lambda value: value, other)
            return
        value = values[key]
        values[key] = run(lambda *v: v if isinstance(value, tuple) else v[0], *(value if isinstance(value, tuple) else (value,)))

    def own_queries():
        values["attn"] = run(functools.partial(attention_back, scalars), qkv, values["own"], qkv, kv_far)

    def far_queries():
        gq, *sums = values["attn"]
        values["q"] = run(functools.partial(far_query, scalars), normed1_far, w_qkv)
        back = run(functools.partial(attention_back, scalars), values["q"], values["g"], qkv, kv_far, *sums)
        values["attn"] = (gq, *back)

    def joint_weights():
        keep, send = run(functools.partial(joint_grads, scalars), normed1, normed1_far, *values["attn"])
        links = [("c", "c")] + list(zip(*QKV_ORDER))
        streams[3] = total(order, keep, send, links, lambda a, b: jnp.concatenate([a, b], -1))
        advance(3)

    def back_joint():
        own, far = run(functools.partial(back_qkv, scalars), *values["attn"], w_qkv)
        values["norm"], values["bf"] = own, order.swap(far, "y")

    def finish_tokens():
        args = (values["norm"], values["bf"], resid, gain1, values["grad2"])
        values["tokens"] = run(functools.partial(token_grad, scalars), *args)

    def unpack(chunk, far):
        nonlocal ff, proj, joint
        own, other = blocks[chunk][far]
        if chunk == 3:
            joint = run(lambda a, b, *f: unpack_qkv(scalars, far, a, b, w_qkv, f), own, other, *joint)
            return
        so_far = ff + proj if chunk == 2 else ff
        weight = w_hbm if (chunk, far) == final else w_up
        result = tuple(
            run(lambda a, b, *f: unpack_ff(scalars, chunk, far, a, b, weight, f), own, other, *so_far)
        )
        ff, proj = result[:3], result[3:] or proj

    w_hbm = pltpu.with_memory_space_constraint(w_up, pltpu.HBM)
    final = [step[1:] for step in PLAN if step[0] == "unpack" and step[1] != 3][-1]
    steps = {
        "ff": feed_forward,
        "dw": weight_grads,
        "go": advance,
        "wait": wait,
        "own": own_queries,
        "far": far_queries,
        "joint": joint_weights,
        "back": back_joint,
        "tokens": finish_tokens,
        "unpack": unpack,
    }
    for name, *args in PLAN:
        steps[name](*args)
    sums2, d_down, d_up = ff
    d_qkv, sums1 = joint
    out, d_tokens, d_proj = values["out"], values["tokens"], proj[0]
    d_gain1 = sums1[:, 0].reshape(-1) / ln1_gain
    d_gain2 = (sums2[0, :, 0] + sums2[1, :, 0]).reshape(-1) / ln2_gain
    return out[None], d_tokens[None], d_gain1, d_qkv, d_proj, d_gain2, d_up, d_down


def layer_norm(values, gain):
    center = values - jnp.mean(values, -1, keepdims=True)
    spread = jnp.mean(center * center, -1, keepdims=True)
    return center * lax.rsqrt(spread + epsilon) * gain


def outer_product(left, right):
    return lax.dot_general(
        left, right, (((0,), (0,)), ((), ())), preferred_element_type=jnp.float32
    )


def times_transposed(left, weight):
    return lax.dot_general(
        left, weight, (((1,), (1,)), ((), ())), preferred_element_type=jnp.float32
    )


def split_blocks(keys, values):
    count = keys.shape[0]
    size = math.gcd(count, 512)
    shape = (count // size, size, HEADS, HD)
    return (keys.reshape(shape), values.reshape(shape))


def general(tokens, visible, ln1_gain, w_qkv, w_proj, ln2_gain, w_up, w_down, d_out):
    rows = tokens.shape[1]
    width = tokens.shape[2]
    factor = HD ** (-0.5)
    resid = tokens[0].astype(jnp.float32) + position_table(visible[0], width)
    normed1, back_one = jax.vjp(layer_norm, resid, ln1_gain)
    normed1 = normed1.astype(jnp.bfloat16)
    qkv = jnp.dot(normed1, w_qkv, preferred_element_type=jnp.float32).astype(jnp.bfloat16)
    query = qkv[:, :width]
    keys = qkv[:, width : 2 * width]
    values = qkv[:, 2 * width :]
    query_heads = query.reshape(rows, HEADS, HD)
    initial = (
        jnp.full((HEADS, rows), -1e30, jnp.float32),
        jnp.zeros((HEADS, rows), jnp.float32),
        jnp.zeros((HEADS, rows, HD), jnp.float32),
    )
    key_blocks, value_blocks = split_blocks(
        lax.all_gather(keys, "blk", axis=0, tiled=True),
        lax.all_gather(values, "blk", axis=0, tiled=True),
    )

    def one_block(state, block):
        running, total, accum = state
        block_keys, block_values = block
        scores = (
            jnp.einsum("qhd,khd->hqk", query_heads, block_keys, preferred_element_type=jnp.float32)
            * factor
        )
        top = jnp.maximum(running, jnp.max(scores, -1))
        weights = jnp.exp(scores - top[..., None])
        shrink = jnp.exp(running - top)
        total = total * shrink + jnp.sum(weights, -1)
        accum = accum * shrink[..., None] + jnp.einsum(
            "hqk,khd->hqd",
            weights.astype(jnp.bfloat16),
            block_values,
            preferred_element_type=jnp.float32,
        )
        return ((top, total, accum), None)

    running, total, accum = lax.scan(one_block, initial, (key_blocks, value_blocks))[0]
    log_total = running + jnp.log(total)
    attended = (accum / total[..., None]).transpose(1, 0, 2).reshape(rows, width)
    attended_low = attended.astype(jnp.bfloat16)
    resid2 = resid + jnp.dot(attended_low, w_proj, preferred_element_type=jnp.float32)
    normed2, back_two = jax.vjp(layer_norm, resid2, ln2_gain)
    normed2 = normed2.astype(jnp.bfloat16)
    hidden = jnp.dot(normed2, w_up, preferred_element_type=jnp.float32)
    activated, back_gelu = jax.vjp(jax.nn.gelu, hidden)
    activated = activated.astype(jnp.bfloat16)
    result = resid2 + jnp.dot(activated, w_down, preferred_element_type=jnp.float32)
    cotangent = d_out[0]
    grad_down = outer_product(activated, cotangent)
    (grad_hidden,) = back_gelu(times_transposed(cotangent, w_down))
    grad_hidden = grad_hidden.astype(jnp.bfloat16)
    grad_up = outer_product(normed2, grad_hidden)
    grad_resid2, grad_gain2 = back_two(times_transposed(grad_hidden, w_up))
    grad_resid2 = grad_resid2 + cotangent.astype(jnp.float32)
    grad_branch = grad_resid2.astype(jnp.bfloat16)
    grad_proj = outer_product(attended_low, grad_branch)
    grad_attended = times_transposed(grad_branch, w_proj).astype(jnp.bfloat16)
    correction = (grad_attended.astype(jnp.float32) * attended).reshape(rows, HEADS, HD)
    correction = jnp.sum(correction, -1).T
    grad_heads = grad_attended.reshape(rows, HEADS, HD)
    all_keys, all_values = (
        lax.all_gather(keys, "blk", axis=0, tiled=True),
        lax.all_gather(values, "blk", axis=0, tiled=True),
    )
    full_rows = all_keys.shape[0]
    key_blocks, value_blocks = split_blocks(all_keys, all_values)

    def back_block(grad_query, block):
        block_keys, block_values = block
        scores = (
            jnp.einsum("qhd,khd->hqk", query_heads, block_keys, preferred_element_type=jnp.float32)
            * factor
        )
        probs = jnp.exp(scores - log_total[..., None])
        grad_value = jnp.einsum(
            "hqk,qhd->khd",
            probs.astype(jnp.bfloat16),
            grad_heads,
            preferred_element_type=jnp.float32,
        )
        grad_probs = jnp.einsum(
            "qhd,khd->hqk", grad_heads, block_values, preferred_element_type=jnp.float32
        )
        grad_scores = (probs * (grad_probs - correction[..., None])).astype(jnp.bfloat16)
        grad_query = grad_query + jnp.einsum(
            "hqk,khd->qhd", grad_scores, block_keys, preferred_element_type=jnp.float32
        )
        grad_key = (
            jnp.einsum("hqk,qhd->khd", grad_scores, query_heads, preferred_element_type=jnp.float32)
            * factor
        )
        return (grad_query, (grad_key, grad_value))

    grad_query, (key_parts, value_parts) = lax.scan(
        back_block, jnp.zeros((rows, HEADS, HD), jnp.float32), (key_blocks, value_blocks)
    )
    grad_query = (grad_query * factor).reshape(rows, width)
    grad_keys, grad_values = (
        lax.psum_scatter(
            key_parts.reshape(full_rows, width).astype(jnp.bfloat16),
            "blk",
            scatter_dimension=0,
            tiled=True,
        ).astype(jnp.float32),
        lax.psum_scatter(
            value_parts.reshape(full_rows, width).astype(jnp.bfloat16),
            "blk",
            scatter_dimension=0,
            tiled=True,
        ).astype(jnp.float32),
    )
    grad_qkv = jnp.concatenate([grad_query, grad_keys, grad_values], 1).astype(jnp.bfloat16)
    grad_joint = outer_product(normed1, grad_qkv)
    grad_resid, grad_gain1 = back_one(times_transposed(grad_qkv, w_qkv))
    input_grad = grad_resid2 + grad_resid
    flats = (
        grad_joint.reshape(-1),
        grad_proj.reshape(-1),
        grad_up.reshape(-1),
        grad_down.reshape(-1),
    )
    shares = (
        lax.psum_scatter(flats[0], ("dp", "blk"), scatter_dimension=0, tiled=True),
        lax.psum_scatter(flats[1], ("dp", "blk"), scatter_dimension=0, tiled=True),
        lax.psum_scatter(flats[2], ("dp", "blk"), scatter_dimension=0, tiled=True),
        lax.psum_scatter(flats[3], ("dp", "blk"), scatter_dimension=0, tiled=True),
    )
    summed = (
        lax.all_gather(shares[0].astype(jnp.bfloat16), ("dp", "blk"), axis=0, tiled=True).astype(
            jnp.float32
        ),
        lax.all_gather(shares[1].astype(jnp.bfloat16), ("dp", "blk"), axis=0, tiled=True).astype(
            jnp.float32
        ),
        lax.all_gather(shares[2].astype(jnp.bfloat16), ("dp", "blk"), axis=0, tiled=True).astype(
            jnp.float32
        ),
        lax.all_gather(shares[3].astype(jnp.bfloat16), ("dp", "blk"), axis=0, tiled=True).astype(
            jnp.float32
        ),
    )
    gain_one, gain_two = lax.psum((grad_gain1, grad_gain2), ("dp", "blk"))
    return (
        result.astype(jnp.bfloat16)[None],
        input_grad[None],
        gain_one,
        summed[0].reshape(w_qkv.shape),
        summed[1].reshape(w_proj.shape),
        gain_two,
        summed[2].reshape(w_up.shape),
        summed[3].reshape(w_down.shape),
    )


def solution(mesh):
    split = mesh.shape["dp"] == 16 and mesh.shape["blk"] == 2

    def local(tokens, *others):
        fits = split and 2 * tokens.shape[1] == tokens.shape[2]
        return (fast if fits else general)(tokens, *others)

    return jax.shard_map(
        local,
        mesh=mesh,
        in_specs=(
            P("dp", "blk", None),
            P("dp", "blk"),
            P(),
            P(),
            P(),
            P(),
            P(),
            P(),
            P("dp", "blk", None),
        ),
        out_specs=(P("dp", "blk", None), P("dp", "blk", None), P(), P(), P(), P(), P(), P()),
        check_vma=False,
    )
```
